128 devices in a mesh: seq: 128 (over z, x, y, core).
Axes of the slice: x: 4, y: 4, z: 4, core: 2. Of those that a mesh axis runs over, the one named last changes fastest.
Arguments:
- tokens: bfloat16 [32768, 1024], P('seq'), may hold values from -6 to 6
- w_in: bfloat16 [1024, 4096], replicated, may hold values from -0.1875 to 0.1875
- w_out: bfloat16 [1024, 1024], replicated, may hold values from -0.1875 to 0.1875
- block_counts: int32 [64], replicated, may hold values from 1 to 16, 256 in all
- tails: int32 [64], replicated, may hold values from 1 to 128
- grad_out: bfloat16 [32768, 1024], P('seq'), may hold values from -6 to 6
Outputs:
- layer_out: bfloat16 [32768, 1024], P('seq')
- grad_tokens: bfloat16 [32768, 1024], P('seq')
- grad_w_in: float32 [4096, 1024], P('seq')
The draws below stay inside these ranges and needn't reach their ends.
Inputs may be any that keep to these rules, and one draw needn't show every extreme that they name: `block_counts`: the block counts sum to 256; one user has exactly 16 blocks.
All inputs are finite; a program needn't handle non-finite values.
Results may differ from the reference program's by a relative error of at most 0.013.
Values may be sent and summed in bfloat16 or wider, within the bound.
A program may use at most 192 MiB of HBM per device.

```python
import math
import jax
import jax.numpy as jnp
import numpy as np
from jax import lax

D = 1024
HEADS = 8
HD = 128
BLK = 128
MAXB = 16
TOK_DEV = 256
TOKENS = 32768
NBLOCKS = 256
USERS = 64
MAXLEN = 2048
HOPS = 8


def with_ends(drawn, stream_key, least, high):
    index_at = [jax.random.randint(jax.random.fold_in(stream_key, axis), (), 0, length) for axis, length in enumerate(drawn.shape)]
    longest = drawn.shape.index(max(drawn.shape))
    next_to = index_at[:longest] + [(index_at[longest] + 1) % drawn.shape[longest]] + index_at[longest + 1:]
    return drawn.at[tuple(index_at)].set(least).at[tuple(next_to)].set(high)


def block_scale(rng, shape, split, least, top_value):
    factor_of, own = 1.0, jax.random.fold_in(rng, 6)
    for axis_at, parts in split:
        draws = jnp.exp(jax.random.uniform(jax.random.fold_in(own, axis_at), (parts,), jnp.float32, least / len(split), top_value / len(split)))
        factor_of = factor_of * jnp.repeat(draws, shape[axis_at] // parts).reshape([-1 if axis == axis_at else 1 for axis in range(len(shape))])
    return factor_of


def profile(amount, total, bound, slope):
    portions = [(1 << 20) // math.isqrt(grade ** slope) + 1 for grade in range(2, amount + 1)]
    surplus, holding = total - bound - (amount - 1), [1] * (amount - 1)
    while surplus > 0:
        candidates = [i for i in range(amount - 1) if holding[i] < bound]
        pool, left = sum([portions[i] for i in candidates]), surplus
        for i in candidates:
            more = min(bound - holding[i], max(1, left * portions[i] // pool), surplus)
            holding[i] = holding[i] + more
            surplus = surplus - more
    return np.array([bound] + holding)


def uneven(stream_key, number_of, total, bound, slope):
    if number_of == 2:
        one = jax.random.randint(stream_key, (), max(1, total - bound), min(bound, total - 1) + 1)
        return jnp.stack([one, total - one])
    sizes = jnp.asarray(profile(number_of, total, bound, slope), jnp.int32)
    couples = (number_of - 1) // 2
    source_of, taker = sizes[1:1 + 2 * couples:2], sizes[2:2 + 2 * couples:2]
    margin = jnp.minimum(source_of - 1, bound - taker)
    moved = jax.random.randint(jax.random.fold_in(stream_key, 1), (couples,), 0, 1 << 20) % (margin + 1)
    sizes = sizes.at[1:1 + 2 * couples:2].set(source_of - moved).at[2:2 + 2 * couples:2].set(taker + moved)
    return sizes[jax.random.permutation(jax.random.fold_in(stream_key, 2), number_of)]


def normal_values(rng, dims, width, reach, shards=(), held_as=jnp.bfloat16):
    loudness = block_scale(rng, dims, shards, -0.22, 0.18) if shards else 1.0
    entries = jax.random.normal(rng, dims, jnp.float32) * width * loudness
    return jnp.minimum(jnp.maximum(entries, -reach), reach).astype(held_as)


def setup_inputs(seed: int = 0) -> dict:
    seeds = jax.random.split(jax.random.key(seed), 7)
    tokens = normal_values(seeds[0], (TOKENS, D), 1.0, 6.0, ((0, 128),))
    w_in = normal_values(seeds[1], (D, 4 * D), D ** -0.5, 0.1875)
    w_out = normal_values(seeds[2], (D, D), D ** -0.5, 0.1875)
    block_counts = uneven(seeds[3], USERS, NBLOCKS, MAXB, 2).astype(jnp.int32)
    tails = with_ends(jax.random.randint(seeds[4], (USERS,), 1, BLK + 1), jax.random.fold_in(seeds[4], 1), 1, BLK).astype(jnp.int32)
    grad_out = normal_values(seeds[5], (TOKENS, D), 1.0, 6.0, ((0, 128),))
    return dict(tokens=tokens, w_in=w_in, w_out=w_out, block_counts=block_counts, tails=tails, grad_out=grad_out)


eps = 1e-05

def row_info(rows, counts, tails):
    ends = jnp.cumsum(counts).astype(jnp.int32) * BLK
    starts = ends - counts * BLK
    lengths = (counts - 1) * BLK + tails
    user = lax.optimization_barrier(jnp.sum((rows[:, None] >= ends[None, :]).astype(jnp.int32), axis=1))
    pick = user[:, None] == jnp.arange(counts.shape[0], dtype=jnp.int32)[None, :]
    start = lax.optimization_barrier(jnp.sum(jnp.where(pick, starts[None, :], 0), axis=1))
    length = lax.optimization_barrier(jnp.sum(jnp.where(pick, lengths[None, :], 0), axis=1))
    valid = (rows >= 0) & (rows - start < length)
    return (user, rows, valid)

def attend(query, keys, values, qinfo, kinfo):
    q_user, q_rows, q_ok = qinfo
    k_user, k_rows, k_ok = kinfo
    qh = query.reshape(query.shape[0], HEADS, HD)
    kh = keys.reshape(keys.shape[0], HEADS, HD)
    vh = values.reshape(values.shape[0], HEADS, HD)
    scores = jnp.einsum('qhd,khd->hqk', qh, kh, preferred_element_type=jnp.float32)
    weights = jax.nn.silu(scores * HD ** (-0.5)) / MAXLEN
    visible = (q_user[:, None] == k_user[None, :]) & (k_rows[None, :] <= q_rows[:, None])
    visible = visible & q_ok[:, None] & k_ok[None, :]
    weights = jnp.where(visible[None], weights, 0.0).astype(jnp.bfloat16)
    out = jnp.einsum('hqk,khd->qhd', weights, vh, preferred_element_type=jnp.float32)
    return out.reshape(query.shape[0], HEADS * HD)

def stem_norm(xf):
    return xf * lax.rsqrt(lax.optimization_barrier(jnp.mean(xf * xf, axis=-1, keepdims=True)) + eps)

def split_parts(pre):
    hidden = jax.nn.silu(pre)
    return tuple((hidden[:, i * D:(i + 1) * D].astype(jnp.bfloat16) for i in range(4)))

def make_tail(w_out):

    def tail_fn(attn, u, xf):
        normed = attn * lax.rsqrt(lax.optimization_barrier(jnp.mean(attn * attn, axis=-1, keepdims=True)) + eps)
        gated = (normed * u).astype(jnp.bfloat16)
        return xf + jnp.dot(gated, w_out, preferred_element_type=jnp.float32)
    return tail_fn

def reference(tokens, w_in, w_out, block_counts, tails, grad_out):
    rows = jnp.arange(TOKENS, dtype=jnp.int32)
    user, rows, valid = row_info(rows, block_counts, tails)
    pad = HOPS * TOK_DEV
    span = (HOPS + 1) * TOK_DEV
    user_pad = jnp.concatenate([jnp.full((pad,), -1, jnp.int32), user])
    rows_pad = jnp.concatenate([jnp.full((pad,), -1, jnp.int32), rows])
    ok_pad = jnp.concatenate([jnp.zeros((pad,), bool), valid])

    def attention(q, k, v):
        k_pad = jnp.concatenate([jnp.zeros((pad, D), jnp.bfloat16), k])
        v_pad = jnp.concatenate([jnp.zeros((pad, D), jnp.bfloat16), v])

        def one(b):
            at = b * TOK_DEV
            qs = lax.dynamic_slice_in_dim(q, at, TOK_DEV, 0)
            qinfo = tuple((lax.dynamic_slice_in_dim(a, at, TOK_DEV, 0) for a in (user, rows, valid)))
            ks = lax.dynamic_slice_in_dim(k_pad, at, span, 0)
            vs = lax.dynamic_slice_in_dim(v_pad, at, span, 0)
            kinfo = tuple((lax.dynamic_slice_in_dim(a, at, span, 0) for a in (user_pad, rows_pad, ok_pad)))
            return attend(qs, ks, vs, qinfo, kinfo)
        out = lax.map(jax.checkpoint(one), jnp.arange(TOKENS // TOK_DEV, dtype=jnp.int32))
        return out.reshape(TOKENS, D)
    xf = tokens.astype(jnp.float32)
    normed_f, norm_back = jax.vjp(stem_norm, xf)
    normed = normed_f.astype(jnp.bfloat16)
    pre = jnp.dot(normed, w_in, preferred_element_type=jnp.float32)
    tail_fn = make_tail(w_out)

    def middle(pre, xf):
        u, v, q, k = split_parts(pre)
        return tail_fn(attention(q, k, v), u, xf)
    out_f, back = jax.vjp(middle, pre, xf)
    layer_out = out_f.astype(jnp.bfloat16)
    d_pre, d_xf = back(grad_out.astype(jnp.float32))
    d_pre_b = d_pre.astype(jnp.bfloat16)
    grad_w_in = lax.dot_general(d_pre_b, normed, (((0,), (0,)), ((), ())), preferred_element_type=jnp.float32)
    d_normed = lax.dot_general(d_pre_b, w_in, (((1,), (1,)), ((), ())), preferred_element_type=jnp.float32)
    grad_tokens = (d_xf + norm_back(d_normed)[0]).astype(jnp.bfloat16)
    return (layer_out, grad_tokens, grad_w_in)
```

```python
import functools

import jax
import jax.numpy as jnp
from jax import lax
from jax.experimental import pallas as pl
from jax.experimental.pallas import tpu as pltpu
from jax.sharding import PartitionSpec as P

MESH = pl.DeviceIdType.MESH
HEADS = 8
HD = 128
BLK = 128
TQ = 256
D = 1024
eps = 1e-05
HALF = 0.5 * HD ** (-0.5)
NT = (((1,), (1,)), ((), ()))
NN = (((1,), (0,)), ((), ()))
TN = (((0,), (0,)), ((), ()))


def dot(a, b, dims, precision=None):
    return lax.dot_general(a, b, dims, precision=precision, preferred_element_type=jnp.float32)


def tile_bounds(start_ref, t, own):
    lo_a, lo_b = start_ref[2 * t], start_ref[2 * t + 1]
    diag = own + t
    return lo_a, lo_b, lo_a // 2, jnp.minimum((lo_b + 1) // 2, diag), diag


def row_valid(rows_ref, t):
    at = lax.broadcasted_iota(jnp.int32, (TQ, HD), 0)
    limit = jnp.where(at < BLK, rows_ref[2 * t], rows_ref[2 * t + 1] + BLK)
    return at < limit


def keep_mask(lo_a, lo_b, diag, kt):
    r = lax.broadcasted_iota(jnp.int32, (TQ, TQ), 0)
    c = lax.broadcasted_iota(jnp.int32, (TQ, TQ), 1) + kt * TQ
    lo = jnp.where(r < BLK, lo_a * BLK, lo_b * BLK)
    return (c >= lo) & (c <= r + diag * TQ)


def fwd_kernel(own, start_ref, rows_ref, q_ref, k_ref, v_ref, u_ref, dg_ref, attn_ref, stat_ref):
    tiles = q_ref.shape[0] // TQ

    @pl.loop(0, tiles)
    def _(t):
        at = pl.ds(pl.multiple_of(t * TQ, TQ), TQ)
        q = jnp.where(row_valid(rows_ref, t), q_ref[at, :].astype(jnp.float32) * HALF, 0.0).astype(jnp.bfloat16)
        lo_a, lo_b, first, full, diag = tile_bounds(start_ref, t, own)

        def body(masked, kt, acc):
            cols = pl.ds(pl.multiple_of(kt * TQ, TQ), TQ)
            x = dot(q, k_ref[cols, :], NT)
            if masked:
                x = jnp.where(keep_mask(lo_a, lo_b, diag, kt), x, 0.0)
            w = (x + x * jnp.tanh(x)).astype(jnp.bfloat16)
            return acc + dot(w, v_ref[cols, :], NN)

        acc = lax.fori_loop(first, full, functools.partial(body, True), jnp.zeros((TQ, HD), jnp.float32))
        acc = lax.fori_loop(full, diag, functools.partial(body, False), acc)
        acc = body(True, diag, acc) * (1.0 / 2048)
        attn_ref[at, :] = acc
        ones = jnp.ones((8, HD), jnp.float32)
        da = dg_ref[at, :].astype(jnp.float32) * u_ref[at, :].astype(jnp.float32)
        for s, val in enumerate((acc * acc, da * acc)):
            sums = dot(ones, val, NT)
            stat_ref[s, pl.ds(2 * t, 1), :] = sums[0:1, :BLK]
            stat_ref[s, pl.ds(2 * t + 1, 1), :] = sums[0:1, BLK:]


def column(stat, t):
    tall = []
    for half in range(2):
        pick = lax.broadcasted_iota(jnp.int32, (16, HD), 0) == 2 * t + half
        tall.append(dot(stat, pick.astype(jnp.float32), TN, lax.Precision.HIGHEST))
    return jnp.concatenate(tall, axis=0)


def bwd_kernel(own, start_ref, rows_ref, q_ref, k_ref, v_ref, u_ref, dg_ref, attn_ref, stat_ref,
               gated_ref, du_ref, dq_ref, dk_ref, dv_ref):
    tiles = q_ref.shape[0] // TQ
    dk_ref[...] = jnp.zeros_like(dk_ref)
    dv_ref[...] = jnp.zeros_like(dv_ref)

    @pl.loop(0, tiles)
    def _(t):
        at = pl.ds(pl.multiple_of(t * TQ, TQ), TQ)
        valid = row_valid(rows_ref, t)
        q = jnp.where(valid, q_ref[at, :].astype(jnp.float32) * HALF, 0.0).astype(jnp.bfloat16)
        square = column(stat_ref[0], t)
        cross = column(stat_ref[1], t)
        r = lax.rsqrt(square * (1.0 / D) + eps)
        attn = attn_ref[at, :]
        u = u_ref[at, :].astype(jnp.float32)
        dg = dg_ref[at, :].astype(jnp.float32)
        na = attn * r
        gated_ref[at, :] = (na * u).astype(gated_ref.dtype)
        du_ref[at, :] = (na * dg).astype(du_ref.dtype)
        d_attn = r * (dg * u) - na * (r * r * cross * (1.0 / D))
        do = jnp.where(valid, d_attn, 0.0).astype(jnp.bfloat16)
        lo_a, lo_b, first, full, diag = tile_bounds(start_ref, t, own)

        def body(masked, kt, dq):
            cols = pl.ds(pl.multiple_of(kt * TQ, TQ), TQ)
            k = k_ref[cols, :]
            x = dot(q, k, NT)
            dw = dot(do, v_ref[cols, :], NT)
            a = 1.0 + jnp.tanh(x)
            w = x * a
            ds = dw * (a + w * (2.0 - a))
            if masked:
                keep = keep_mask(lo_a, lo_b, diag, kt)
                w = jnp.where(keep, w, 0.0)
                ds = jnp.where(keep, ds, 0.0)
            w = w.astype(jnp.bfloat16)
            ds = ds.astype(jnp.bfloat16)
            dv_ref[cols, :] += dot(w, do, TN)
            dk_ref[cols, :] += dot(ds, q, TN)
            return dq + dot(ds, k, NN)

        dq = lax.fori_loop(first, full, functools.partial(body, True), jnp.zeros((TQ, HD), jnp.float32))
        dq = lax.fori_loop(full, diag, functools.partial(body, False), dq)
        dq = body(True, diag, dq)
        dq_ref[at, :] = dq * (HALF / 2048)


def remote(src, dst, send, recv, device):
    return pltpu.make_async_remote_copy(
        src_ref=src, dst_ref=dst, send_sem=send, recv_sem=recv, device_id=(device,), device_id_type=MESH
    )


def greet(devices):
    barrier = pltpu.get_barrier_semaphore()
    for device in devices:
        pl.semaphore_signal(barrier, inc=1, device_id=(device,), device_id_type=MESH)
    return barrier


def place():
    me = lax.axis_index("seq")
    return me, lax.rem(me, HEADS), me // HEADS


def group_peers(me, pos):
    return [me - pos + lax.rem(pos + step, HEADS) for step in range(1, HEADS)]


def gather_kernel(x_ref, dg_ref, x_out, dg_out, local, link_s, link_r, core_s, core_r, dg_s, dg_r):
    me, pos, _ = place()
    base, core, y = me - pos, lax.rem(pos, 2), pos // 2
    peers = group_peers(me, pos)
    pl.semaphore_wait(greet(peers), len(peers))
    rows = x_ref.shape[0]
    half = rows // 2
    halves = [pl.ds(0, half), pl.ds(half, half)]

    def at(step):
        return lax.rem(y + step + 4, 4) * 2 + core

    ahead, behind, other = base + at(1), base + at(-1), base + pos + 1 - 2 * core
    own = [
        pltpu.make_async_copy(x_ref, x_out.at[pos], local.at[0]),
        pltpu.make_async_copy(dg_ref.at[:, pl.ds(pl.multiple_of(pos * HD, HD), HD)], dg_out.at[pos], local.at[1]),
    ]
    for copy in own:
        copy.start()
    sent = []

    def send(src, dst, s, r, device):
        copy = remote(src, dst, s, r, device)
        copy.start()
        sent.append(copy)
        return copy

    first = {}
    for h in (0, 1):
        first["up", h] = send(x_ref.at[halves[h]], x_out.at[pos, halves[h]], link_s.at[0, h], link_r.at[0, h], ahead)
        first["down", 1 - h] = send(
            x_ref.at[halves[1 - h]], x_out.at[pos, halves[1 - h]], link_s.at[1, 1 - h], link_r.at[1, 1 - h], behind)
    cores = [send(x_ref, x_out.at[pos], core_s.at[0], core_r.at[0], other)]
    for i, peer in enumerate(peers):
        to = lax.rem(pos + i + 1, HEADS)
        send(dg_ref.at[:, pl.ds(pl.multiple_of(to * HD, HD), HD)], dg_out.at[pos], dg_s.at[i], dg_r.at[i], peer)
    low, high, far = at(-1), at(1), at(2)
    first["up", 0].wait_recv()
    second_up = send(x_out.at[low, halves[0]], x_out.at[low, halves[0]], link_s.at[2, 0], link_r.at[2, 0], ahead)
    first["down", 1].wait_recv()
    second_down = send(x_out.at[high, halves[1]], x_out.at[high, halves[1]], link_s.at[2, 1], link_r.at[2, 1], behind)
    first["up", 1].wait_recv()
    cores.append(send(x_out.at[low], x_out.at[low], core_s.at[1], core_r.at[1], other))
    first["down", 0].wait_recv()
    cores.append(send(x_out.at[high], x_out.at[high], core_s.at[2], core_r.at[2], other))
    second_up.wait_recv()
    second_down.wait_recv()
    cores.append(send(x_out.at[far], x_out.at[far], core_s.at[3], core_r.at[3], other))
    for copy in cores:
        copy.wait_recv()
    for i in range(HEADS - 1):
        sent[5 + i].wait_recv()
    for copy in sent:
        copy.wait_send()
    for copy in own:
        copy.wait()


def gather(x, dg):
    rows = x.shape[0]
    dma = pltpu.SemaphoreType.DMA
    return pl.pallas_call(
        gather_kernel,
        out_shape=[
            jax.ShapeDtypeStruct((HEADS, rows, D), jnp.bfloat16),
            jax.ShapeDtypeStruct((HEADS, rows, HD), jnp.bfloat16),
        ],
        in_specs=[pl.BlockSpec(memory_space=pl.ANY)] * 2,
        out_specs=[pl.BlockSpec(memory_space=pl.ANY)] * 2,
        scratch_shapes=[dma((2,)), dma((3, 2)), dma((3, 2)), dma((4,)), dma((4,)), dma((7,)), dma((7,))],
        compiler_params=pltpu.CompilerParams(collective_id=1, has_side_effects=True),
        name="gather",
    )(x, dg)


def stats_kernel(s_ref, out_ref, held, send_sem, recv_sem):
    me, pos, _ = place()
    peers = group_peers(me, pos)
    pl.semaphore_wait(greet(peers), len(peers))
    copies = []
    for i, peer in enumerate(peers):
        copy = remote(s_ref, held.at[i], send_sem.at[i], recv_sem.at[i], peer)
        copy.start()
        copies.append(copy)
    total = s_ref[...]
    for i, copy in enumerate(copies):
        copy.wait_recv()
        total = total + held[i]
    out_ref[...] = total
    for copy in copies:
        copy.wait_send()


def sum_stats(stats):
    dma = pltpu.SemaphoreType.DMA
    return pl.pallas_call(
        stats_kernel,
        out_shape=jax.ShapeDtypeStruct(stats.shape, jnp.float32),
        in_specs=[pl.BlockSpec(memory_space=pltpu.VMEM)],
        out_specs=pl.BlockSpec(memory_space=pltpu.VMEM),
        scratch_shapes=[pltpu.VMEM((7,) + stats.shape, jnp.float32), dma((7,)), dma((7,))],
        compiler_params=pltpu.CompilerParams(collective_id=2, has_side_effects=True),
        name="stats",
    )(stats)


def final_kernel(d_ref, g_ref, w_ref, d_out, g_out, w_out, held, total, local, d_s, d_r, g_s, g_r, w_s, w_r, last_s, last_r):
    me, pos, group = place()
    base = me - pos
    groups = held.shape[0]
    rows = d_out.shape[0]
    piece = held.shape[1]
    peers = group_peers(me, pos)
    plane = [lax.rem(group + step, groups) * HEADS + pos for step in range(1, groups)]
    dest = (group // 4) * 32 + pos * 4 + lax.rem(group, 4)
    source = ((me // 32) * 4 + lax.rem(me, 4)) * HEADS + lax.rem(me, 32) // 4
    barrier = greet(peers + plane)

    @pl.when(source != me)
    def _():
        pl.semaphore_signal(barrier, inc=1, device_id=(source,), device_id_type=MESH)

    pl.semaphore_wait(barrier, len(peers) + len(plane) + jnp.where(dest != me, 1, 0))

    def part(p):
        return pl.ds(pl.multiple_of(p * piece, piece), piece)

    keep = pltpu.make_async_copy(w_ref.at[part(group)], held.at[group], local.at[0])
    keep.start()
    scattered = []
    for i, peer in enumerate(plane):
        to = lax.rem(group + i + 1, groups)
        copy = remote(w_ref.at[part(to)], held.at[group], w_s.at[i], w_r.at[i], peer)
        copy.start()
        scattered.append(copy)
    mine = pl.ds(pl.multiple_of(pos * HD, HD), HD)
    moved, own = [], []

    def block(p):
        return pl.ds(pl.multiple_of(p * rows, rows), rows)

    for b in range(4):
        cols = pl.ds(pl.multiple_of(b * D + pos * HD, HD), HD)
        own.append(pltpu.make_async_copy(d_ref.at[b, block(pos)], d_out.at[:, cols], local.at[1 + b]))
    own.append(pltpu.make_async_copy(g_ref.at[block(pos)], g_out.at[:, mine], local.at[5]))
    for copy in own:
        copy.start()
    for i, peer in enumerate(peers):
        to = lax.rem(pos + i + 1, HEADS)
        for b in range(4):
            cols = pl.ds(pl.multiple_of(b * D + pos * HD, HD), HD)
            moved.append(remote(d_ref.at[b, block(to)], d_out.at[:, cols], d_s.at[b, i], d_r.at[b, i], peer))
        moved.append(remote(g_ref.at[block(to)], g_out.at[:, mine], g_s.at[i], g_r.at[i], peer))
    for copy in moved:
        copy.start()
    keep.wait()
    for copy in scattered:
        copy.wait_recv()
    acc = held[0].astype(jnp.float32)
    for g in range(1, groups):
        acc = acc + held[g].astype(jnp.float32)
    total[...] = acc

    @pl.when(dest != me)
    def _():
        copy = remote(total, w_out, last_s, last_r, dest)
        copy.start()
        copy.wait()

    @pl.when(dest == me)
    def _():
        copy = pltpu.make_async_copy(total, w_out, local.at[0])
        copy.start()
        copy.wait()

    for copy in moved:
        copy.wait_recv()
    for copy in moved + scattered:
        copy.wait_send()
    for copy in own:
        copy.wait()


def final(d_pre, gated, gw, groups, rows):
    dma = pltpu.SemaphoreType.DMA
    piece = gw.shape[0] // groups
    anywhere = pl.BlockSpec(memory_space=pl.ANY)
    return pl.pallas_call(
        final_kernel,
        out_shape=[
            jax.ShapeDtypeStruct((rows, 4 * D), jnp.bfloat16),
            jax.ShapeDtypeStruct((rows, D), jnp.bfloat16),
            jax.ShapeDtypeStruct((piece, D), jnp.float32),
        ],
        in_specs=[anywhere] * 3,
        out_specs=[anywhere] * 3,
        scratch_shapes=[
            pltpu.VMEM((groups, piece, D), jnp.bfloat16),
            pltpu.VMEM((piece, D), jnp.float32),
            dma((6,)), dma((4, 7)), dma((4, 7)), dma((7,)), dma((7,)),
            dma((groups - 1,)), dma((groups - 1,)), dma(()), dma(()),
        ],
        compiler_params=pltpu.CompilerParams(collective_id=3, has_side_effects=True),
        name="final",
    )(d_pre, gated, gw)


def block_tables(counts, tails, group, own):
    n = counts.shape[0]
    order = jnp.arange(n, dtype=jnp.int32)
    ends = jnp.sum(jnp.where(order[None, :] <= order[:, None], counts[None, :], 0), axis=1)
    blocks = group * own + jnp.arange(own, dtype=jnp.int32)
    starts = ends - counts
    start = jnp.max(jnp.where(starts[None, :] <= blocks[:, None], starts[None, :], 0), axis=1)
    short = jnp.sum(jnp.where(ends[None, :] - 1 == blocks[:, None], tails[None, :] - BLK, 0), axis=1)
    return start - (group - 1) * own, short + BLK


def attention_call(kernel, name, tables, arrays, outs, flops):
    vmem = pl.BlockSpec(memory_space=pltpu.VMEM)
    return pl.pallas_call(
        kernel,
        grid_spec=pltpu.PrefetchScalarGridSpec(
            num_scalar_prefetch=2, grid=(1,), in_specs=[vmem] * len(arrays), out_specs=[vmem] * len(outs)),
        out_shape=outs,
        compiler_params=pltpu.CompilerParams(vmem_limit_bytes=40 * 2**20),
        cost_estimate=pl.CostEstimate(flops=flops, bytes_accessed=4 * 2**20, transcendentals=2**21),
        name=name,
    )(*tables, *arrays)


def per_device(n, tokens, w_in, w_out, counts, tails, grad_out):
    rows = tokens.shape[0]
    span = rows * HEADS
    groups = n // HEADS
    me, pos, group = place()
    tables = block_tables(counts, tails, group, span // BLK)
    shape = jax.ShapeDtypeStruct
    bf, f32 = jnp.bfloat16, jnp.float32
    xf = tokens.astype(f32)
    inv = lax.rsqrt(jnp.mean(xf * xf, axis=-1, keepdims=True) + eps)
    normed = (xf * inv).astype(bf)
    d_gated = dot(grad_out, w_out, NT).astype(bf)
    all_normed, dg = gather(normed, d_gated)
    all_normed = all_normed.reshape(span, D)
    dg = dg.reshape(span, HD)
    w_head = lax.dynamic_slice(w_in.reshape(D, 4, D), (0, 0, pos * HD), (D, 4, HD)).reshape(D, 4 * HD)
    pre = dot(all_normed, w_head, NN)
    sig = jax.nn.sigmoid(pre)
    hidden = (pre * sig).astype(bf)
    slope = (sig * (1.0 + pre * (1.0 - sig))).astype(bf)
    u, v, q, k = (hidden[:, i * HD : (i + 1) * HD] for i in range(4))
    forward = [(i, i + HEADS) for i in range(n - HEADS)]
    behind = lax.ppermute(jnp.stack([k, v]), "seq", forward)
    k_all = jnp.concatenate([behind[0], k])
    v_all = jnp.concatenate([behind[1], v])
    own = span // TQ
    stat_shape = (2, span // BLK, HD)
    attn, stats = attention_call(
        functools.partial(fwd_kernel, own), "attn_fwd", tables, (q, k_all, v_all, u, dg),
        [shape((span, HD), f32), shape(stat_shape, f32)], 10**9)
    stats = sum_stats(stats)
    gated, d_u, d_q, d_k, d_v = attention_call(
        functools.partial(bwd_kernel, own), "attn_bwd", tables, (q, k_all, v_all, u, dg, attn, stats),
        [shape((span, HD), bf), shape((span, HD), bf), shape((span, HD), f32),
         shape((2 * span, HD), f32), shape((2 * span, HD), f32)], 2 * 10**9)
    far = jnp.stack([d_k[:span], d_v[:span]]).astype(bf)
    ahead = lax.ppermute(far, "seq", [(i + HEADS, i) for i in range(n - HEADS)]).astype(f32)
    d_k = (d_k[span:] + ahead[0]) * (1.0 / 2048)
    d_v = (d_v[span:] + ahead[1]) * (1.0 / 2048)
    d_pre = jnp.stack([
        (d.astype(f32) * slope[:, i * HD : (i + 1) * HD].astype(f32)).astype(bf)
        for i, d in enumerate((d_u, d_v, d_q, d_k))
    ])
    gw = jnp.concatenate([dot(d_pre[i], all_normed, TN).astype(bf) for i in range(4)])
    d_full, g_full, grad_w = final(d_pre, gated, gw, groups, rows)
    gf = grad_out.astype(f32)
    layer_out = (xf + dot(g_full, w_out, NN)).astype(bf)
    d_normed = dot(d_full, w_in, NT)
    mean = jnp.mean(d_normed * xf, axis=-1, keepdims=True)
    grad_tokens = (gf + inv * (d_normed - xf * (inv * inv * mean))).astype(bf)
    return layer_out, grad_tokens, grad_w


def solution(mesh):
    in_specs = (P("seq", None), P(), P(), P(), P(), P("seq", None))
    out_specs = (P("seq", None), P("seq", None), P("seq", None))
    return jax.shard_map(
        functools.partial(per_device, mesh.shape["seq"]),
        mesh=mesh, in_specs=in_specs, out_specs=out_specs, check_vma=False,
    )
```

```python
import functools

import jax
import jax.numpy as jnp
from jax import lax
from jax.experimental import pallas as pl
from jax.experimental.pallas import tpu as pltpu
from jax.sharding import PartitionSpec as P

MESH = pl.DeviceIdType.MESH
HEADS = 8
HD = 128
BLK = 128
TQ = 256
D = 1024
eps = 1e-05
HALF = 0.5 * HD ** (-0.5)
NT = (((1,), (1,)), ((), ()))
NN = (((1,), (0,)), ((), ()))
TN = (((0,), (0,)), ((), ()))


def dot(a, b, dims, precision=None):
    return lax.dot_general(a, b, dims, precision=precision, preferred_element_type=jnp.float32)


def tile_bounds(start_ref, t, own):
    lo_a, lo_b = start_ref[2 * t], start_ref[2 * t + 1]
    diag = own + t
    return lo_a, lo_b, lo_a // 2, jnp.minimum((lo_b + 1) // 2, diag), diag


def row_valid(rows_ref, t):
    at = lax.broadcasted_iota(jnp.int32, (TQ, HD), 0)
    limit = jnp.where(at < BLK, rows_ref[2 * t], rows_ref[2 * t + 1] + BLK)
    return at < limit


def keep_mask(lo_a, lo_b, diag, kt):
    r = lax.broadcasted_iota(jnp.int32, (TQ, TQ), 0)
    c = lax.broadcasted_iota(jnp.int32, (TQ, TQ), 1) + kt * TQ
    lo = jnp.where(r < BLK, lo_a * BLK, lo_b * BLK)
    return (c >= lo) & (c <= r + diag * TQ)


def fwd_kernel(own, start_ref, rows_ref, q_ref, k_ref, v_ref, u_ref, dg_ref, attn_ref, stat_ref):
    tiles = q_ref.shape[0] // TQ

    @pl.loop(0, tiles)
    def _(t):
        at = pl.ds(pl.multiple_of(t * TQ, TQ), TQ)
        q = jnp.where(row_valid(rows_ref, t), q_ref[at, :], jnp.zeros((), jnp.bfloat16))
        lo_a, lo_b, first, full, diag = tile_bounds(start_ref, t, own)

        def body(masked, kt, acc):
            cols = pl.ds(pl.multiple_of(kt * TQ, TQ), TQ)
            x = dot(q, k_ref[cols, :], NT)
            if masked:
                x = jnp.where(keep_mask(lo_a, lo_b, diag, kt), x, 0.0)
            w = (x + x * jnp.tanh(x)).astype(jnp.bfloat16)
            return acc + dot(w, v_ref[cols, :], NN)

        acc = lax.fori_loop(first, full, functools.partial(body, True), jnp.zeros((TQ, HD), jnp.float32))
        acc = lax.fori_loop(full, diag, functools.partial(body, False), acc)
        acc = body(True, diag, acc) * (1.0 / 2048)
        attn_ref[at, :] = acc
        ones = jnp.ones((8, HD), jnp.float32)
        da = dg_ref[at, :].astype(jnp.float32) * u_ref[at, :].astype(jnp.float32)
        for s, val in enumerate((acc * acc, da * acc)):
            sums = dot(ones, val, NT)
            stat_ref[s, pl.ds(2 * t, 1), :] = sums[0:1, :BLK]
            stat_ref[s, pl.ds(2 * t + 1, 1), :] = sums[0:1, BLK:]


def column(stat, t):
    tall = []
    for half in range(2):
        pick = lax.broadcasted_iota(jnp.int32, (16, HD), 0) == 2 * t + half
        tall.append(dot(stat, pick.astype(jnp.float32), TN, lax.Precision.HIGHEST))
    return jnp.concatenate(tall, axis=0)


def bwd_kernel(own, start_ref, rows_ref, q_ref, k_ref, v_ref, u_ref, dg_ref, attn_ref, stat_ref, slope_ref,
               gated_ref, du_ref, dq_ref, dk_own, dv_own, dk_far, dv_far, dk_ref, dv_ref):
    span = q_ref.shape[0]
    tiles = span // TQ
    dk_ref[...] = jnp.zeros_like(dk_ref)
    dv_ref[...] = jnp.zeros_like(dv_ref)

    @pl.loop(0, tiles)
    def _(t):
        at = pl.ds(pl.multiple_of(t * TQ, TQ), TQ)
        valid = row_valid(rows_ref, t)
        q = jnp.where(valid, q_ref[at, :], jnp.zeros((), jnp.bfloat16))
        square = column(stat_ref[0], t)
        cross = column(stat_ref[1], t)
        r = lax.rsqrt(square * (1.0 / D) + eps)
        attn = attn_ref[at, :]
        u = u_ref[at, :].astype(jnp.float32)
        dg = dg_ref[at, :].astype(jnp.float32)
        na = attn * r
        gated_ref[at, :] = (na * u).astype(gated_ref.dtype)
        du_ref[at, :] = (na * dg * slope_ref[at, :HD].astype(jnp.float32)).astype(du_ref.dtype)
        d_attn = r * (dg * u) - na * (r * r * cross * (1.0 / D))
        do = jnp.where(valid, d_attn, 0.0).astype(jnp.bfloat16)
        lo_a, lo_b, first, full, diag = tile_bounds(start_ref, t, own)

        def body(masked, kt, dq):
            cols = pl.ds(pl.multiple_of(kt * TQ, TQ), TQ)
            k = k_ref[cols, :]
            x = dot(q, k, NT)
            dw = dot(do, v_ref[cols, :], NT)
            a = 1.0 + jnp.tanh(x)
            w = x * a
            ds = dw * (a + w * (2.0 - a))
            if masked:
                keep = keep_mask(lo_a, lo_b, diag, kt)
                w = jnp.where(keep, w, 0.0)
                ds = jnp.where(keep, ds, 0.0)
            w = w.astype(jnp.bfloat16)
            ds = ds.astype(jnp.bfloat16)
            dv_ref[cols, :] += dot(w, do, TN)
            dk_ref[cols, :] += dot(ds, q, TN)
            return dq + dot(ds, k, NN)

        dq = lax.fori_loop(first, full, functools.partial(body, True), jnp.zeros((TQ, HD), jnp.float32))
        dq = lax.fori_loop(full, diag, functools.partial(body, False), dq)
        dq = body(True, diag, dq)
        dq = dq * (HALF / 2048) * slope_ref[at, 2 * HD : 3 * HD].astype(jnp.float32)
        dq_ref[at, :] = dq.astype(dq_ref.dtype)

    for total, far, mine, b in ((dk_ref, dk_far, dk_own, 3), (dv_ref, dv_far, dv_own, 1)):
        far[...] = (total[:span, :] * (1.0 / 2048)).astype(far.dtype)
        mine[...] = total[span:, :] * (1.0 / 2048)


def remote(src, dst, send, recv, device):
    return pltpu.make_async_remote_copy(
        src_ref=src, dst_ref=dst, send_sem=send, recv_sem=recv, device_id=(device,), device_id_type=MESH
    )


def greet(devices):
    barrier = pltpu.get_barrier_semaphore()
    for device in devices:
        pl.semaphore_signal(barrier, inc=1, device_id=(device,), device_id_type=MESH)
    return barrier


def place():
    me = lax.axis_index("seq")
    return me, lax.rem(me, HEADS), me // HEADS


def group_peers(me, pos):
    return [me - pos + lax.rem(pos + step, HEADS) for step in range(1, HEADS)]


def front_kernel(tok_ref, go_ref, win_ref, wout_ref, x_out, q_out, u_out, k_out, v_out, dg_out, slope_out,
                 xs, wh, wo, dgs, w_sem, out_sem, link_s, link_r, core_s, core_r, dg_s, dg_r, kv_s, kv_r):
    me, pos, _ = place()
    n = lax.axis_size("seq")
    base, core, y = me - pos, lax.rem(pos, 2), pos // 2
    rows = tok_ref.shape[0]
    span = rows * HEADS
    peers = group_peers(me, pos)
    after, before = lax.rem(me + HEADS, n), lax.rem(me + n - HEADS, n)
    barrier = greet(peers + [after, before])
    loads = [
        pltpu.make_async_copy(
            win_ref.at[:, pl.ds(pl.multiple_of(b * D + pos * HD, HD), HD)], wh.at[:, pl.ds(b * HD, HD)], w_sem.at[b])
        for b in range(4)
    ]
    loads.append(pltpu.make_async_copy(wout_ref, wo, w_sem.at[4]))
    for copy in loads:
        copy.start()
    xf = tok_ref[...].astype(jnp.float32)
    inv = lax.rsqrt(jnp.mean(xf * xf, axis=-1, keepdims=True) + eps)
    xs[pos] = (xf * inv).astype(jnp.bfloat16)
    half = rows // 2
    halves = [pl.ds(0, half), pl.ds(half, half)]

    def at(step):
        return lax.rem(y + step + 4, 4) * 2 + core

    flip = 1 - 2 * core
    ahead, behind, other = base + at(1), base + at(-1), base + pos + flip
    sent, local = [], []

    def send(src, dst, s, r, device):
        copy = remote(src, dst, s, r, device)
        copy.start()
        sent.append(copy)
        return copy

    pl.semaphore_wait(barrier, len(peers) + 2)
    first = {}
    for h in (0, 1):
        for way, device, part in (("up", ahead, h), ("down", behind, 1 - h)):
            block = xs.at[pos, halves[part]]
            i = 0 if way == "up" else 1
            first[way, part] = send(block, block, link_s.at[i, part], link_r.at[i, part], device)
    cores = [send(xs.at[pos], xs.at[pos], core_s.at[0], core_r.at[0], other)]
    loads[4].wait()
    dgs[...] = dot(go_ref[...], wo[...], NT).astype(jnp.bfloat16)
    mine = pl.ds(pl.multiple_of(pos * rows, rows), rows)
    grads = []
    for i, peer in enumerate(peers):
        to = lax.rem(pos + i + 1, HEADS)
        cols = pl.ds(pl.multiple_of(to * HD, HD), HD)
        grads.append(send(dgs.at[:, cols], dg_out.at[mine], dg_s.at[i], dg_r.at[i], peer))
    dg_out[mine, :] = dgs[:, pl.ds(pl.multiple_of(pos * HD, HD), HD)]
    for copy in loads[:4]:
        copy.wait()
    halo = []

    def process(slot):
        i = len(local)
        local.append(pltpu.make_async_copy(xs.at[slot], x_out.at[slot], out_sem.at[i]))
        local[-1].start()
        pre = dot(xs[slot], wh[...], NN)
        sig = 0.5 + 0.5 * jnp.tanh(0.5 * pre)
        hidden = pre * sig
        where = pl.ds(pl.multiple_of(slot * rows, rows), rows)
        own = pl.ds(pl.multiple_of(span + slot * rows, rows), rows)
        slope_out[where, :] = (sig * (1.0 + pre - hidden)).astype(jnp.bfloat16)
        u_out[where, :] = hidden[:, :HD].astype(jnp.bfloat16)
        v_out[own, :] = hidden[:, HD : 2 * HD].astype(jnp.bfloat16)
        q_out[where, :] = (hidden[:, 2 * HD : 3 * HD] * HALF).astype(jnp.bfloat16)
        k_out[own, :] = hidden[:, 3 * HD :].astype(jnp.bfloat16)
        halo.append(send(k_out.at[own], k_out.at[where], kv_s.at[0, i], kv_r.at[0, i], after))
        halo.append(send(v_out.at[own], v_out.at[where], kv_s.at[1, i], kv_r.at[1, i], after))

    process(pos)
    cores[0].wait_recv()
    process(pos + flip)
    low, high, far = at(-1), at(1), at(2)
    first["up", 0].wait_recv()
    block = xs.at[low, halves[0]]
    second_up = send(block, block, link_s.at[2, 0], link_r.at[2, 0], ahead)
    first["down", 1].wait_recv()
    block = xs.at[high, halves[1]]
    second_down = send(block, block, link_s.at[2, 1], link_r.at[2, 1], behind)
    first["up", 1].wait_recv()
    cores.append(send(xs.at[low], xs.at[low], core_s.at[1], core_r.at[1], other))
    first["down", 0].wait_recv()
    cores.append(send(xs.at[high], xs.at[high], core_s.at[2], core_r.at[2], other))
    process(low)
    process(high)
    cores[1].wait_recv()
    process(low + flip)
    cores[2].wait_recv()
    process(high + flip)
    second_up.wait_recv()
    second_down.wait_recv()
    cores.append(send(xs.at[far], xs.at[far], core_s.at[3], core_r.at[3], other))
    process(far)
    cores[3].wait_recv()
    process(far + flip)
    for copy in grads + halo:
        copy.wait_recv()
    for copy in sent:
        copy.wait_send()
    for copy in local:
        copy.wait()


def front(tokens, grad_out, w_in, w_out):
    rows = tokens.shape[0]
    span = rows * HEADS
    dma = pltpu.SemaphoreType.DMA
    vmem, anywhere = pl.BlockSpec(memory_space=pltpu.VMEM), pl.BlockSpec(memory_space=pl.ANY)

    def shape(*dims):
        return jax.ShapeDtypeStruct(dims, jnp.bfloat16)

    return pl.pallas_call(
        front_kernel,
        out_shape=[shape(HEADS, rows, D), shape(span, HD), shape(span, HD), shape(2 * span, HD),
                   shape(2 * span, HD), shape(span, HD), shape(span, 4 * HD)],
        in_specs=[vmem, vmem, anywhere, anywhere],
        out_specs=[anywhere] + [vmem] * 6,
        scratch_shapes=[
            pltpu.VMEM((HEADS, rows, D), jnp.bfloat16),
            pltpu.VMEM((D, 4 * HD), jnp.bfloat16),
            pltpu.VMEM((D, D), jnp.bfloat16),
            pltpu.VMEM((rows, D), jnp.bfloat16),
            dma((5,)), dma((HEADS,)), dma((3, 2)), dma((3, 2)), dma((4,)), dma((4,)), dma((7,)), dma((7,)),
            dma((2, HEADS)), dma((2, HEADS)),
        ],
        compiler_params=pltpu.CompilerParams(collective_id=1, has_side_effects=True, vmem_limit_bytes=44 * 2**20),
        name="front",
    )(tokens, grad_out, w_in, w_out)


def stats_kernel(s_ref, out_ref, held, send_sem, recv_sem):
    me, pos, _ = place()
    peers = group_peers(me, pos)
    pl.semaphore_wait(greet(peers), len(peers))
    copies = []
    for i, peer in enumerate(peers):
        copy = remote(s_ref, held.at[i], send_sem.at[i], recv_sem.at[i], peer)
        copy.start()
        copies.append(copy)
    total = s_ref[...]
    for i, copy in enumerate(copies):
        copy.wait_recv()
        total = total + held[i]
    out_ref[...] = total
    for copy in copies:
        copy.wait_send()


def sum_stats(stats):
    dma = pltpu.SemaphoreType.DMA
    return pl.pallas_call(
        stats_kernel,
        out_shape=jax.ShapeDtypeStruct(stats.shape, jnp.float32),
        in_specs=[pl.BlockSpec(memory_space=pltpu.VMEM)],
        out_specs=pl.BlockSpec(memory_space=pltpu.VMEM),
        scratch_shapes=[pltpu.VMEM((7,) + stats.shape, jnp.float32), dma((7,)), dma((7,))],
        compiler_params=pltpu.CompilerParams(collective_id=2, has_side_effects=True, vmem_limit_bytes=2 * 2**20),
        name="stats",
    )(stats)


def back_kernel(tok_ref, go_ref, gated_ref, du_ref, dq_ref, dk_ref, dv_ref, kfar_ref, vfar_ref, slope_ref, x_ref, win_ref,
                wout_ref, out_ref, gt_ref, gw_ref, xs, wi, wo, near, d_full, g_full, d_k, d_v, parts, held, total,
                load_sem, move_s, move_r, halo_s, halo_r, late_s, late_r, w_s, w_r, w_own, last_s, last_r, last_own):
    me, pos, group = place()
    n = lax.axis_size("seq")
    groups = held.shape[0]
    rows = tok_ref.shape[0]
    piece = held.shape[1]
    peers = group_peers(me, pos)
    plane = [lax.rem(group + step, groups) * HEADS + pos for step in range(1, groups)]
    after, before = lax.rem(me + HEADS, n), lax.rem(me + n - HEADS, n)
    z, x = group // 4, lax.rem(group, 4)
    dest = lax.rem(x - z + 4, 4) * 32 + pos * 4 + z
    z_from, branch_from = lax.rem(me, 4), me // 32
    source = (z_from * 4 + lax.rem(branch_from + z_from, 4)) * HEADS + lax.rem(me, 32) // 4
    barrier = greet(peers + plane)

    @pl.when(source != me)
    def _():
        pl.semaphore_signal(barrier, inc=1, device_id=(source,), device_id_type=MESH)

    loads = [
        pltpu.make_async_copy(x_ref, xs, load_sem.at[0]),
        pltpu.make_async_copy(wout_ref, wo, load_sem.at[1]),
        pltpu.make_async_copy(win_ref, wi, load_sem.at[2]),
    ]
    for copy in loads:
        copy.start()

    def block(p):
        return pl.ds(pl.multiple_of(p * rows, rows), rows)

    def columns(b):
        return pl.ds(pl.multiple_of(b * D + pos * HD, HD), HD)

    def send(src, dst, s, r, device):
        copy = remote(src, dst, s, r, device)
        copy.start()
        return copy

    pl.semaphore_wait(barrier, len(peers) + len(plane) + jnp.where(dest != me, 1, 0))
    turn = [lax.rem(pos + i + 1, HEADS) for i in range(HEADS)]
    halo = []
    for i, to in enumerate(turn):
        halo.append([
            send(far.at[block(to)], near.at[j, block(to)], halo_s.at[j, i], halo_r.at[j, i], before)
            for j, far in enumerate((kfar_ref, vfar_ref))
        ])
    mine = pl.ds(pl.multiple_of(pos * HD, HD), HD)
    moved = []
    for i, peer in enumerate(peers):
        moved.append([
            send(gated_ref.at[block(turn[i])], g_full.at[:, mine], move_s.at[0, i], move_r.at[0, i], peer),
            send(du_ref.at[block(turn[i])], d_full.at[:, columns(0)], move_s.at[1, i], move_r.at[1, i], peer),
            send(dq_ref.at[block(turn[i])], d_full.at[:, columns(2)], move_s.at[2, i], move_r.at[2, i], peer),
        ])
    g_full[:, mine] = gated_ref[block(pos), :]
    d_full[:, columns(0)] = du_ref[block(pos), :]
    d_full[:, columns(2)] = dq_ref[block(pos), :]

    scattered = []

    def scatter(b, d_ref):
        parts[b] = dot(d_ref[...], xs[...], TN).astype(jnp.bfloat16)
        for sub in range(4):
            to = sub * 4 + (b + sub) % 4
            src = parts.at[b, pl.ds(sub * piece, piece)]
            copy = remote(src, held.at[group], w_s.at[b, sub], w_r.at[group], to * HEADS + pos)

            @pl.when(group != to)
            def _():
                copy.start()

            @pl.when(group == to)
            def _():
                keep = pltpu.make_async_copy(src, held.at[group], w_own)
                keep.start()
                keep.wait()

            scattered.append((to, copy))

    loads[0].wait()
    scatter(0, du_ref)
    scatter(2, dq_ref)
    late = []
    for i, to in enumerate(turn):
        for copy in halo[i]:
            copy.wait_recv()
        here = block(to)
        for j, (own, dst, b) in enumerate(((dk_ref, d_k, 3), (dv_ref, d_v, 1))):
            slope = slope_ref[here, b * HD : (b + 1) * HD].astype(jnp.float32)
            val = ((own[here, :] + near[j, here, :].astype(jnp.float32)) * slope).astype(jnp.bfloat16)
            dst[here, :] = val
            if i < HEADS - 1:
                late.append(send(dst.at[here], d_full.at[:, columns(b)], late_s.at[j, i], late_r.at[j, i], peers[i]))
            else:
                d_full[:, columns(b)] = val
    scatter(3, d_k)
    scatter(1, d_v)
    loads[1].wait()
    for trio in moved:
        trio[0].wait_recv()
    out_ref[...] = (tok_ref[...].astype(jnp.float32) + dot(g_full[...], wo[...], NN)).astype(jnp.bfloat16)
    loads[2].wait()

    def back_dot(b):
        return dot(d_full[:, b * D : (b + 1) * D], wi[:, b * D : (b + 1) * D], NT)

    for trio in moved:
        trio[1].wait_recv()
        trio[2].wait_recv()
    d_normed = back_dot(0) + back_dot(2)
    for copy in late:
        copy.wait_recv()
    d_normed = d_normed + back_dot(3) + back_dot(1)
    xf = tok_ref[...].astype(jnp.float32)
    inv = lax.rsqrt(jnp.mean(xf * xf, axis=-1, keepdims=True) + eps)
    mean = jnp.mean(d_normed * xf, axis=-1, keepdims=True)
    gt_ref[...] = (go_ref[...].astype(jnp.float32) + inv * (d_normed - xf * (inv * inv * mean))).astype(jnp.bfloat16)

    for step in range(1, groups):
        slot = lax.rem(group + step, groups)
        remote(parts.at[0, pl.ds(0, piece)], held.at[slot], w_s.at[0, 0], w_r.at[slot], after).wait_recv()
    acc = held[0].astype(jnp.float32)
    for g in range(1, groups):
        acc = acc + held[g].astype(jnp.float32)
    total[...] = acc

    @pl.when(dest != me)
    def _():
        copy = remote(total, gw_ref, last_s, last_r, dest)
        copy.start()
        copy.wait()

    @pl.when(dest == me)
    def _():
        copy = pltpu.make_async_copy(total, gw_ref, last_own)
        copy.start()
        copy.wait()

    for to, copy in scattered:
        @pl.when(group != to)
        def _():
            copy.wait_send()

    for trio in moved + halo + [late]:
        for copy in trio:
            copy.wait_send()


def back(tokens, grad_out, gated, d_u, d_q, d_k, d_v, k_far, v_far, slope, all_normed, w_in, w_out, groups):
    rows = tokens.shape[0]
    span = rows * HEADS
    dma = pltpu.SemaphoreType.DMA
    piece = 4 * HD // groups
    bf, f32 = jnp.bfloat16, jnp.float32
    vmem, anywhere = pl.BlockSpec(memory_space=pltpu.VMEM), pl.BlockSpec(memory_space=pl.ANY)
    shape = jax.ShapeDtypeStruct
    return pl.pallas_call(
        back_kernel,
        out_shape=[shape((rows, D), bf), shape((rows, D), bf), shape((piece, D), f32)],
        in_specs=[vmem] * 10 + [anywhere] * 3,
        out_specs=[vmem] * 3,
        scratch_shapes=[
            pltpu.VMEM((span, D), bf), pltpu.VMEM((D, 4 * D), bf), pltpu.VMEM((D, D), bf),
            pltpu.VMEM((2, span, HD), bf), pltpu.VMEM((rows, 4 * D), bf), pltpu.VMEM((rows, D), bf),
            pltpu.VMEM((span, HD), bf), pltpu.VMEM((span, HD), bf), pltpu.VMEM((4, HD, D), bf),
            pltpu.VMEM((groups, piece, D), bf), pltpu.VMEM((piece, D), f32),
            dma((3,)), dma((3, 7)), dma((3, 7)), dma((2, HEADS)), dma((2, HEADS)), dma((2, 7)), dma((2, 7)),
            dma((4, 4)), dma((groups,)), dma(()), dma(()), dma(()), dma(()),
        ],
        compiler_params=pltpu.CompilerParams(collective_id=3, has_side_effects=True, vmem_limit_bytes=46 * 2**20),
        name="back",
    )(tokens, grad_out, gated, d_u, d_q, d_k, d_v, k_far, v_far, slope, all_normed, w_in, w_out)


def block_tables(counts, tails, group, own):
    n = counts.shape[0]
    order = jnp.arange(n, dtype=jnp.int32)
    ends = jnp.sum(jnp.where(order[None, :] <= order[:, None], counts[None, :], 0), axis=1)
    blocks = group * own + jnp.arange(own, dtype=jnp.int32)
    starts = ends - counts
    start = jnp.max(jnp.where(starts[None, :] <= blocks[:, None], starts[None, :], 0), axis=1)
    short = jnp.sum(jnp.where(ends[None, :] - 1 == blocks[:, None], tails[None, :] - BLK, 0), axis=1)
    return start - (group - 1) * own, short + BLK


def attention_call(kernel, name, tables, arrays, outs, flops, scratch=()):
    vmem = pl.BlockSpec(memory_space=pltpu.VMEM)
    return pl.pallas_call(
        kernel,
        grid_spec=pltpu.PrefetchScalarGridSpec(
            num_scalar_prefetch=2, grid=(1,), in_specs=[vmem] * len(arrays), out_specs=[vmem] * len(outs),
            scratch_shapes=scratch),
        out_shape=outs,
        compiler_params=pltpu.CompilerParams(vmem_limit_bytes=40 * 2**20),
        cost_estimate=pl.CostEstimate(flops=flops, bytes_accessed=4 * 2**20, transcendentals=2**21),
        name=name,
    )(*tables, *arrays)


def per_device(n, tokens, w_in, w_out, counts, tails, grad_out):
    rows = tokens.shape[0]
    span = rows * HEADS
    groups = n // HEADS
    me, pos, group = place()
    tables = block_tables(counts, tails, group, span // BLK)
    shape = jax.ShapeDtypeStruct
    bf, f32 = jnp.bfloat16, jnp.float32
    all_normed, q, u, k_all, v_all, dg, slope = front(tokens, grad_out, w_in, w_out)
    all_normed = all_normed.reshape(span, D)
    own = span // TQ
    stat_shape = (2, span // BLK, HD)
    attn, stats = attention_call(
        functools.partial(fwd_kernel, own), "attn_fwd", tables, (q, k_all, v_all, u, dg),
        [shape((span, HD), f32), shape(stat_shape, f32)], 10**9)
    stats = sum_stats(stats)
    small, wide = shape((span, HD), bf), shape((span, HD), f32)
    gradients = attention_call(
        functools.partial(bwd_kernel, own), "attn_bwd", tables, (q, k_all, v_all, u, dg, attn, stats, slope),
        [small, small, small, wide, wide, small, small], 2 * 10**9, [pltpu.VMEM((2 * span, HD), f32)] * 2)
    return back(tokens, grad_out, *gradients, slope, all_normed, w_in, w_out, groups)


def solution(mesh):
    in_specs = (P("seq", None), P(), P(), P(), P(), P("seq", None))
    out_specs = (P("seq", None), P("seq", None), P("seq", None))
    return jax.shard_map(
        functools.partial(per_device, mesh.shape["seq"]),
        mesh=mesh, in_specs=in_specs, out_specs=out_specs, check_vma=False,
    )
```

```python
import functools

import jax
import jax.numpy as jnp
from jax import lax
from jax.experimental import pallas as pl
from jax.experimental.pallas import tpu as pltpu
from jax.sharding import PartitionSpec as P

MESH = pl.DeviceIdType.MESH
HEADS = 8
HD = 128
BLK = 128
D = 1024
eps = 1e-05
HALF = 0.5 * HD ** (-0.5)
NT = (((1,), (1,)), ((), ()))
NN = (((1,), (0,)), ((), ()))
TN = (((0,), (0,)), ((), ()))
WIDE = 512
STEP = 256


def dot(a, b, dims):
    return lax.dot_general(a, b, dims, preferred_element_type=jnp.float32)


def group_index():
    return lax.axis_index("seq") // HEADS


def rows_at(start, size):
    return pl.ds(pl.multiple_of(start, BLK), size)


def for_query_tiles(counts_ref, tails_ref, span, visit):
    blocks = span // BLK
    first = group_index() * blocks
    shift = span - first * BLK

    def user(n, begin):
        end = begin + counts_ref[n]
        low, high = jnp.maximum(begin, first), jnp.minimum(end, first + blocks)

        @pl.when(high > low)
        def _():
            count = high - low
            rest = lax.rem(count, 4)
            wide = count // 4 + jnp.where(rest == 3, 1, 0)
            stop = jnp.minimum((end - 1) * BLK + tails_ref[n], high * BLK) + shift
            row, key = low * BLK + shift, begin * BLK + shift
            pl.loop(0, wide)(lambda i: visit(WIDE, row + i * WIDE, key, stop))
            pl.when((rest == 1) | (rest == 2))(lambda: visit(WIDE // 2, row + (count // 4) * WIDE, key, stop))

        return end

    lax.fori_loop(0, counts_ref.shape[0], user, 0)


def valid_rows(size, start, row, stop):
    r = lax.broadcasted_iota(jnp.int32, (size, HD), 0) + start
    return (r >= row) & (r < stop)


def for_key_tiles(size, start, key, body, carry):
    r = lax.broadcasted_iota(jnp.int32, (size, size), 0)
    c = lax.broadcasted_iota(jnp.int32, (size, size), 1)
    back = jnp.maximum(start - key, 0)
    full = back // WIDE

    def plain(j, carry):
        return body(rows_at(start - (j + 1) * WIDE, WIDE), None, carry)

    def part(_, carry):
        end = start - full * WIDE
        base = jnp.maximum(end - WIDE, 0)
        col = lax.broadcasted_iota(jnp.int32, (size, WIDE), 1) + base
        return body(rows_at(base, WIDE), (col >= key) & (col < end), carry)

    carry = lax.fori_loop(0, full, plain, carry)
    carry = lax.fori_loop(0, jnp.where(back > full * WIDE, 1, 0), part, carry)
    return body(rows_at(start, size), (c <= r) & (c >= key - start), carry)


def fwd_kernel(counts_ref, tails_ref, q_ref, kv_ref, u_ref, dg_ref, attn_ref, stat_ref):
    span = q_ref.shape[0]
    attn_ref[...] = jnp.zeros_like(attn_ref)

    def visit(size, row, key, stop):
        start = jnp.minimum(row, 2 * span - size)
        at = rows_at(start - span, size)
        q = jnp.where(valid_rows(size, start, row, stop), q_ref[at, :], jnp.zeros((), jnp.bfloat16))

        def body(cols, keep, acc):
            x = dot(q, kv_ref[cols, :HD], NT)
            if keep is not None:
                x = jnp.where(keep, x, 0.0)
            w = (x + x * jnp.tanh(x)).astype(jnp.bfloat16)
            return acc + dot(w, kv_ref[cols, HD:], NN)

        attn_ref[at, :] += for_key_tiles(size, start, key, body, jnp.zeros((size, HD), jnp.float32)) * (1.0 / 2048)

    for_query_tiles(counts_ref, tails_ref, span, visit)
    ones = jnp.ones((8, HD), jnp.float32)
    for t in range(span // STEP):
        at = pl.ds(t * STEP, STEP)
        acc = attn_ref[at, :]
        da = dg_ref[at, :].astype(jnp.float32) * u_ref[at, :].astype(jnp.float32)
        for s, val in enumerate((acc * acc, da * acc)):
            sums = dot(ones, val, NT)
            for i in range(STEP // BLK):
                stat_ref[s, pl.ds(t * (STEP // BLK) + i, 1), :] = sums[0:1, i * BLK : (i + 1) * BLK]


def bwd_kernel(counts_ref, tails_ref, q_ref, kv_ref, u_ref, dg_ref, attn_ref, stat_ref, slope_ref,
               gated_ref, du_ref, dq_ref, own_ref, far_ref, dk_ref, dv_ref, do_ref, dq_sum):
    span = q_ref.shape[0]
    for ref in (dk_ref, dv_ref, dq_sum):
        ref[...] = jnp.zeros_like(ref)
    r_all = lax.rsqrt(stat_ref[0] * (1.0 / D) + eps)
    c_all = r_all * r_all * r_all * stat_ref[1] * (1.0 / D)
    r_all, c_all = r_all.T, c_all.T
    for t in range(span // BLK):
        at = pl.ds(t * BLK, BLK)
        r, c = (jnp.broadcast_to(val[:, t : t + 1], (BLK, HD)) for val in (r_all, c_all))
        attn = attn_ref[at, :]
        u = u_ref[at, :].astype(jnp.float32)
        dg = dg_ref[at, :].astype(jnp.float32)
        na = attn * r
        gated_ref[at, :] = (na * u).astype(gated_ref.dtype)
        du_ref[at, :] = (na * dg * slope_ref[at, :HD].astype(jnp.float32)).astype(du_ref.dtype)
        do_ref[at, :] = (r * (dg * u) - attn * c).astype(do_ref.dtype)

    def visit(size, row, key, stop):
        start = jnp.minimum(row, 2 * span - size)
        at = rows_at(start - span, size)
        valid = valid_rows(size, start, row, stop)
        q = jnp.where(valid, q_ref[at, :], jnp.zeros((), jnp.bfloat16))
        do = jnp.where(valid, do_ref[at, :], jnp.zeros((), jnp.bfloat16))

        def body(cols, keep, dq):
            k = kv_ref[cols, :HD]
            x = dot(q, k, NT)
            dw = dot(do, kv_ref[cols, HD:], NT)
            a = 1.0 + jnp.tanh(x)
            w = x * a
            ds = dw * (a + w * (2.0 - a))
            if keep is not None:
                w = jnp.where(keep, w, 0.0)
                ds = jnp.where(keep, ds, 0.0)
            w = w.astype(jnp.bfloat16)
            ds = ds.astype(jnp.bfloat16)
            dv_ref[cols, :] += dot(w, do, TN)
            dk_ref[cols, :] += dot(ds, q, TN)
            return dq + dot(ds, k, NN)

        dq_sum[at, :] += for_key_tiles(size, start, key, body, jnp.zeros((size, HD), jnp.float32))

    for_query_tiles(counts_ref, tails_ref, span, visit)
    dq = dq_sum[...] * (HALF / 2048) * slope_ref[:, 2 * HD : 3 * HD].astype(jnp.float32)
    dq_ref[...] = dq.astype(dq_ref.dtype)
    for total, cols in ((dk_ref, slice(0, HD)), (dv_ref, slice(HD, 2 * HD))):
        far_ref[:, cols] = (total[:span, :] * (1.0 / 2048)).astype(far_ref.dtype)
        own_ref[:, cols] = total[span:, :] * (1.0 / 2048)


def remote(src, dst, send, recv, device):
    return pltpu.make_async_remote_copy(
        src_ref=src, dst_ref=dst, send_sem=send, recv_sem=recv, device_id=(device,), device_id_type=MESH
    )


def greet(devices):
    barrier = pltpu.get_barrier_semaphore()
    for device in devices:
        pl.semaphore_signal(barrier, inc=1, device_id=(device,), device_id_type=MESH)
    return barrier


def place():
    me = lax.axis_index("seq")
    return me, lax.rem(me, HEADS), me // HEADS


def group_peers(me, pos):
    return [me - pos + lax.rem(pos + step, HEADS) for step in range(1, HEADS)]


def front_kernel(tok_ref, go_ref, win_ref, wout_ref, x_out, q_out, u_out, kv_out, dg_out, slope_out,
                 tok, go, xs, wh, wo, dgs, slope, load_sem, out_sem, slope_sem, link_s, link_r, core_s, core_r, dg_s, dg_r, kv_s, kv_r):
    me, pos, _ = place()
    n = lax.axis_size("seq")
    base, core, y = me - pos, lax.rem(pos, 2), pos // 2
    rows = tok.shape[0]
    span = rows * HEADS
    half = rows // 2
    peers = group_peers(me, pos)
    after, before = lax.rem(me + HEADS, n), lax.rem(me + n - HEADS, n)
    loads = [pltpu.make_async_copy(tok_ref, tok, load_sem.at[0])]
    loads += [
        pltpu.make_async_copy(
            win_ref.at[:, pl.ds(pl.multiple_of(b * D + pos * HD, HD), HD)], wh.at[:, pl.ds(b * HD, HD)],
            load_sem.at[1 + b])
        for b in range(4)
    ]
    loads += [pltpu.make_async_copy(go_ref, go, load_sem.at[5]), pltpu.make_async_copy(wout_ref, wo, load_sem.at[6])]
    for copy in loads:
        copy.start()
    barrier = greet(peers + [after, before])
    loads[0].wait()
    xf = tok[...].astype(jnp.float32)
    inv = lax.rsqrt(jnp.mean(xf * xf, axis=-1, keepdims=True) + eps)
    xs[pos] = (xf * inv).astype(jnp.bfloat16)

    def at(step):
        return lax.rem(y + step + 4, 4) * 2 + core

    flip = 1 - 2 * core
    ahead, behind, other = base + at(1), base + at(-1), base + pos + flip
    low, high, far = at(-1), at(1), at(2)
    sent, local, halo = [], [], []

    def send(src, dst, s, r, device):
        copy = remote(src, dst, s, r, device)
        copy.start()
        sent.append(copy)
        return copy

    def part(slot, h):
        return xs.at[slot, pl.ds(h * half, half)]

    def link(slot, i, h, device):
        return send(part(slot, h), part(slot, h), link_s.at[i, h], link_r.at[i, h], device)

    def across(slot, i, h):
        return send(part(slot, h), part(slot, h), core_s.at[i, h], core_r.at[i, h], other)

    pl.semaphore_wait(barrier, len(peers) + 2)
    up = {0: link(pos, 0, 0, ahead)}
    down = {1: link(pos, 1, 1, behind)}
    cores = {}
    for h in (0, 1):
        cores[0, h] = across(pos, 0, h)
    up[1] = link(pos, 0, 1, ahead)
    down[0] = link(pos, 1, 0, behind)
    for copy in loads[1:5]:
        copy.wait()

    def process(slot, h, i):
        pre = dot(xs[slot, h * half : (h + 1) * half, :], wh[...], NN)
        sig = 0.5 + 0.5 * jnp.tanh(0.5 * pre)
        hidden = pre * sig
        at_row = pl.multiple_of(slot * rows + h * half, half)
        where, own = pl.ds(at_row, half), pl.ds(pl.multiple_of(span + at_row, half), half)
        kv_out[own, :HD] = hidden[:, 3 * HD :].astype(jnp.bfloat16)
        kv_out[own, HD:] = hidden[:, HD : 2 * HD].astype(jnp.bfloat16)
        copy = remote(kv_out.at[own], kv_out.at[where], kv_s.at[i, h], kv_r.at[i, h], after)
        needed = slot + h > 0
        pl.when(needed)(copy.start)
        halo.append((needed, copy))
        slope[where, :] = (sig * (1.0 + pre - hidden)).astype(jnp.bfloat16)
        local.append(pltpu.make_async_copy(slope.at[where], slope_out.at[where], slope_sem.at[i, h]))
        local[-1].start()
        u_out[where, :] = hidden[:, :HD].astype(jnp.bfloat16)
        q_out[where, :] = (hidden[:, 2 * HD : 3 * HD] * HALF).astype(jnp.bfloat16)

    def keep(slot):
        local.append(pltpu.make_async_copy(xs.at[slot], x_out.at[slot], out_sem.at[slot]))
        local[-1].start()

    for h in (0, 1):
        process(pos, h, 0)
    for h in (0, 1):
        cores[0, h].wait_recv()
        process(pos + flip, h, 1)
    up[0].wait_recv()
    second_up = link(low, 2, 0, ahead)
    cores[1, 0] = across(low, 1, 0)
    down[1].wait_recv()
    second_down = link(high, 2, 1, behind)
    cores[2, 1] = across(high, 2, 1)
    process(low, 0, 2)
    process(high, 1, 3)
    loads[5].wait()
    loads[6].wait()
    dgs[...] = dot(go[...], wo[...], NT).astype(jnp.bfloat16)
    mine = pl.ds(pl.multiple_of(pos * rows, rows), rows)
    grads = []
    for i, peer in enumerate(peers):
        to = lax.rem(pos + i + 1, HEADS)
        cols = pl.ds(pl.multiple_of(to * HD, HD), HD)
        grads.append(send(dgs.at[:, cols], dg_out.at[mine], dg_s.at[i], dg_r.at[i], peer))
    dg_out[mine, :] = dgs[:, pl.ds(pl.multiple_of(pos * HD, HD), HD)]
    cores[1, 0].wait_recv()
    process(low + flip, 0, 4)
    cores[2, 1].wait_recv()
    process(high + flip, 1, 5)
    up[1].wait_recv()
    cores[1, 1] = across(low, 1, 1)
    down[0].wait_recv()
    cores[2, 0] = across(high, 2, 0)
    process(low, 1, 2)
    process(high, 0, 3)
    cores[1, 1].wait_recv()
    process(low + flip, 1, 4)
    cores[2, 0].wait_recv()
    process(high + flip, 0, 5)
    keep(pos)
    keep(pos + flip)
    keep(low)
    keep(high)
    keep(low + flip)
    keep(high + flip)
    second_up.wait_recv()
    cores[3, 0] = across(far, 3, 0)
    second_down.wait_recv()
    cores[3, 1] = across(far, 3, 1)
    for h in (0, 1):
        process(far, h, 6)
    for h in (0, 1):
        cores[3, h].wait_recv()
        process(far + flip, h, 7)
    keep(far)
    keep(far + flip)
    kv_out[:BLK, :] = jnp.zeros((BLK, 2 * HD), jnp.bfloat16)
    for copy in grads:
        copy.wait_recv()
    for needed, copy in halo:
        pl.when(needed)(copy.wait)
    for copy in sent:
        copy.wait_send()
    for copy in local:
        copy.wait()


def front(tokens, grad_out, w_in, w_out):
    rows = tokens.shape[0]
    span = rows * HEADS
    dma = pltpu.SemaphoreType.DMA
    vmem, hbm = pl.BlockSpec(memory_space=pltpu.VMEM), pl.BlockSpec(memory_space=pltpu.HBM)

    def shape(*dims):
        return jax.ShapeDtypeStruct(dims, jnp.bfloat16)

    def scratch(*dims):
        return pltpu.VMEM(dims, jnp.bfloat16)

    return pl.pallas_call(
        front_kernel,
        out_shape=[shape(HEADS, rows, D), shape(span, HD), shape(span, HD), shape(2 * span, 2 * HD),
                   shape(span, HD), shape(span, 4 * HD)],
        in_specs=[hbm] * 4,
        out_specs=[hbm] + [vmem] * 4 + [hbm],
        scratch_shapes=[
            scratch(rows, D), scratch(rows, D), scratch(HEADS, rows, D), scratch(D, 4 * HD), scratch(D, D),
            scratch(rows, D), scratch(span, 4 * HD), dma((7,)), dma((HEADS,)), dma((HEADS, 2)), dma((3, 2)), dma((3, 2)), dma((4, 2)), dma((4, 2)),
            dma((7,)), dma((7,)), dma((HEADS, 2)), dma((HEADS, 2)),
        ],
        compiler_params=pltpu.CompilerParams(collective_id=1, has_side_effects=True, vmem_limit_bytes=48 * 2**20),
        name="front",
    )(tokens, grad_out, w_in, w_out)


def stats_kernel(s_ref, out_ref, held, send_sem, recv_sem):
    me, pos, _ = place()
    peers = group_peers(me, pos)
    pl.semaphore_wait(greet(peers), len(peers))
    copies = []
    for i, peer in enumerate(peers):
        copy = remote(s_ref, held.at[i], send_sem.at[i], recv_sem.at[i], peer)
        copy.start()
        copies.append(copy)
    total = s_ref[...]
    for i, copy in enumerate(copies):
        copy.wait_recv()
        total = total + held[i]
    out_ref[...] = total
    for copy in copies:
        copy.wait_send()


def sum_stats(stats):
    dma = pltpu.SemaphoreType.DMA
    return pl.pallas_call(
        stats_kernel,
        out_shape=jax.ShapeDtypeStruct(stats.shape, jnp.float32),
        in_specs=[pl.BlockSpec(memory_space=pltpu.VMEM)],
        out_specs=pl.BlockSpec(memory_space=pltpu.VMEM),
        scratch_shapes=[pltpu.VMEM((7,) + stats.shape, jnp.float32), dma((7,)), dma((7,))],
        compiler_params=pltpu.CompilerParams(collective_id=2, has_side_effects=True, vmem_limit_bytes=2 * 2**20),
        name="stats",
    )(stats)


def back_kernel(tok_ref, go_ref, gated_ref, du_ref, dq_ref, own_ref, far_ref, slope_ref, x_ref, win_ref,
                wout_ref, out_ref, gt_ref, gw_ref, xs, wi, wo, near, d_full, g_full, d_kv, grads, parts, held, total,
                load_sem, move_s, move_r, halo_s, halo_r, late_s, late_r, w_s, w_r, w_own, last_s, last_r, last_own):
    me, pos, group = place()
    n = lax.axis_size("seq")
    groups = held.shape[0]
    rows = tok_ref.shape[0]
    piece = held.shape[1]
    peers = group_peers(me, pos)
    plane = [lax.rem(group + step, groups) * HEADS + pos for step in range(1, groups)]
    after, before = lax.rem(me + HEADS, n), lax.rem(me + n - HEADS, n)
    z, x = group // 4, lax.rem(group, 4)
    dest = lax.rem(x - z + 4, 4) * 32 + pos * 4 + z
    z_from, branch_from = lax.rem(me, 4), me // 32
    source = (z_from * 4 + lax.rem(branch_from + z_from, 4)) * HEADS + lax.rem(me, 32) // 4
    barrier = greet(peers + plane)

    @pl.when(source != me)
    def _():
        pl.semaphore_signal(barrier, inc=1, device_id=(source,), device_id_type=MESH)

    loads = [
        pltpu.make_async_copy(x_ref, xs, load_sem.at[0]),
        pltpu.make_async_copy(wout_ref, wo, load_sem.at[1]),
        pltpu.make_async_copy(win_ref, wi, load_sem.at[2]),
    ]
    for copy in loads:
        copy.start()

    def block(p):
        return pl.ds(pl.multiple_of(p * rows, rows), rows)

    def columns(b):
        return pl.ds(pl.multiple_of(b * D + pos * HD, HD), HD)

    def send(src, dst, s, r, device):
        copy = remote(src, dst, s, r, device)
        copy.start()
        return copy

    pl.semaphore_wait(barrier, len(peers) + len(plane) + jnp.where(dest != me, 1, 0))
    turn = [lax.rem(pos + i + 1, HEADS) for i in range(HEADS)]
    halo = []
    for i, to in enumerate(turn):
        for h in (0, 1):
            part = pl.ds(pl.multiple_of(to * rows + h * BLK, BLK), BLK)
            copy = remote(far_ref.at[part], near.at[part], halo_s.at[i, h], halo_r.at[i, h], before)
            needed = to + h > 0
            pl.when(needed)(copy.start)
            halo.append((needed, copy))
    near[:BLK, :] = jnp.zeros((BLK, 2 * HD), jnp.bfloat16)
    mine = pl.ds(pl.multiple_of(pos * HD, HD), HD)
    moved = []
    for i, peer in enumerate(peers):
        moved.append([
            send(gated_ref.at[block(turn[i])], g_full.at[:, mine], move_s.at[0, i], move_r.at[0, i], peer),
            send(du_ref.at[block(turn[i])], d_full.at[:, columns(0)], move_s.at[1, i], move_r.at[1, i], peer),
            send(dq_ref.at[block(turn[i])], d_full.at[:, columns(2)], move_s.at[2, i], move_r.at[2, i], peer),
        ])
    g_full[:, mine] = gated_ref[block(pos), :]
    d_full[:, columns(0)] = du_ref[block(pos), :]
    d_full[:, columns(2)] = dq_ref[block(pos), :]

    scattered = []

    def scatter(b, grad):
        parts[b] = grad.astype(jnp.bfloat16)
        for sub in range(4):
            to = sub * 4 + (b + sub) % 4
            src = parts.at[b, pl.ds(sub * piece, piece)]
            copy = remote(src, held.at[group], w_s.at[b, sub], w_r.at[group], to * HEADS + pos)

            @pl.when(group != to)
            def _():
                copy.start()

            @pl.when(group == to)
            def _():
                keep = pltpu.make_async_copy(src, held.at[group], w_own)
                keep.start()
                keep.wait()

            scattered.append((to, copy))

    loads[0].wait()
    scatter(0, dot(du_ref[...], xs[...], TN))
    scatter(2, dot(dq_ref[...], xs[...], TN))
    late = []
    for i, to in enumerate(turn):
        for needed, copy in halo[2 * i : 2 * i + 2]:
            pl.when(needed)(copy.wait_recv)
        here = block(to)
        for j, b in enumerate((3, 1)):
            cols = slice(j * HD, (j + 1) * HD)
            slope = slope_ref[here, b * HD : (b + 1) * HD].astype(jnp.float32)
            val = ((own_ref[here, cols] + near[here, cols].astype(jnp.float32)) * slope).astype(jnp.bfloat16)
            d_kv[j, here, :] = val
            if i < HEADS - 1:
                dst = d_full.at[:, columns(b)]
                late.append(send(d_kv.at[j, here], dst, late_s.at[j, i], late_r.at[j, i], peers[i]))
            else:
                d_full[:, columns(b)] = val
        for j, b in enumerate((3, 1)):
            grad = dot(d_kv[j, here, :], xs[here, :], TN)
            if i == 0:
                grads[j] = grad
            elif i < HEADS - 1:
                grads[j] += grad
            else:
                scatter(b, grads[j] + grad)
    loads[1].wait()
    for trio in moved:
        trio[0].wait_recv()
    out_ref[...] = (tok_ref[...].astype(jnp.float32) + dot(g_full[...], wo[...], NN)).astype(jnp.bfloat16)
    loads[2].wait()

    def back_dot(b):
        return dot(d_full[:, b * D : (b + 1) * D], wi[:, b * D : (b + 1) * D], NT)

    for trio in moved:
        trio[1].wait_recv()
        trio[2].wait_recv()
    d_normed = back_dot(0) + back_dot(2)
    for step in range(1, groups):
        slot = lax.rem(group + step, groups)
        remote(parts.at[0, pl.ds(0, piece)], held.at[slot], w_s.at[0, 0], w_r.at[slot], after).wait_recv()
    acc = held[0].astype(jnp.float32)
    for g in range(1, groups):
        acc = acc + held[g].astype(jnp.float32)
    total[...] = acc
    last = remote(total, gw_ref, last_s, last_r, dest)
    stay = pltpu.make_async_copy(total, gw_ref, last_own)
    pl.when(dest != me)(last.start)
    pl.when(dest == me)(stay.start)
    for copy in late:
        copy.wait_recv()
    d_normed = d_normed + back_dot(3) + back_dot(1)
    xf = tok_ref[...].astype(jnp.float32)
    inv = lax.rsqrt(jnp.mean(xf * xf, axis=-1, keepdims=True) + eps)
    mean = jnp.mean(d_normed * xf, axis=-1, keepdims=True)
    gt_ref[...] = (go_ref[...].astype(jnp.float32) + inv * (d_normed - xf * (inv * inv * mean))).astype(jnp.bfloat16)
    pl.when(dest != me)(last.wait)
    pl.when(dest == me)(stay.wait)
    for to, copy in scattered:
        pl.when(group != to)(copy.wait_send)
    for needed, copy in halo:
        pl.when(needed)(copy.wait_send)
    for copy in [copy for trio in moved for copy in trio] + late:
        copy.wait_send()


def back(tokens, grad_out, gated, d_u, d_q, own, far, slope, all_normed, w_in, w_out, groups):
    rows = tokens.shape[0]
    span = rows * HEADS
    dma = pltpu.SemaphoreType.DMA
    piece = 4 * HD // groups
    bf, f32 = jnp.bfloat16, jnp.float32
    vmem, anywhere = pl.BlockSpec(memory_space=pltpu.VMEM), pl.BlockSpec(memory_space=pl.ANY)
    shape = jax.ShapeDtypeStruct
    return pl.pallas_call(
        back_kernel,
        out_shape=[shape((rows, D), bf), shape((rows, D), bf), shape((piece, D), f32)],
        in_specs=[vmem] * 8 + [anywhere] * 3,
        out_specs=[vmem] * 3,
        scratch_shapes=[
            pltpu.VMEM((span, D), bf), pltpu.VMEM((D, 4 * D), bf), pltpu.VMEM((D, D), bf),
            pltpu.VMEM((span, 2 * HD), bf), pltpu.VMEM((rows, 4 * D), bf), pltpu.VMEM((rows, D), bf),
            pltpu.VMEM((2, span, HD), bf), pltpu.VMEM((2, HD, D), f32), pltpu.VMEM((4, HD, D), bf),
            pltpu.VMEM((groups, piece, D), bf), pltpu.VMEM((piece, D), f32),
            dma((3,)), dma((3, 7)), dma((3, 7)), dma((HEADS, 2)), dma((HEADS, 2)), dma((2, 7)), dma((2, 7)),
            dma((4, 4)), dma((groups,)), dma(()), dma(()), dma(()), dma(()),
        ],
        compiler_params=pltpu.CompilerParams(collective_id=3, has_side_effects=True, vmem_limit_bytes=46 * 2**20),
        name="back",
    )(tokens, grad_out, gated, d_u, d_q, own, far, slope, all_normed, w_in, w_out)


def attention_call(kernel, name, tables, arrays, outs, flops, scratch=()):
    vmem = pl.BlockSpec(memory_space=pltpu.VMEM)
    return pl.pallas_call(
        kernel,
        grid_spec=pltpu.PrefetchScalarGridSpec(
            num_scalar_prefetch=2, grid=(1,), in_specs=[vmem] * len(arrays), out_specs=[vmem] * len(outs),
            scratch_shapes=scratch),
        out_shape=outs,
        compiler_params=pltpu.CompilerParams(vmem_limit_bytes=40 * 2**20),
        cost_estimate=pl.CostEstimate(flops=flops, bytes_accessed=4 * 2**20, transcendentals=2**21),
        name=name,
    )(*tables, *arrays)


def per_device(n, tokens, w_in, w_out, counts, tails, grad_out):
    rows = tokens.shape[0]
    span = rows * HEADS
    shape = jax.ShapeDtypeStruct
    bf, f32 = jnp.bfloat16, jnp.float32
    all_normed, q, u, kv, dg, slope = front(tokens, grad_out, w_in, w_out)
    all_normed = all_normed.reshape(span, D)
    users = (counts, tails)
    attn, stats = attention_call(
        fwd_kernel, "attn_fwd", users, (q, kv, u, dg),
        [shape((span, HD), f32), shape((2, span // BLK, HD), f32)], 10**9)
    stats = sum_stats(stats)
    small, pair = shape((span, HD), bf), (span, 2 * HD)
    both = pltpu.VMEM((2 * span, HD), f32)
    gradients = attention_call(
        bwd_kernel, "attn_bwd", users, (q, kv, u, dg, attn, stats, slope),
        [small, small, small, shape(pair, f32), shape(pair, bf)], 2 * 10**9,
        [both, both, pltpu.VMEM((span, HD), bf), pltpu.VMEM((span, HD), f32)])
    return back(tokens, grad_out, *gradients, slope, all_normed, w_in, w_out, n // HEADS)


def solution(mesh):
    in_specs = (P("seq", None), P(), P(), P(), P(), P("seq", None))
    out_specs = (P("seq", None), P("seq", None), P("seq", None))
    return jax.shard_map(
        functools.partial(per_device, mesh.shape["seq"]),
        mesh=mesh, in_specs=in_specs, out_specs=out_specs, check_vma=False,
    )
```

```python
import functools

import jax
import jax.numpy as jnp
from jax import lax
from jax.experimental import pallas as pl
from jax.experimental.pallas import tpu as pltpu
from jax.sharding import PartitionSpec as P

MESH = pl.DeviceIdType.MESH
HEADS = 8
HD = 128
BLK = 128
D = 1024
eps = 1e-05
HALF = 0.5 * HD ** (-0.5)
NT = (((1,), (1,)), ((), ()))
NN = (((1,), (0,)), ((), ()))
TN = (((0,), (0,)), ((), ()))
WIDE = 512
STEP = 256


def dot(a, b, dims):
    return lax.dot_general(a, b, dims, preferred_element_type=jnp.float32)


def group_index():
    return lax.axis_index("seq") // HEADS


def rows_at(start, size):
    return pl.ds(pl.multiple_of(start, BLK), size)


def for_query_tiles(counts_ref, tails_ref, span, visit):
    blocks = span // BLK
    first = group_index() * blocks
    shift = span - first * BLK

    def user(n, begin):
        end = begin + counts_ref[n]
        low, high = jnp.maximum(begin, first), jnp.minimum(end, first + blocks)

        @pl.when(high > low)
        def _():
            count = high - low
            rest = lax.rem(count, 4)
            wide = count // 4 + jnp.where(rest == 3, 1, 0)
            stop = jnp.minimum((end - 1) * BLK + tails_ref[n], high * BLK) + shift
            row, key = low * BLK + shift, begin * BLK + shift
            pl.loop(0, wide)(lambda i: visit(WIDE, row + i * WIDE, key, stop))
            pl.when((rest == 1) | (rest == 2))(lambda: visit(WIDE // 2, row + (count // 4) * WIDE, key, stop))

        return end

    lax.fori_loop(0, counts_ref.shape[0], user, 0)


def valid_rows(size, start, row, stop):
    r = lax.broadcasted_iota(jnp.int32, (size, HD), 0) + start
    return (r >= row) & (r < stop)


def for_key_tiles(size, start, key, body, diagonal, carry, k_dim):
    back = jnp.maximum(start - key, 0)
    full = back // WIDE

    def index(shape, dim):
        return lax.broadcasted_iota(jnp.int32, shape, dim)

    def plain(j, carry):
        return carry + body(rows_at(start - (j + 1) * WIDE, WIDE), slice(0, size), None)

    def part(_, carry):
        end = start - full * WIDE
        base = jnp.maximum(end - WIDE, 0)
        col = index((size, WIDE) if k_dim else (WIDE, size), k_dim) + base
        return carry + body(rows_at(base, WIDE), slice(0, size), (col >= key) & (col < end))

    def piece(q_low, q_high, k_low, k_high):
        dims = (q_high - q_low, k_high - k_low)
        dims = dims if k_dim else dims[::-1]
        r, c = index(dims, 1 - k_dim) + q_low, index(dims, k_dim) + k_low
        keep = (c <= r) & (c >= key - start)
        return body(rows_at(start + k_low, k_high - k_low), slice(q_low, q_high), keep)

    carry = lax.fori_loop(0, full, plain, carry)
    carry = lax.fori_loop(0, jnp.where(back > full * WIDE, 1, 0), part, carry)
    return carry + diagonal(piece, size)


def fwd_kernel(counts_ref, tails_ref, q_ref, kv_ref, u_ref, dg_ref, attn_ref, stat_ref):
    span = q_ref.shape[0]
    attn_ref[...] = jnp.zeros_like(attn_ref)

    def visit(size, row, key, stop):
        start = jnp.minimum(row, 2 * span - size)
        at = rows_at(start - span, size)
        q = jnp.where(valid_rows(size, start, row, stop), q_ref[at, :], jnp.zeros((), jnp.bfloat16))

        def body(cols, picked, keep):
            x = dot(q[picked, :], kv_ref[cols, :HD], NT)
            if keep is not None:
                x = jnp.where(keep, x, 0.0)
            w = (x + x * jnp.tanh(x)).astype(jnp.bfloat16)
            return dot(w, kv_ref[cols, HD:], NN)

        def diagonal(piece, size):
            return piece(0, size, 0, size)

        acc = for_key_tiles(size, start, key, body, diagonal, jnp.zeros((size, HD), jnp.float32), 1)
        attn_ref[at, :] += acc * (1.0 / 2048)

    for_query_tiles(counts_ref, tails_ref, span, visit)
    ones = jnp.ones((8, HD), jnp.float32)
    for t in range(span // STEP):
        at = pl.ds(t * STEP, STEP)
        acc = attn_ref[at, :]
        da = dg_ref[at, :].astype(jnp.float32) * u_ref[at, :].astype(jnp.float32)
        for s, val in enumerate((acc * acc, da * acc)):
            sums = dot(ones, val, NT)
            for i in range(STEP // BLK):
                stat_ref[s, pl.ds(t * (STEP // BLK) + i, 1), :] = sums[0:1, i * BLK : (i + 1) * BLK]


def bwd_kernel(counts_ref, tails_ref, q_ref, kv_ref, u_ref, dg_ref, attn_ref, stat_ref, slope_ref,
               gated_ref, du_ref, dq_ref, own_ref, far_ref, dk_ref, dv_ref, do_ref, dq_sum):
    span = q_ref.shape[0]
    for ref in (dk_ref, dv_ref, dq_sum):
        ref[...] = jnp.zeros_like(ref)
    r_all = lax.rsqrt(stat_ref[0] * (1.0 / D) + eps)
    c_all = r_all * r_all * r_all * stat_ref[1] * (1.0 / D)
    r_all, c_all = r_all.T, c_all.T
    for t in range(span // BLK):
        at = pl.ds(t * BLK, BLK)
        r, c = (jnp.broadcast_to(val[:, t : t + 1], (BLK, HD)) for val in (r_all, c_all))
        attn = attn_ref[at, :]
        u = u_ref[at, :].astype(jnp.float32)
        dg = dg_ref[at, :].astype(jnp.float32)
        na = attn * r
        gated_ref[at, :] = (na * u).astype(gated_ref.dtype)
        du_ref[at, :] = (na * dg * slope_ref[at, :HD].astype(jnp.float32)).astype(du_ref.dtype)
        do_ref[at, :] = (r * (dg * u) - attn * c).astype(do_ref.dtype)

    def visit(size, row, key, stop):
        start = jnp.minimum(row, 2 * span - size)
        at = rows_at(start - span, size)
        valid = valid_rows(size, start, row, stop)
        q = jnp.where(valid, q_ref[at, :], jnp.zeros((), jnp.bfloat16))
        do = jnp.where(valid, do_ref[at, :], jnp.zeros((), jnp.bfloat16))

        def body(cols, picked, keep):
            k, here, d_here = kv_ref[cols, :HD], q[picked, :], do[picked, :]
            x = dot(k, here, NT)
            dw = dot(kv_ref[cols, HD:], d_here, NT)
            a = 1.0 + jnp.tanh(x)
            w = x * a
            ds = dw * (a + w * (2.0 - a))
            if keep is not None:
                w = jnp.where(keep, w, 0.0)
                ds = jnp.where(keep, ds, 0.0)
            w = w.astype(jnp.bfloat16)
            ds = ds.astype(jnp.bfloat16)
            dv_ref[cols, :] += dot(w, d_here, NN)
            dk_ref[cols, :] += dot(ds, here, NN)
            return dot(k, ds, TN)

        def diagonal(piece, size):
            if size < WIDE:
                return piece(0, size, 0, size)
            mid = size // 2
            early, late = piece(0, size, 0, mid), piece(mid, size, mid, size)
            return jnp.concatenate([early[:, :mid], early[:, mid:] + late], axis=1)

        dq = for_key_tiles(size, start, key, body, diagonal, jnp.zeros((HD, size), jnp.float32), 0)
        dq_sum[at, :] += dq.T

    for_query_tiles(counts_ref, tails_ref, span, visit)
    dq = dq_sum[...] * (HALF / 2048) * slope_ref[:, 2 * HD : 3 * HD].astype(jnp.float32)
    dq_ref[...] = dq.astype(dq_ref.dtype)
    for total, cols in ((dk_ref, slice(0, HD)), (dv_ref, slice(HD, 2 * HD))):
        far_ref[:, cols] = (total[:span, :] * (1.0 / 2048)).astype(far_ref.dtype)
        own_ref[:, cols] = total[span:, :] * (1.0 / 2048)


def remote(src, dst, send, recv, device):
    return pltpu.make_async_remote_copy(
        src_ref=src, dst_ref=dst, send_sem=send, recv_sem=recv, device_id=(device,), device_id_type=MESH
    )


def greet(devices):
    barrier = pltpu.get_barrier_semaphore()
    for device in devices:
        pl.semaphore_signal(barrier, inc=1, device_id=(device,), device_id_type=MESH)
    return barrier


def place():
    me = lax.axis_index("seq")
    return me, lax.rem(me, HEADS), me // HEADS


def group_peers(me, pos):
    return [me - pos + lax.rem(pos + step, HEADS) for step in range(1, HEADS)]


def front_kernel(tok_ref, go_ref, win_ref, wout_ref, x_out, q_out, u_out, kv_out, dg_out, slope_out,
                 tok, go, xs, wh, wo, dgs, slope, load_sem, out_sem, slope_sem, link_s, link_r, core_s, core_r, dg_s, dg_r, kv_s, kv_r):
    me, pos, group = place()
    n = lax.axis_size("seq")
    base, core, y = me - pos, lax.rem(pos, 2), pos // 2
    rows = tok.shape[0]
    span = rows * HEADS
    half = rows // 2
    peers = group_peers(me, pos)
    after, before = lax.rem(me + HEADS, n), lax.rem(me + n - HEADS, n)
    loads = [pltpu.make_async_copy(tok_ref, tok, load_sem.at[0])]
    loads += [
        pltpu.make_async_copy(
            win_ref.at[:, pl.ds(pl.multiple_of(b * D + pos * HD, HD), HD)], wh.at[:, pl.ds(b * HD, HD)],
            load_sem.at[1 + b])
        for b in range(4)
    ]
    loads += [pltpu.make_async_copy(go_ref, go, load_sem.at[5]), pltpu.make_async_copy(wout_ref, wo, load_sem.at[6])]
    for copy in loads:
        copy.start()
    barrier = greet(peers)
    has_before, has_after = group > 0, group < n // HEADS - 1
    for has, device in ((has_before, before), (has_after, after)):
        @pl.when(has)
        def _():
            pl.semaphore_signal(barrier, inc=1, device_id=(device,), device_id_type=MESH)

    loads[0].wait()
    xf = tok[...].astype(jnp.float32)
    inv = lax.rsqrt(jnp.mean(xf * xf, axis=-1, keepdims=True) + eps)
    xs[pos] = (xf * inv).astype(jnp.bfloat16)

    def at(step):
        return lax.rem(y + step + 4, 4) * 2 + core

    flip = 1 - 2 * core
    ahead, behind, other = base + at(1), base + at(-1), base + pos + flip
    low, high, far = at(-1), at(1), at(2)
    sent, local, halo = [], [], []

    def send(src, dst, s, r, device):
        copy = remote(src, dst, s, r, device)
        copy.start()
        sent.append(copy)
        return copy

    def part(slot, h):
        return xs.at[slot, pl.ds(h * half, half)]

    def link(slot, i, h, device):
        return send(part(slot, h), part(slot, h), link_s.at[i, h], link_r.at[i, h], device)

    def across(slot, i, h):
        return send(part(slot, h), part(slot, h), core_s.at[i, h], core_r.at[i, h], other)

    pl.semaphore_wait(barrier, len(peers) + jnp.where(has_before, 1, 0) + jnp.where(has_after, 1, 0))
    up = {0: link(pos, 0, 0, ahead)}
    down = {1: link(pos, 1, 1, behind)}
    cores = {}
    for h in (0, 1):
        cores[0, h] = across(pos, 0, h)
    up[1] = link(pos, 0, 1, ahead)
    down[0] = link(pos, 1, 0, behind)
    for copy in loads[1:5]:
        copy.wait()

    def process(slot, h, i):
        pre = dot(xs[slot, h * half : (h + 1) * half, :], wh[...], NN)
        sig = 0.5 + 0.5 * jnp.tanh(0.5 * pre)
        hidden = pre * sig
        at_row = pl.multiple_of(slot * rows + h * half, half)
        where, own = pl.ds(at_row, half), pl.ds(pl.multiple_of(span + at_row, half), half)
        kv_out[own, :HD] = hidden[:, 3 * HD :].astype(jnp.bfloat16)
        kv_out[own, HD:] = hidden[:, HD : 2 * HD].astype(jnp.bfloat16)
        copy = remote(kv_out.at[own], kv_out.at[where], kv_s.at[i, h], kv_r.at[i, h], after)
        needed = slot + h > 0
        pl.when(needed & has_after)(copy.start)
        halo.append((needed, copy))
        slope[where, :] = (sig * (1.0 + pre - hidden)).astype(jnp.bfloat16)
        local.append(pltpu.make_async_copy(slope.at[where], slope_out.at[where], slope_sem.at[i, h]))
        local[-1].start()
        u_out[where, :] = hidden[:, :HD].astype(jnp.bfloat16)
        q_out[where, :] = (hidden[:, 2 * HD : 3 * HD] * HALF).astype(jnp.bfloat16)

    def keep(slot):
        local.append(pltpu.make_async_copy(xs.at[slot], x_out.at[slot], out_sem.at[slot]))
        local[-1].start()

    for h in (0, 1):
        process(pos, h, 0)
    for h in (0, 1):
        cores[0, h].wait_recv()
        process(pos + flip, h, 1)
    up[0].wait_recv()
    second_up = link(low, 2, 0, ahead)
    cores[1, 0] = across(low, 1, 0)
    down[1].wait_recv()
    second_down = link(high, 2, 1, behind)
    cores[2, 1] = across(high, 2, 1)
    process(low, 0, 2)
    process(high, 1, 3)
    loads[5].wait()
    loads[6].wait()
    dgs[...] = dot(go[...], wo[...], NT).astype(jnp.bfloat16)
    mine = pl.ds(pl.multiple_of(pos * rows, rows), rows)
    grads = []
    for i, peer in enumerate(peers):
        to = lax.rem(pos + i + 1, HEADS)
        cols = pl.ds(pl.multiple_of(to * HD, HD), HD)
        grads.append(send(dgs.at[:, cols], dg_out.at[mine], dg_s.at[i], dg_r.at[i], peer))
    dg_out[mine, :] = dgs[:, pl.ds(pl.multiple_of(pos * HD, HD), HD)]
    cores[1, 0].wait_recv()
    process(low + flip, 0, 4)
    cores[2, 1].wait_recv()
    process(high + flip, 1, 5)
    up[1].wait_recv()
    cores[1, 1] = across(low, 1, 1)
    down[0].wait_recv()
    cores[2, 0] = across(high, 2, 0)
    process(low, 1, 2)
    process(high, 0, 3)
    cores[1, 1].wait_recv()
    process(low + flip, 1, 4)
    cores[2, 0].wait_recv()
    process(high + flip, 0, 5)
    keep(pos)
    keep(pos + flip)
    keep(low)
    keep(high)
    keep(low + flip)
    keep(high + flip)
    second_up.wait_recv()
    cores[3, 0] = across(far, 3, 0)
    second_down.wait_recv()
    cores[3, 1] = across(far, 3, 1)
    for h in (0, 1):
        process(far, h, 6)
    for h in (0, 1):
        cores[3, h].wait_recv()
        process(far + flip, h, 7)
    keep(far)
    keep(far + flip)
    kv_out[:BLK, :] = jnp.zeros((BLK, 2 * HD), jnp.bfloat16)

    @pl.when(group == 0)
    def _():
        kv_out[BLK:span, :] = jnp.zeros((span - BLK, 2 * HD), jnp.bfloat16)

    for copy in grads:
        copy.wait_recv()
    for needed, copy in halo:
        pl.when(needed & has_before)(copy.wait_recv)
        pl.when(needed & has_after)(copy.wait_send)
    for copy in sent:
        copy.wait_send()
    for copy in local:
        copy.wait()


def front(tokens, grad_out, w_in, w_out):
    rows = tokens.shape[0]
    span = rows * HEADS
    dma = pltpu.SemaphoreType.DMA
    vmem, hbm = pl.BlockSpec(memory_space=pltpu.VMEM), pl.BlockSpec(memory_space=pltpu.HBM)

    def shape(*dims):
        return jax.ShapeDtypeStruct(dims, jnp.bfloat16)

    def scratch(*dims):
        return pltpu.VMEM(dims, jnp.bfloat16)

    return pl.pallas_call(
        front_kernel,
        out_shape=[shape(HEADS, rows, D), shape(span, HD), shape(span, HD), shape(2 * span, 2 * HD),
                   shape(span, HD), shape(span, 4 * HD)],
        in_specs=[hbm] * 4,
        out_specs=[hbm] + [vmem] * 4 + [hbm],
        scratch_shapes=[
            scratch(rows, D), scratch(rows, D), scratch(HEADS, rows, D), scratch(D, 4 * HD), scratch(D, D),
            scratch(rows, D), scratch(span, 4 * HD), dma((7,)), dma((HEADS,)), dma((HEADS, 2)), dma((3, 2)), dma((3, 2)), dma((4, 2)), dma((4, 2)),
            dma((7,)), dma((7,)), dma((HEADS, 2)), dma((HEADS, 2)),
        ],
        compiler_params=pltpu.CompilerParams(collective_id=1, has_side_effects=True, vmem_limit_bytes=48 * 2**20),
        name="front",
    )(tokens, grad_out, w_in, w_out)


def stats_kernel(s_ref, out_ref, held, send_sem, recv_sem):
    me, pos, _ = place()
    peers = group_peers(me, pos)
    pl.semaphore_wait(greet(peers), len(peers))
    copies = []
    for i, peer in enumerate(peers):
        copy = remote(s_ref, held.at[i], send_sem.at[i], recv_sem.at[i], peer)
        copy.start()
        copies.append(copy)
    total = s_ref[...]
    for i, copy in enumerate(copies):
        copy.wait_recv()
        total = total + held[i]
    out_ref[...] = total
    for copy in copies:
        copy.wait_send()


def sum_stats(stats):
    dma = pltpu.SemaphoreType.DMA
    return pl.pallas_call(
        stats_kernel,
        out_shape=jax.ShapeDtypeStruct(stats.shape, jnp.float32),
        in_specs=[pl.BlockSpec(memory_space=pltpu.VMEM)],
        out_specs=pl.BlockSpec(memory_space=pltpu.VMEM),
        scratch_shapes=[pltpu.VMEM((7,) + stats.shape, jnp.float32), dma((7,)), dma((7,))],
        compiler_params=pltpu.CompilerParams(collective_id=2, has_side_effects=True, vmem_limit_bytes=2 * 2**20),
        name="stats",
    )(stats)


def back_kernel(tok_ref, go_ref, gated_ref, du_ref, dq_ref, own_ref, far_ref, slope_ref, x_ref, win_ref,
                wout_ref, out_ref, gt_ref, gw_ref, xs, wi, wo, near, d_full, g_full, d_kv, grads, parts, held, total, landed,
                load_sem, move_s, move_r, halo_s, halo_r, late_s, late_r, w_s, w_r, last_s, last_r):
    me, pos, group = place()
    n = lax.axis_size("seq")
    groups, piece = held.shape[1] + 1, held.shape[2]
    rows = tok_ref.shape[0]
    peers = group_peers(me, pos)
    plane = [lax.rem(group + step, groups) * HEADS + pos for step in range(1, groups)]
    after, before = lax.rem(me + HEADS, n), lax.rem(me + n - HEADS, n)
    has_before, has_after = group > 0, group < groups - 1
    dests = [(2 * (group // 8) + r) * 32 + pos * 4 + lax.rem(group, 8) // 2 for r in range(2)]
    sources = [((me // 64) * 8 + 2 * lax.rem(me, 4) + i) * HEADS + lax.rem(me, 32) // 4 for i in range(2)]
    barrier = greet(peers + plane)
    for source in sources:
        @pl.when(source != me)
        def _():
            pl.semaphore_signal(barrier, inc=1, device_id=(source,), device_id_type=MESH)

    loads = [
        pltpu.make_async_copy(x_ref, xs, load_sem.at[0]),
        pltpu.make_async_copy(wout_ref, wo, load_sem.at[1]),
        pltpu.make_async_copy(win_ref, wi, load_sem.at[2]),
    ]
    loads[0].start()
    loads[1].start()

    def block(p):
        return pl.ds(pl.multiple_of(p * rows, rows), rows)

    def columns(b):
        return pl.ds(pl.multiple_of(b * D + pos * HD, HD), HD)

    def send(src, dst, s, r, device):
        copy = remote(src, dst, s, r, device)
        copy.start()
        return copy

    pl.semaphore_wait(barrier, len(peers) + len(plane) + sum(jnp.where(dest != me, 1, 0) for dest in dests))
    turn = [lax.rem(pos + i + 1, HEADS) for i in range(HEADS)]
    halo = []
    for i, to in enumerate(turn):
        for h in (0, 1):
            part = pl.ds(pl.multiple_of(to * rows + h * BLK, BLK), BLK)
            copy = remote(far_ref.at[part], near.at[part], halo_s.at[i, h], halo_r.at[i, h], before)
            needed = to + h > 0
            pl.when(needed & has_before)(copy.start)
            halo.append((needed, copy))
    near[:BLK, :] = jnp.zeros((BLK, 2 * HD), jnp.bfloat16)

    @pl.when(jnp.logical_not(has_after))
    def _():
        near[BLK:, :] = jnp.zeros((near.shape[0] - BLK, 2 * HD), jnp.bfloat16)

    mine = pl.ds(pl.multiple_of(pos * HD, HD), HD)
    moved = []
    for i, peer in enumerate(peers):
        moved.append([
            send(gated_ref.at[block(turn[i])], g_full.at[:, mine], move_s.at[0, i], move_r.at[0, i], peer),
            send(du_ref.at[block(turn[i])], d_full.at[:, columns(0)], move_s.at[1, i], move_r.at[1, i], peer),
            send(dq_ref.at[block(turn[i])], d_full.at[:, columns(2)], move_s.at[2, i], move_r.at[2, i], peer),
        ])
    g_full[:, mine] = gated_ref[block(pos), :]
    d_full[:, columns(0)] = du_ref[block(pos), :]
    d_full[:, columns(2)] = dq_ref[block(pos), :]

    scattered = []

    def fill(r, pair):
        for j, grad in enumerate(pair):
            parts[r, j * HD : (j + 1) * HD, :] = grad.astype(jnp.bfloat16)

    def share(index, size):
        return pl.ds(pl.multiple_of(index * size, piece), size)

    def scatter(r):
        for i, peer in enumerate(plane):
            to = lax.rem(group + i + 1, groups)
            scattered.append(send(parts.at[r, share(to, piece)], held.at[r, i], w_s.at[r, i], w_r.at[r, i], peer))

    def collect(r):
        acc = parts[r, share(group, piece), :].astype(jnp.float32)
        for i in range(groups - 1):
            scattered[r * (groups - 1) + i].wait_recv()
            acc = acc + held[r, i].astype(jnp.float32)
        return acc

    half = share(lax.rem(group, 2), piece)

    def pass_on(r, acc):
        total[r] = acc.astype(jnp.bfloat16)
        copy = remote(total.at[r], landed.at[half], last_s.at[r], last_r.at[lax.rem(group, 2)], dests[r])
        pl.when(dests[r] != me)(copy.start)

        @pl.when(dests[r] == me)
        def _():
            landed[half, :] = total[r]

        return copy

    loads[0].wait()
    loads[2].start()
    grad = dot(jnp.concatenate([du_ref[...], dq_ref[...]], axis=1), xs[...], TN)
    fill(0, [grad[:HD], grad[HD:]])
    scatter(0)
    late = []
    for i, to in enumerate(turn):
        for needed, copy in halo[2 * i : 2 * i + 2]:
            pl.when(needed & has_after)(copy.wait_recv)
        here = block(to)
        for j, b in ((0, 3), (1, 1)):
            cols = slice(j * HD, (j + 1) * HD)
            slope = slope_ref[here, b * HD : (b + 1) * HD].astype(jnp.float32)
            val = ((own_ref[here, cols] + near[here, cols].astype(jnp.float32)) * slope).astype(jnp.bfloat16)
            d_kv[here, cols] = val
            if i < HEADS - 1:
                dst = d_full.at[:, columns(b)]
                late.append(send(d_kv.at[here, cols], dst, late_s.at[j, i], late_r.at[j, i], peers[i]))
            else:
                d_full[:, columns(b)] = val
        grad = dot(d_kv[here, :], xs[here, :], TN)
        if i < HEADS - 1:
            grads[...] = grad if i == 0 else grads[...] + grad
    grad = grads[...] + grad
    fill(1, [grad[HD:], grad[:HD]])
    scatter(1)
    loads[1].wait()
    for trio in moved:
        trio[0].wait_recv()
    out_ref[...] = (tok_ref[...].astype(jnp.float32) + dot(g_full[...], wo[...], NN)).astype(jnp.bfloat16)
    loads[2].wait()

    def back_dot(b):
        return dot(d_full[:, b * D : (b + 1) * D], wi[:, b * D : (b + 1) * D], NT)

    for trio in moved:
        trio[1].wait_recv()
        trio[2].wait_recv()
    d_normed = back_dot(0) + back_dot(2)
    last = [pass_on(0, collect(0)), pass_on(1, collect(1))]
    for copy in late:
        copy.wait_recv()
    d_normed = d_normed + back_dot(3) + back_dot(1)
    xf = tok_ref[...].astype(jnp.float32)
    inv = lax.rsqrt(jnp.mean(xf * xf, axis=-1, keepdims=True) + eps)
    mean = jnp.mean(d_normed * xf, axis=-1, keepdims=True)
    gt_ref[...] = (go_ref[...].astype(jnp.float32) + inv * (d_normed - xf * (inv * inv * mean))).astype(jnp.bfloat16)
    for i, source in enumerate(sources):
        rows_i = landed.at[pl.ds(i * piece, piece)]
        copy = remote(total.at[0], rows_i, last_s.at[0], last_r.at[i], after)
        pl.when(source != me)(copy.wait_recv)
    gw_ref[...] = landed[...].astype(jnp.float32)
    for dest, copy in zip(dests, last):
        pl.when(dest != me)(copy.wait_send)
    for needed, copy in halo:
        pl.when(needed & has_before)(copy.wait_send)
    for copy in [copy for trio in moved for copy in trio] + late + scattered:
        copy.wait_send()


def back(tokens, grad_out, gated, d_u, d_q, own, far, slope, all_normed, w_in, w_out, groups):
    rows = tokens.shape[0]
    span = rows * HEADS
    dma = pltpu.SemaphoreType.DMA
    piece = 2 * HD // groups
    bf, f32 = jnp.bfloat16, jnp.float32
    vmem, anywhere = pl.BlockSpec(memory_space=pltpu.VMEM), pl.BlockSpec(memory_space=pl.ANY)
    shape = jax.ShapeDtypeStruct
    return pl.pallas_call(
        back_kernel,
        out_shape=[shape((rows, D), bf), shape((rows, D), bf), shape((2 * piece, D), f32)],
        in_specs=[vmem] * 8 + [anywhere] * 3,
        out_specs=[vmem] * 3,
        scratch_shapes=[
            pltpu.VMEM((span, D), bf), pltpu.VMEM((D, 4 * D), bf), pltpu.VMEM((D, D), bf),
            pltpu.VMEM((span, 2 * HD), bf), pltpu.VMEM((rows, 4 * D), bf), pltpu.VMEM((rows, D), bf),
            pltpu.VMEM((span, 2 * HD), bf), pltpu.VMEM((2 * HD, D), f32), pltpu.VMEM((2, 2 * HD, D), bf),
            pltpu.VMEM((2, groups - 1, piece, D), bf), pltpu.VMEM((2, piece, D), bf), pltpu.VMEM((2 * piece, D), bf),
            dma((3,)), dma((3, 7)), dma((3, 7)), dma((HEADS, 2)), dma((HEADS, 2)), dma((2, 7)), dma((2, 7)),
            dma((2, groups - 1)), dma((2, groups - 1)), dma((2,)), dma((2,)),
        ],
        compiler_params=pltpu.CompilerParams(collective_id=3, has_side_effects=True, vmem_limit_bytes=46 * 2**20),
        name="back",
    )(tokens, grad_out, gated, d_u, d_q, own, far, slope, all_normed, w_in, w_out)


def attention_call(kernel, name, tables, arrays, outs, flops, scratch=()):
    vmem = pl.BlockSpec(memory_space=pltpu.VMEM)
    return pl.pallas_call(
        kernel,
        grid_spec=pltpu.PrefetchScalarGridSpec(
            num_scalar_prefetch=2, grid=(1,), in_specs=[vmem] * len(arrays), out_specs=[vmem] * len(outs),
            scratch_shapes=scratch),
        out_shape=outs,
        compiler_params=pltpu.CompilerParams(vmem_limit_bytes=40 * 2**20),
        cost_estimate=pl.CostEstimate(flops=flops, bytes_accessed=4 * 2**20, transcendentals=2**21),
        name=name,
    )(*tables, *arrays)


def per_device(n, tokens, w_in, w_out, counts, tails, grad_out):
    rows = tokens.shape[0]
    span = rows * HEADS
    shape = jax.ShapeDtypeStruct
    bf, f32 = jnp.bfloat16, jnp.float32
    all_normed, q, u, kv, dg, slope = front(*(pltpu.with_memory_space_constraint(a, pltpu.HBM) for a in (tokens, grad_out, w_in, w_out)))
    all_normed = all_normed.reshape(span, D)
    users = (counts, tails)
    attn, stats = attention_call(
        fwd_kernel, "attn_fwd", users, (q, kv, u, dg),
        [shape((span, HD), f32), shape((2, span // BLK, HD), f32)], 10**9)
    stats = sum_stats(stats)
    small, pair = shape((span, HD), bf), (span, 2 * HD)
    both = pltpu.VMEM((2 * span, HD), f32)
    gradients = attention_call(
        bwd_kernel, "attn_bwd", users, (q, kv, u, dg, attn, stats, slope),
        [small, small, small, shape(pair, f32), shape(pair, bf)], 2 * 10**9,
        [both, both, pltpu.VMEM((span, HD), bf), pltpu.VMEM((span, HD), f32)])
    return back(tokens, grad_out, *gradients, slope, all_normed, w_in, w_out, n // HEADS)


def solution(mesh):
    in_specs = (P("seq", None), P(), P(), P(), P(), P("seq", None))
    out_specs = (P("seq", None), P("seq", None), P("seq", None))
    return jax.shard_map(
        functools.partial(per_device, mesh.shape["seq"]),
        mesh=mesh, in_specs=in_specs, out_specs=out_specs, check_vma=False,
    )
```

```python
import functools

import jax
import jax.numpy as jnp
from jax import lax
from jax.experimental import pallas as pl
from jax.experimental.pallas import tpu as pltpu
from jax.sharding import PartitionSpec as P

MESH = pl.DeviceIdType.MESH
HEADS = 8
HD = 128
BLK = 128
D = 1024
eps = 1e-05
HALF = 0.5 * HD ** (-0.5)
NT = (((1,), (1,)), ((), ()))
NN = (((1,), (0,)), ((), ()))
TN = (((0,), (0,)), ((), ()))
WIDE = 512
STEP = 256


def dot(a, b, dims):
    return lax.dot_general(a, b, dims, preferred_element_type=jnp.float32)


def group_index():
    return lax.axis_index("seq") // HEADS


def rows_at(start, size):
    return pl.ds(pl.multiple_of(start, BLK), size)


def for_query_tiles(counts_ref, tails_ref, span, visit):
    blocks = span // BLK
    first = group_index() * blocks
    shift = span - first * BLK

    def user(n, begin):
        end = begin + counts_ref[n]
        low, high = jnp.maximum(begin, first), jnp.minimum(end, first + blocks)

        @pl.when(high > low)
        def _():
            top = jnp.minimum((end - 1) * BLK + tails_ref[n], high * BLK) + shift

            @pl.loop((low - begin) // 4, (high - begin + 3) // 4)
            def _(tile):
                near = jnp.maximum(begin + 4 * tile, low)
                past = jnp.minimum(begin + 4 * tile + 4, high)
                row, stop = near * BLK + shift, jnp.minimum(top, past * BLK + shift)
                pl.when(past - near > 2)(lambda: visit(WIDE, row, begin * BLK + shift, stop))
                pl.when(past - near <= 2)(lambda: visit(WIDE // 2, row, begin * BLK + shift, stop))

        return end

    lax.fori_loop(0, counts_ref.shape[0], user, 0)


def valid_rows(size, start, row, stop):
    r = lax.broadcasted_iota(jnp.int32, (size, HD), 0) + start
    return (r >= row) & (r < stop)


def for_key_tiles(size, start, key, body, diagonal, carry, k_dim):
    back = jnp.maximum(start - key, 0)
    full = back // WIDE

    def index(shape, dim):
        return lax.broadcasted_iota(jnp.int32, shape, dim)

    def plain(j, carry):
        return carry + body(rows_at(start - (j + 1) * WIDE, WIDE), slice(0, size), None)

    def part(_, carry):
        end = start - full * WIDE
        base = jnp.maximum(end - WIDE, 0)
        col = index((size, WIDE) if k_dim else (WIDE, size), k_dim) + base
        return carry + body(rows_at(base, WIDE), slice(0, size), (col >= key) & (col < end))

    def piece(q_low, q_high, k_low, k_high):
        dims = (q_high - q_low, k_high - k_low)
        dims = dims if k_dim else dims[::-1]
        r, c = index(dims, 1 - k_dim) + q_low, index(dims, k_dim) + k_low
        keep = (c <= r) & (c >= key - start)
        return body(rows_at(start + k_low, k_high - k_low), slice(q_low, q_high), keep)

    pairs = full // 2 if k_dim == 0 else 0

    def pair(j, carry):
        return carry + body(rows_at(start - (j + 1) * 2 * WIDE, 2 * WIDE), slice(0, size), None)

    carry = lax.fori_loop(0, pairs, pair, carry)
    carry = lax.fori_loop(2 * pairs, full, plain, carry)
    carry = lax.fori_loop(0, jnp.where(back > full * WIDE, 1, 0), part, carry)
    return carry + diagonal(piece, size)


def fwd_kernel(counts_ref, tails_ref, q_ref, kv_ref, u_ref, dg_ref, attn_ref, stat_ref):
    span = q_ref.shape[0]
    attn_ref[...] = jnp.zeros_like(attn_ref)

    def visit(size, row, key, stop):
        start = jnp.minimum(row, 2 * span - size)
        at = rows_at(start - span, size)
        q = jnp.where(valid_rows(size, start, row, stop), q_ref[at, :], jnp.zeros((), jnp.bfloat16))

        def body(cols, picked, keep):
            x = dot(q[picked, :], kv_ref[cols, :HD], NT)
            if keep is not None:
                x = jnp.where(keep, x, 0.0)
            w = (x + x * jnp.tanh(x)).astype(jnp.bfloat16)
            return dot(w, kv_ref[cols, HD:], NN)

        def diagonal(piece, size):
            return piece(0, size, 0, size)

        acc = for_key_tiles(size, start, key, body, diagonal, jnp.zeros((size, HD), jnp.float32), 1)
        attn_ref[at, :] += acc * (1.0 / 2048)

    for_query_tiles(counts_ref, tails_ref, span, visit)
    ones = jnp.ones((8, HD), jnp.float32)
    for t in range(span // STEP):
        at = pl.ds(t * STEP, STEP)
        acc = attn_ref[at, :]
        da = dg_ref[at, :].astype(jnp.float32) * u_ref[at, :].astype(jnp.float32)
        for s, val in enumerate((acc * acc, da * acc)):
            sums = dot(ones, val, NT)
            for i in range(STEP // BLK):
                stat_ref[s, pl.ds(t * (STEP // BLK) + i, 1), :] = sums[0:1, i * BLK : (i + 1) * BLK]


def bwd_kernel(counts_ref, tails_ref, q_ref, kv_ref, u_ref, dg_ref, attn_ref, stat_ref, slope_ref,
               gated_ref, du_ref, dq_ref, own_ref, far_ref, dk_ref, dv_ref, do_ref, dq_sum):
    span = q_ref.shape[0]
    for ref in (dk_ref, dv_ref, dq_sum):
        ref[...] = jnp.zeros_like(ref)
    r_all = lax.rsqrt(stat_ref[0] * (1.0 / D) + eps)
    c_all = r_all * r_all * r_all * stat_ref[1] * (1.0 / D)
    r_all, c_all = r_all.T, c_all.T
    for t in range(span // BLK):
        at = pl.ds(t * BLK, BLK)
        r, c = (jnp.broadcast_to(val[:, t : t + 1], (BLK, HD)) for val in (r_all, c_all))
        attn = attn_ref[at, :]
        u = u_ref[at, :].astype(jnp.float32)
        dg = dg_ref[at, :].astype(jnp.float32)
        na = attn * r
        gated_ref[at, :] = (na * u).astype(gated_ref.dtype)
        du_ref[at, :] = (na * dg * slope_ref[at, :HD].astype(jnp.float32)).astype(du_ref.dtype)
        do_ref[at, :] = (r * (dg * u) - attn * c).astype(do_ref.dtype)

    def visit(size, row, key, stop):
        start = jnp.minimum(row, 2 * span - size)
        at = rows_at(start - span, size)
        valid = valid_rows(size, start, row, stop)
        q = jnp.where(valid, q_ref[at, :], jnp.zeros((), jnp.bfloat16))
        do = jnp.where(valid, do_ref[at, :], jnp.zeros((), jnp.bfloat16))

        def body(cols, picked, keep):
            k, here, d_here = kv_ref[cols, :HD], q[picked, :], do[picked, :]
            x = dot(k, here, NT)
            dw = dot(kv_ref[cols, HD:], d_here, NT)
            a = 1.0 + jnp.tanh(x)
            w = x * a
            ds = dw * (a + w * (2.0 - a))
            if keep is not None:
                w = jnp.where(keep, w, 0.0)
                ds = jnp.where(keep, ds, 0.0)
            w = w.astype(jnp.bfloat16)
            ds = ds.astype(jnp.bfloat16)
            dv_ref[cols, :] += dot(w, d_here, NN)
            dk_ref[cols, :] += dot(ds, here, NN)
            return dot(k, ds, TN)

        def diagonal(piece, size):
            if size < WIDE:
                return piece(0, size, 0, size)
            mid = size // 2
            early, late = piece(0, size, 0, mid), piece(mid, size, mid, size)
            return jnp.concatenate([early[:, :mid], early[:, mid:] + late], axis=1)

        dq = for_key_tiles(size, start, key, body, diagonal, jnp.zeros((HD, size), jnp.float32), 0)
        dq_sum[at, :] += dq.T

    for_query_tiles(counts_ref, tails_ref, span, visit)
    dq = dq_sum[...] * (HALF / 2048) * slope_ref[:, 2 * HD : 3 * HD].astype(jnp.float32)
    dq_ref[...] = dq.astype(dq_ref.dtype)
    for total, cols in ((dk_ref, slice(0, HD)), (dv_ref, slice(HD, 2 * HD))):
        far_ref[:, cols] = (total[:span, :] * (1.0 / 2048)).astype(far_ref.dtype)
        own_ref[:, cols] = total[span:, :] * (1.0 / 2048)


def remote(src, dst, send, recv, device):
    return pltpu.make_async_remote_copy(
        src_ref=src, dst_ref=dst, send_sem=send, recv_sem=recv, device_id=(device,), device_id_type=MESH
    )


def greet(devices):
    barrier = pltpu.get_barrier_semaphore()
    for device in devices:
        pl.semaphore_signal(barrier, inc=1, device_id=(device,), device_id_type=MESH)
    return barrier


def place():
    me = lax.axis_index("seq")
    return me, lax.rem(me, HEADS), me // HEADS


def group_peers(me, pos):
    return [me - pos + lax.rem(pos + step, HEADS) for step in range(1, HEADS)]


def front_kernel(tok_ref, go_ref, win_ref, wout_ref, x_out, q_out, u_out, kv_out, dg_out, slope_out,
                 tok, go, xs, wh, wo, dgs, slope, load_sem, out_sem, slope_sem, link_s, link_r, core_s, core_r, dg_s, dg_r, kv_s, kv_r):
    me, pos, group = place()
    n = lax.axis_size("seq")
    base, core, y = me - pos, lax.rem(pos, 2), pos // 2
    rows = tok.shape[0]
    span = rows * HEADS
    half = rows // 2
    peers = group_peers(me, pos)
    after, before = lax.rem(me + HEADS, n), lax.rem(me + n - HEADS, n)
    loads = [pltpu.make_async_copy(tok_ref, tok, load_sem.at[0])]
    loads += [
        pltpu.make_async_copy(
            win_ref.at[:, pl.ds(pl.multiple_of(b * D + pos * HD, HD), HD)], wh.at[:, pl.ds(b * HD, HD)],
            load_sem.at[1 + b])
        for b in range(4)
    ]
    loads += [pltpu.make_async_copy(go_ref, go, load_sem.at[5]), pltpu.make_async_copy(wout_ref, wo, load_sem.at[6])]
    for copy in loads:
        copy.start()
    barrier = greet(peers)
    has_before, has_after = group > 0, group < n // HEADS - 1
    for has, device in ((has_before, before), (has_after, after)):
        @pl.when(has)
        def _():
            pl.semaphore_signal(barrier, inc=1, device_id=(device,), device_id_type=MESH)

    loads[0].wait()
    xf = tok[...].astype(jnp.float32)
    inv = lax.rsqrt(jnp.mean(xf * xf, axis=-1, keepdims=True) + eps)
    xs[pos] = (xf * inv).astype(jnp.bfloat16)

    def at(step):
        return lax.rem(y + step + 4, 4) * 2 + core

    flip = 1 - 2 * core
    ahead, behind, other = base + at(1), base + at(-1), base + pos + flip
    low, high, far = at(-1), at(1), at(2)
    sent, local, halo = [], [], []

    def send(src, dst, s, r, device):
        copy = remote(src, dst, s, r, device)
        copy.start()
        sent.append(copy)
        return copy

    def part(slot, h):
        return xs.at[slot, pl.ds(h * half, half)]

    def link(slot, i, h, device):
        return send(part(slot, h), part(slot, h), link_s.at[i, h], link_r.at[i, h], device)

    def across(slot, i, h):
        return send(part(slot, h), part(slot, h), core_s.at[i, h], core_r.at[i, h], other)

    pl.semaphore_wait(barrier, len(peers) + jnp.where(has_before, 1, 0) + jnp.where(has_after, 1, 0))
    up = {0: link(pos, 0, 0, ahead)}
    down = {1: link(pos, 1, 1, behind)}
    cores = {}
    for h in (0, 1):
        cores[0, h] = across(pos, 0, h)
    up[1] = link(pos, 0, 1, ahead)
    down[0] = link(pos, 1, 0, behind)
    for copy in loads[1:5]:
        copy.wait()

    def process(slot, h, i):
        pre = dot(xs[slot, h * half : (h + 1) * half, :], wh[...], NN)
        sig = 0.5 + 0.5 * jnp.tanh(0.5 * pre)
        hidden = pre * sig
        at_row = pl.multiple_of(slot * rows + h * half, half)
        where, own = pl.ds(at_row, half), pl.ds(pl.multiple_of(span + at_row, half), half)
        kv_out[own, :HD] = hidden[:, 3 * HD :].astype(jnp.bfloat16)
        kv_out[own, HD:] = hidden[:, HD : 2 * HD].astype(jnp.bfloat16)
        copy = remote(kv_out.at[own], kv_out.at[where], kv_s.at[i, h], kv_r.at[i, h], after)
        needed = slot + h > 0
        pl.when(needed & has_after)(copy.start)
        halo.append((needed, copy))
        slope[where, :] = (sig * (1.0 + pre - hidden)).astype(jnp.bfloat16)
        local.append(pltpu.make_async_copy(slope.at[where], slope_out.at[where], slope_sem.at[i, h]))
        local[-1].start()
        u_out[where, :] = hidden[:, :HD].astype(jnp.bfloat16)
        q_out[where, :] = (hidden[:, 2 * HD : 3 * HD] * HALF).astype(jnp.bfloat16)

    def keep(slot):
        local.append(pltpu.make_async_copy(xs.at[slot], x_out.at[slot], out_sem.at[slot]))
        local[-1].start()

    for h in (0, 1):
        process(pos, h, 0)
    for h in (0, 1):
        cores[0, h].wait_recv()
        process(pos + flip, h, 1)
    up[0].wait_recv()
    second_up = link(low, 2, 0, ahead)
    cores[1, 0] = across(low, 1, 0)
    down[1].wait_recv()
    second_down = link(high, 2, 1, behind)
    cores[2, 1] = across(high, 2, 1)
    process(low, 0, 2)
    process(high, 1, 3)
    loads[5].wait()
    loads[6].wait()
    dgs[...] = dot(go[...], wo[...], NT).astype(jnp.bfloat16)
    mine = pl.ds(pl.multiple_of(pos * rows, rows), rows)
    grads = []
    for i, peer in enumerate(peers):
        to = lax.rem(pos + i + 1, HEADS)
        cols = pl.ds(pl.multiple_of(to * HD, HD), HD)
        grads.append(send(dgs.at[:, cols], dg_out.at[mine], dg_s.at[i], dg_r.at[i], peer))
    dg_out[mine, :] = dgs[:, pl.ds(pl.multiple_of(pos * HD, HD), HD)]
    cores[1, 0].wait_recv()
    process(low + flip, 0, 4)
    cores[2, 1].wait_recv()
    process(high + flip, 1, 5)
    up[1].wait_recv()
    cores[1, 1] = across(low, 1, 1)
    down[0].wait_recv()
    cores[2, 0] = across(high, 2, 0)
    process(low, 1, 2)
    process(high, 0, 3)
    cores[1, 1].wait_recv()
    process(low + flip, 1, 4)
    cores[2, 0].wait_recv()
    process(high + flip, 0, 5)
    keep(pos)
    keep(pos + flip)
    keep(low)
    keep(high)
    keep(low + flip)
    keep(high + flip)
    second_up.wait_recv()
    cores[3, 0] = across(far, 3, 0)
    second_down.wait_recv()
    cores[3, 1] = across(far, 3, 1)
    for h in (0, 1):
        process(far, h, 6)
    for h in (0, 1):
        cores[3, h].wait_recv()
        process(far + flip, h, 7)
    keep(far)
    keep(far + flip)
    kv_out[:BLK, :] = jnp.zeros((BLK, 2 * HD), jnp.bfloat16)

    @pl.when(group == 0)
    def _():
        kv_out[BLK:span, :] = jnp.zeros((span - BLK, 2 * HD), jnp.bfloat16)

    for copy in grads:
        copy.wait_recv()
    for needed, copy in halo:
        pl.when(needed & has_before)(copy.wait_recv)
        pl.when(needed & has_after)(copy.wait_send)
    for copy in sent:
        copy.wait_send()
    for copy in local:
        copy.wait()


def front(tokens, grad_out, w_in, w_out):
    rows = tokens.shape[0]
    span = rows * HEADS
    dma = pltpu.SemaphoreType.DMA
    vmem, hbm = pl.BlockSpec(memory_space=pltpu.VMEM), pl.BlockSpec(memory_space=pltpu.HBM)

    def shape(*dims):
        return jax.ShapeDtypeStruct(dims, jnp.bfloat16)

    def scratch(*dims):
        return pltpu.VMEM(dims, jnp.bfloat16)

    return pl.pallas_call(
        front_kernel,
        out_shape=[shape(HEADS, rows, D), shape(span, HD), shape(span, HD), shape(2 * span, 2 * HD),
                   shape(span, HD), shape(span, 4 * HD)],
        in_specs=[hbm] * 4,
        out_specs=[hbm] + [vmem] * 4 + [hbm],
        scratch_shapes=[
            scratch(rows, D), scratch(rows, D), scratch(HEADS, rows, D), scratch(D, 4 * HD), scratch(D, D),
            scratch(rows, D), scratch(span, 4 * HD), dma((7,)), dma((HEADS,)), dma((HEADS, 2)), dma((3, 2)), dma((3, 2)), dma((4, 2)), dma((4, 2)),
            dma((7,)), dma((7,)), dma((HEADS, 2)), dma((HEADS, 2)),
        ],
        compiler_params=pltpu.CompilerParams(collective_id=1, has_side_effects=True, vmem_limit_bytes=48 * 2**20),
        name="front",
    )(tokens, grad_out, w_in, w_out)


def stats_kernel(s_ref, out_ref, held, send_sem, recv_sem):
    me, pos, _ = place()
    peers = group_peers(me, pos)
    pl.semaphore_wait(greet(peers), len(peers))
    copies = []
    for i, peer in enumerate(peers):
        copy = remote(s_ref, held.at[i], send_sem.at[i], recv_sem.at[i], peer)
        copy.start()
        copies.append(copy)
    total = s_ref[...]
    for i, copy in enumerate(copies):
        copy.wait_recv()
        total = total + held[i]
    out_ref[...] = total
    for copy in copies:
        copy.wait_send()


def sum_stats(stats):
    dma = pltpu.SemaphoreType.DMA
    return pl.pallas_call(
        stats_kernel,
        out_shape=jax.ShapeDtypeStruct(stats.shape, jnp.float32),
        in_specs=[pl.BlockSpec(memory_space=pltpu.VMEM)],
        out_specs=pl.BlockSpec(memory_space=pltpu.VMEM),
        scratch_shapes=[pltpu.VMEM((7,) + stats.shape, jnp.float32), dma((7,)), dma((7,))],
        compiler_params=pltpu.CompilerParams(collective_id=2, has_side_effects=True, vmem_limit_bytes=2 * 2**20),
        name="stats",
    )(stats)


def back_kernel(tok_ref, go_ref, gated_ref, du_ref, dq_ref, own_ref, far_ref, slope_ref, x_ref, win_ref,
                wout_ref, out_ref, gt_ref, gw_ref, xs, wi, wo, near, d_full, g_full, d_kv, grads, parts, held, total, landed,
                load_sem, move_s, move_r, halo_s, halo_r, late_s, late_r, w_s, w_r, last_s, last_r):
    me, pos, group = place()
    n = lax.axis_size("seq")
    groups, piece = held.shape[1] + 1, held.shape[2]
    rows = tok_ref.shape[0]
    peers = group_peers(me, pos)
    plane = [lax.rem(group + step, groups) * HEADS + pos for step in range(1, groups)]
    after, before = lax.rem(me + HEADS, n), lax.rem(me + n - HEADS, n)
    has_before, has_after = group > 0, group < groups - 1
    dests = [(2 * (group // 8) + r) * 32 + pos * 4 + lax.rem(group, 8) // 2 for r in range(2)]
    sources = [((me // 64) * 8 + 2 * lax.rem(me, 4) + i) * HEADS + lax.rem(me, 32) // 4 for i in range(2)]
    barrier = greet(peers + plane)
    for source in sources:
        @pl.when(source != me)
        def _():
            pl.semaphore_signal(barrier, inc=1, device_id=(source,), device_id_type=MESH)

    loads = [
        pltpu.make_async_copy(x_ref, xs, load_sem.at[0]),
        pltpu.make_async_copy(wout_ref, wo, load_sem.at[1]),
        pltpu.make_async_copy(win_ref, wi, load_sem.at[2]),
    ]
    loads[0].start()
    loads[1].start()

    def block(p):
        return pl.ds(pl.multiple_of(p * rows, rows), rows)

    def columns(b):
        return pl.ds(pl.multiple_of(b * D + pos * HD, HD), HD)

    def send(src, dst, s, r, device):
        copy = remote(src, dst, s, r, device)
        copy.start()
        return copy

    pl.semaphore_wait(barrier, len(peers) + len(plane) + sum(jnp.where(dest != me, 1, 0) for dest in dests))
    turn = [lax.rem(pos + i + 1, HEADS) for i in range(HEADS)]
    halo = []
    for i, to in enumerate(turn):
        for h in (0, 1):
            part = pl.ds(pl.multiple_of(to * rows + h * BLK, BLK), BLK)
            copy = remote(far_ref.at[part], near.at[part], halo_s.at[i, h], halo_r.at[i, h], before)
            needed = to + h > 0
            pl.when(needed & has_before)(copy.start)
            halo.append((needed, copy))
    near[:BLK, :] = jnp.zeros((BLK, 2 * HD), jnp.bfloat16)

    @pl.when(jnp.logical_not(has_after))
    def _():
        near[BLK:, :] = jnp.zeros((near.shape[0] - BLK, 2 * HD), jnp.bfloat16)

    mine = pl.ds(pl.multiple_of(pos * HD, HD), HD)
    moved = []
    for i, peer in enumerate(peers):
        moved.append([
            send(gated_ref.at[block(turn[i])], g_full.at[:, mine], move_s.at[0, i], move_r.at[0, i], peer),
            send(du_ref.at[block(turn[i])], d_full.at[:, columns(0)], move_s.at[1, i], move_r.at[1, i], peer),
            send(dq_ref.at[block(turn[i])], d_full.at[:, columns(2)], move_s.at[2, i], move_r.at[2, i], peer),
        ])
    g_full[:, mine] = gated_ref[block(pos), :]
    d_full[:, columns(0)] = du_ref[block(pos), :]
    d_full[:, columns(2)] = dq_ref[block(pos), :]

    scattered = []

    def fill(r, pair):
        for j, grad in enumerate(pair):
            parts[r, j * HD : (j + 1) * HD, :] = grad.astype(jnp.bfloat16)

    def share(index, size):
        return pl.ds(pl.multiple_of(index * size, piece), size)

    def scatter(r):
        for i, peer in enumerate(plane):
            to = lax.rem(group + i + 1, groups)
            scattered.append(send(parts.at[r, share(to, piece)], held.at[r, i], w_s.at[r, i], w_r.at[r, i], peer))

    def collect(r):
        acc = parts[r, share(group, piece), :].astype(jnp.float32)
        for i in range(groups - 1):
            scattered[r * (groups - 1) + i].wait_recv()
            acc = acc + held[r, i].astype(jnp.float32)
        return acc

    half = share(lax.rem(group, 2), piece)

    def pass_on(r, acc):
        total[r] = acc.astype(jnp.bfloat16)
        copy = remote(total.at[r], landed.at[half], last_s.at[r], last_r.at[lax.rem(group, 2)], dests[r])
        pl.when(dests[r] != me)(copy.start)

        @pl.when(dests[r] == me)
        def _():
            landed[half, :] = total[r]

        return copy

    loads[0].wait()
    loads[2].start()
    grad = dot(jnp.concatenate([du_ref[...], dq_ref[...]], axis=1), xs[...], TN)
    fill(0, [grad[:HD], grad[HD:]])
    scatter(0)
    late = []
    for i, to in enumerate(turn):
        for needed, copy in halo[2 * i : 2 * i + 2]:
            pl.when(needed & has_after)(copy.wait_recv)
        here = block(to)
        for j, b in ((0, 3), (1, 1)):
            cols = slice(j * HD, (j + 1) * HD)
            slope = slope_ref[here, b * HD : (b + 1) * HD].astype(jnp.float32)
            val = ((own_ref[here, cols] + near[here, cols].astype(jnp.float32)) * slope).astype(jnp.bfloat16)
            d_kv[here, cols] = val
            if i < HEADS - 1:
                dst = d_full.at[:, columns(b)]
                late.append(send(d_kv.at[here, cols], dst, late_s.at[j, i], late_r.at[j, i], peers[i]))
            else:
                d_full[:, columns(b)] = val
        grad = dot(d_kv[here, :], xs[here, :], TN)
        if i < HEADS - 1:
            grads[...] = grad if i == 0 else grads[...] + grad
    grad = grads[...] + grad
    fill(1, [grad[HD:], grad[:HD]])
    scatter(1)
    loads[1].wait()
    for trio in moved:
        trio[0].wait_recv()
    out_ref[...] = (tok_ref[...].astype(jnp.float32) + dot(g_full[...], wo[...], NN)).astype(jnp.bfloat16)
    loads[2].wait()

    def back_dot(b):
        return dot(d_full[:, b * D : (b + 1) * D], wi[:, b * D : (b + 1) * D], NT)

    for trio in moved:
        trio[1].wait_recv()
        trio[2].wait_recv()
    d_normed = back_dot(0) + back_dot(2)
    last = [pass_on(0, collect(0)), pass_on(1, collect(1))]
    for copy in late:
        copy.wait_recv()
    d_normed = d_normed + back_dot(3) + back_dot(1)
    xf = tok_ref[...].astype(jnp.float32)
    inv = lax.rsqrt(jnp.mean(xf * xf, axis=-1, keepdims=True) + eps)
    mean = jnp.mean(d_normed * xf, axis=-1, keepdims=True)
    gt_ref[...] = (go_ref[...].astype(jnp.float32) + inv * (d_normed - xf * (inv * inv * mean))).astype(jnp.bfloat16)
    for i, source in enumerate(sources):
        rows_i = landed.at[pl.ds(i * piece, piece)]
        copy = remote(total.at[0], rows_i, last_s.at[0], last_r.at[i], after)
        pl.when(source != me)(copy.wait_recv)
    gw_ref[...] = landed[...].astype(jnp.float32)
    for dest, copy in zip(dests, last):
        pl.when(dest != me)(copy.wait_send)
    for needed, copy in halo:
        pl.when(needed & has_before)(copy.wait_send)
    for copy in [copy for trio in moved for copy in trio] + late + scattered:
        copy.wait_send()


def back(tokens, grad_out, gated, d_u, d_q, own, far, slope, all_normed, w_in, w_out, groups):
    rows = tokens.shape[0]
    span = rows * HEADS
    dma = pltpu.SemaphoreType.DMA
    piece = 2 * HD // groups
    bf, f32 = jnp.bfloat16, jnp.float32
    vmem, anywhere = pl.BlockSpec(memory_space=pltpu.VMEM), pl.BlockSpec(memory_space=pl.ANY)
    shape = jax.ShapeDtypeStruct
    return pl.pallas_call(
        back_kernel,
        out_shape=[shape((rows, D), bf), shape((rows, D), bf), shape((2 * piece, D), f32)],
        in_specs=[vmem] * 8 + [anywhere] * 3,
        out_specs=[vmem] * 3,
        scratch_shapes=[
            pltpu.VMEM((span, D), bf), pltpu.VMEM((D, 4 * D), bf), pltpu.VMEM((D, D), bf),
            pltpu.VMEM((span, 2 * HD), bf), pltpu.VMEM((rows, 4 * D), bf), pltpu.VMEM((rows, D), bf),
            pltpu.VMEM((span, 2 * HD), bf), pltpu.VMEM((2 * HD, D), f32), pltpu.VMEM((2, 2 * HD, D), bf),
            pltpu.VMEM((2, groups - 1, piece, D), bf), pltpu.VMEM((2, piece, D), bf), pltpu.VMEM((2 * piece, D), bf),
            dma((3,)), dma((3, 7)), dma((3, 7)), dma((HEADS, 2)), dma((HEADS, 2)), dma((2, 7)), dma((2, 7)),
            dma((2, groups - 1)), dma((2, groups - 1)), dma((2,)), dma((2,)),
        ],
        compiler_params=pltpu.CompilerParams(collective_id=3, has_side_effects=True, vmem_limit_bytes=46 * 2**20),
        name="back",
    )(tokens, grad_out, gated, d_u, d_q, own, far, slope, all_normed, w_in, w_out)


def store_kernel(*refs):
    count = len(refs) // 2
    sems = refs[-1]
    copies = [pltpu.make_async_copy(refs[i], refs[count + i], sems.at[i]) for i in range(count)]
    for copy in copies:
        copy.start()
    for copy in copies:
        copy.wait()


def store(*arrays):
    return pl.pallas_call(
        store_kernel,
        out_shape=[jax.ShapeDtypeStruct(a.shape, a.dtype) for a in arrays],
        in_specs=[pl.BlockSpec(memory_space=pltpu.VMEM)] * len(arrays),
        out_specs=[pl.BlockSpec(memory_space=pltpu.HBM)] * len(arrays),
        scratch_shapes=[pltpu.SemaphoreType.DMA((len(arrays),))],
        compiler_params=pltpu.CompilerParams(vmem_limit_bytes=2 * 2**20),
        name="store",
    )(*arrays)


def attention_call(kernel, name, tables, arrays, outs, flops, scratch=()):
    vmem = pl.BlockSpec(memory_space=pltpu.VMEM)
    return pl.pallas_call(
        kernel,
        grid_spec=pltpu.PrefetchScalarGridSpec(
            num_scalar_prefetch=2, grid=(1,), in_specs=[vmem] * len(arrays), out_specs=[vmem] * len(outs),
            scratch_shapes=scratch),
        out_shape=outs,
        compiler_params=pltpu.CompilerParams(vmem_limit_bytes=40 * 2**20),
        cost_estimate=pl.CostEstimate(flops=flops, bytes_accessed=4 * 2**20, transcendentals=2**21),
        name=name,
    )(*tables, *arrays)


def per_device(n, tokens, w_in, w_out, counts, tails, grad_out):
    rows = tokens.shape[0]
    span = rows * HEADS
    shape = jax.ShapeDtypeStruct
    bf, f32 = jnp.bfloat16, jnp.float32
    all_normed, q, u, kv, dg, slope = front(*(pltpu.with_memory_space_constraint(a, pltpu.HBM) for a in (tokens, grad_out, w_in, w_out)))
    all_normed = all_normed.reshape(span, D)
    users = (counts, tails)
    attn, stats = attention_call(
        fwd_kernel, "attn_fwd", users, (q, kv, u, dg),
        [shape((span, HD), f32), shape((2, span // BLK, HD), f32)], 10**9)
    stats = sum_stats(stats)
    small, pair = shape((span, HD), bf), (span, 2 * HD)
    both = pltpu.VMEM((2 * span, HD), f32)
    gradients = attention_call(
        bwd_kernel, "attn_bwd", users, (q, kv, u, dg, attn, stats, slope),
        [small, small, small, shape(pair, f32), shape(pair, bf)], 2 * 10**9,
        [both, both, pltpu.VMEM((span, HD), bf), pltpu.VMEM((span, HD), f32)])
    return store(*back(tokens, grad_out, *gradients, slope, all_normed, w_in, w_out, n // HEADS))


def solution(mesh):
    in_specs = (P("seq", None), P(), P(), P(), P(), P("seq", None))
    out_specs = (P("seq", None), P("seq", None), P("seq", None))
    return jax.shard_map(
        functools.partial(per_device, mesh.shape["seq"]),
        mesh=mesh, in_specs=in_specs, out_specs=out_specs, check_vma=False,
    )
```

```python
import functools

import jax
import jax.numpy as jnp
from jax import lax
from jax.experimental import pallas as pl
from jax.experimental.pallas import tpu as pltpu
from jax.sharding import PartitionSpec as P

MESH = pl.DeviceIdType.MESH
HEADS = 8
HD = 128
BLK = 128
D = 1024
eps = 1e-05
HALF = 0.5 * HD ** (-0.5)
NT = (((1,), (1,)), ((), ()))
NN = (((1,), (0,)), ((), ()))
TN = (((0,), (0,)), ((), ()))
WIDE = 512
STEP = 256


def dot(a, b, dims):
    return lax.dot_general(a, b, dims, preferred_element_type=jnp.float32)


def group_index():
    return lax.axis_index("seq") // HEADS


def rows_at(start, size):
    return pl.ds(pl.multiple_of(start, BLK), size)


def for_query_tiles(counts_ref, tails_ref, span, visit):
    blocks = span // BLK
    first = group_index() * blocks
    shift = span - first * BLK

    def user(n, begin):
        end = begin + counts_ref[n]
        low, high = jnp.maximum(begin, first), jnp.minimum(end, first + blocks)

        @pl.when(high > low)
        def _():
            top = jnp.minimum((end - 1) * BLK + tails_ref[n], high * BLK) + shift

            @pl.loop((low - begin) // 4, (high - begin + 3) // 4)
            def _(tile):
                near = jnp.maximum(begin + 4 * tile, low)
                past = jnp.minimum(begin + 4 * tile + 4, high)
                row, stop = near * BLK + shift, jnp.minimum(top, past * BLK + shift)
                pl.when(past - near > 2)(lambda: visit(WIDE, row, begin * BLK + shift, stop))
                pl.when(past - near <= 2)(lambda: visit(WIDE // 2, row, begin * BLK + shift, stop))

        return end

    lax.fori_loop(0, counts_ref.shape[0], user, 0)


def valid_rows(size, start, row, stop):
    r = lax.broadcasted_iota(jnp.int32, (size, HD), 0) + start
    return (r >= row) & (r < stop)


def for_key_tiles(size, start, key, body, diagonal, carry, k_dim):
    back = jnp.maximum(start - key, 0)
    full = back // WIDE

    def index(shape, dim):
        return lax.broadcasted_iota(jnp.int32, shape, dim)

    def plain(j, carry):
        return carry + body(rows_at(start - (j + 1) * WIDE, WIDE), slice(0, size), None)

    def part(_, carry):
        end = start - full * WIDE
        base = jnp.maximum(end - WIDE, 0)
        col = index((size, WIDE) if k_dim else (WIDE, size), k_dim) + base
        return carry + body(rows_at(base, WIDE), slice(0, size), (col >= key) & (col < end))

    def piece(q_low, q_high, k_low, k_high):
        dims = (q_high - q_low, k_high - k_low)
        dims = dims if k_dim else dims[::-1]
        r, c = index(dims, 1 - k_dim) + q_low, index(dims, k_dim) + k_low
        keep = (c <= r) & (c >= key - start)
        return body(rows_at(start + k_low, k_high - k_low), slice(q_low, q_high), keep)

    pairs = full // 2 if k_dim == 0 else 0

    def pair(j, carry):
        return carry + body(rows_at(start - (j + 1) * 2 * WIDE, 2 * WIDE), slice(0, size), None)

    carry = lax.fori_loop(0, pairs, pair, carry)
    carry = lax.fori_loop(2 * pairs, full, plain, carry)
    carry = lax.fori_loop(0, jnp.where(back > full * WIDE, 1, 0), part, carry)
    return carry + diagonal(piece, size)


def fwd_kernel(counts_ref, tails_ref, q_ref, kv_ref, u_ref, dg_ref, attn_ref, stat_ref):
    span = q_ref.shape[0]
    attn_ref[...] = jnp.zeros_like(attn_ref)

    def visit(size, row, key, stop):
        start = jnp.minimum(row, 2 * span - size)
        at = rows_at(start - span, size)
        q = jnp.where(valid_rows(size, start, row, stop), q_ref[at, :], jnp.zeros((), jnp.bfloat16))

        def body(cols, picked, keep):
            x = dot(q[picked, :], kv_ref[cols, :HD], NT)
            if keep is not None:
                x = jnp.where(keep, x, 0.0)
            w = (x + x * jnp.tanh(x)).astype(jnp.bfloat16)
            return dot(w, kv_ref[cols, HD:], NN)

        def diagonal(piece, size):
            return piece(0, size, 0, size)

        acc = for_key_tiles(size, start, key, body, diagonal, jnp.zeros((size, HD), jnp.float32), 1)
        attn_ref[at, :] += acc * (1.0 / 2048)

    for_query_tiles(counts_ref, tails_ref, span, visit)
    ones = jnp.ones((8, HD), jnp.float32)
    for t in range(span // STEP):
        at = pl.ds(t * STEP, STEP)
        acc = attn_ref[at, :]
        da = dg_ref[at, :].astype(jnp.float32) * u_ref[at, :].astype(jnp.float32)
        for s, val in enumerate((acc * acc, da * acc)):
            sums = dot(ones, val, NT)
            for i in range(STEP // BLK):
                stat_ref[s, pl.ds(t * (STEP // BLK) + i, 1), :] = sums[0:1, i * BLK : (i + 1) * BLK]


def bwd_kernel(counts_ref, tails_ref, q_ref, kv_ref, u_ref, dg_ref, attn_ref, stat_ref, slope_ref,
               gated_ref, du_ref, dq_ref, own_ref, far_ref, dk_ref, dv_ref, do_ref, dq_sum):
    span = q_ref.shape[0]
    for ref in (dk_ref, dv_ref, dq_sum):
        ref[...] = jnp.zeros_like(ref)
    r_all = lax.rsqrt(stat_ref[0] * (1.0 / D) + eps)
    c_all = r_all * r_all * r_all * stat_ref[1] * (1.0 / D)
    r_all, c_all = r_all.T, c_all.T
    for t in range(span // BLK):
        at = pl.ds(t * BLK, BLK)
        r, c = (jnp.broadcast_to(val[:, t : t + 1], (BLK, HD)) for val in (r_all, c_all))
        attn = attn_ref[at, :]
        u = u_ref[at, :].astype(jnp.float32)
        dg = dg_ref[at, :].astype(jnp.float32)
        na = attn * r
        gated_ref[at, :] = (na * u).astype(gated_ref.dtype)
        du_ref[at, :] = (na * dg * slope_ref[at, :HD].astype(jnp.float32)).astype(du_ref.dtype)
        do_ref[at, :] = (r * (dg * u) - attn * c).astype(do_ref.dtype)

    def visit(size, row, key, stop):
        start = jnp.minimum(row, 2 * span - size)
        at = rows_at(start - span, size)
        valid = valid_rows(size, start, row, stop)
        q = jnp.where(valid, q_ref[at, :], jnp.zeros((), jnp.bfloat16))
        do = jnp.where(valid, do_ref[at, :], jnp.zeros((), jnp.bfloat16))

        def body(cols, picked, keep):
            k, here, d_here = kv_ref[cols, :HD], q[picked, :], do[picked, :]
            x = dot(k, here, NT)
            dw = dot(kv_ref[cols, HD:], d_here, NT)
            a = 1.0 + jnp.tanh(x)
            w = x * a
            ds = dw * (a + w * (2.0 - a))
            if keep is not None:
                w = jnp.where(keep, w, 0.0)
                ds = jnp.where(keep, ds, 0.0)
            w = w.astype(jnp.bfloat16)
            ds = ds.astype(jnp.bfloat16)
            dv_ref[cols, :] += dot(w, d_here, NN)
            dk_ref[cols, :] += dot(ds, here, NN)
            return dot(k, ds, TN)

        def diagonal(piece, size):
            if size < WIDE:
                return piece(0, size, 0, size)
            mid = size // 2
            early, late = piece(0, size, 0, mid), piece(mid, size, mid, size)
            return jnp.concatenate([early[:, :mid], early[:, mid:] + late], axis=1)

        dq = for_key_tiles(size, start, key, body, diagonal, jnp.zeros((HD, size), jnp.float32), 0)
        dq_sum[at, :] += dq.T

    for_query_tiles(counts_ref, tails_ref, span, visit)
    dq = dq_sum[...] * (HALF / 2048) * slope_ref[:, 2 * HD : 3 * HD].astype(jnp.float32)
    dq_ref[...] = dq.astype(dq_ref.dtype)
    for total, cols in ((dk_ref, slice(0, HD)), (dv_ref, slice(HD, 2 * HD))):
        far_ref[:, cols] = (total[:span, :] * (1.0 / 2048)).astype(far_ref.dtype)
        own_ref[:, cols] = total[span:, :] * (1.0 / 2048)


def remote(src, dst, send, recv, device):
    return pltpu.make_async_remote_copy(
        src_ref=src, dst_ref=dst, send_sem=send, recv_sem=recv, device_id=(device,), device_id_type=MESH
    )


def greet(devices):
    barrier = pltpu.get_barrier_semaphore()
    for device in devices:
        pl.semaphore_signal(barrier, inc=1, device_id=(device,), device_id_type=MESH)
    return barrier


def place():
    me = lax.axis_index("seq")
    return me, lax.rem(me, HEADS), me // HEADS


def group_peers(me, pos):
    return [me - pos + lax.rem(pos + step, HEADS) for step in range(1, HEADS)]


def front_kernel(tok_ref, go_ref, win_ref, wout_ref, x_out, q_out, u_out, kv_out, dg_out, slope_out,
                 tok, go, xs, wh, wo, dgs, slope, load_sem, out_sem, slope_sem, link_s, link_r, core_s, core_r, dg_s, dg_r, kv_s, kv_r):
    me, pos, group = place()
    n = lax.axis_size("seq")
    base, core, y = me - pos, lax.rem(pos, 2), pos // 2
    rows = tok.shape[0]
    span = rows * HEADS
    half = rows // 2
    peers = group_peers(me, pos)
    after, before = lax.rem(me + HEADS, n), lax.rem(me + n - HEADS, n)
    loads = [pltpu.make_async_copy(tok_ref, tok, load_sem.at[0])]
    loads += [
        pltpu.make_async_copy(
            win_ref.at[:, pl.ds(pl.multiple_of(b * D + pos * HD, HD), HD)], wh.at[:, pl.ds(b * HD, HD)],
            load_sem.at[1 + b])
        for b in range(4)
    ]
    loads += [pltpu.make_async_copy(go_ref, go, load_sem.at[5]), pltpu.make_async_copy(wout_ref, wo, load_sem.at[6])]
    for copy in loads:
        copy.start()
    barrier = greet(peers)
    has_before, has_after = group > 0, group < n // HEADS - 1
    for has, device in ((has_before, before), (has_after, after)):
        @pl.when(has)
        def _():
            pl.semaphore_signal(barrier, inc=1, device_id=(device,), device_id_type=MESH)

    loads[0].wait()
    xf = tok[...].astype(jnp.float32)
    inv = lax.rsqrt(jnp.mean(xf * xf, axis=-1, keepdims=True) + eps)
    xs[pos] = (xf * inv).astype(jnp.bfloat16)

    def at(step):
        return lax.rem(y + step + 4, 4) * 2 + core

    flip = 1 - 2 * core
    ahead, behind, other = base + at(1), base + at(-1), base + pos + flip
    low, high, far = at(-1), at(1), at(2)
    sent, local, halo = [], [], []

    def send(src, dst, s, r, device):
        copy = remote(src, dst, s, r, device)
        copy.start()
        sent.append(copy)
        return copy

    def part(slot, h):
        return xs.at[slot, pl.ds(h * half, half)]

    def link(slot, i, h, device):
        return send(part(slot, h), part(slot, h), link_s.at[i, h], link_r.at[i, h], device)

    def across(slot, i, h):
        return send(part(slot, h), part(slot, h), core_s.at[i, h], core_r.at[i, h], other)

    pl.semaphore_wait(barrier, len(peers) + jnp.where(has_before, 1, 0) + jnp.where(has_after, 1, 0))
    up = {0: link(pos, 0, 0, ahead)}
    down = {1: link(pos, 1, 1, behind)}
    cores = {}
    for h in (0, 1):
        cores[0, h] = across(pos, 0, h)
    up[1] = link(pos, 0, 1, ahead)
    down[0] = link(pos, 1, 0, behind)
    for copy in loads[1:5]:
        copy.wait()

    def process(slot, h, i):
        pre = dot(xs[slot, h * half : (h + 1) * half, :], wh[...], NN)
        sig = 0.5 + 0.5 * jnp.tanh(0.5 * pre)
        hidden = pre * sig
        at_row = pl.multiple_of(slot * rows + h * half, half)
        where, own = pl.ds(at_row, half), pl.ds(pl.multiple_of(span + at_row, half), half)
        kv_out[own, :HD] = hidden[:, 3 * HD :].astype(jnp.bfloat16)
        kv_out[own, HD:] = hidden[:, HD : 2 * HD].astype(jnp.bfloat16)
        copy = remote(kv_out.at[own], kv_out.at[where], kv_s.at[i, h], kv_r.at[i, h], after)
        needed = slot + h > 0
        pl.when(needed & has_after)(copy.start)
        halo.append((needed, copy))
        slope[where, :] = (sig * (1.0 + pre - hidden)).astype(jnp.bfloat16)
        local.append(pltpu.make_async_copy(slope.at[where], slope_out.at[where], slope_sem.at[i, h]))
        local[-1].start()
        u_out[where, :] = hidden[:, :HD].astype(jnp.bfloat16)
        q_out[where, :] = (hidden[:, 2 * HD : 3 * HD] * HALF).astype(jnp.bfloat16)

    def keep(slot):
        local.append(pltpu.make_async_copy(xs.at[slot], x_out.at[slot], out_sem.at[slot]))
        local[-1].start()

    for h in (0, 1):
        process(pos, h, 0)
    for h in (0, 1):
        cores[0, h].wait_recv()
        process(pos + flip, h, 1)
    up[0].wait_recv()
    second_up = link(low, 2, 0, ahead)
    cores[1, 0] = across(low, 1, 0)
    down[1].wait_recv()
    second_down = link(high, 2, 1, behind)
    cores[2, 1] = across(high, 2, 1)
    process(low, 0, 2)
    process(high, 1, 3)
    loads[5].wait()
    loads[6].wait()
    dgs[...] = dot(go[...], wo[...], NT).astype(jnp.bfloat16)
    mine = pl.ds(pl.multiple_of(pos * rows, rows), rows)
    grads = []
    for i, peer in enumerate(peers):
        to = lax.rem(pos + i + 1, HEADS)
        cols = pl.ds(pl.multiple_of(to * HD, HD), HD)
        grads.append(send(dgs.at[:, cols], dg_out.at[mine], dg_s.at[i], dg_r.at[i], peer))
    dg_out[mine, :] = dgs[:, pl.ds(pl.multiple_of(pos * HD, HD), HD)]
    cores[1, 0].wait_recv()
    process(low + flip, 0, 4)
    cores[2, 1].wait_recv()
    process(high + flip, 1, 5)
    up[1].wait_recv()
    cores[1, 1] = across(low, 1, 1)
    down[0].wait_recv()
    cores[2, 0] = across(high, 2, 0)
    process(low, 1, 2)
    process(high, 0, 3)
    cores[1, 1].wait_recv()
    process(low + flip, 1, 4)
    cores[2, 0].wait_recv()
    process(high + flip, 0, 5)
    keep(pos)
    keep(pos + flip)
    keep(low)
    keep(high)
    keep(low + flip)
    keep(high + flip)
    second_up.wait_recv()
    cores[3, 0] = across(far, 3, 0)
    second_down.wait_recv()
    cores[3, 1] = across(far, 3, 1)
    for h in (0, 1):
        process(far, h, 6)
    for h in (0, 1):
        cores[3, h].wait_recv()
        process(far + flip, h, 7)
    keep(far)
    keep(far + flip)
    kv_out[:BLK, :] = jnp.zeros((BLK, 2 * HD), jnp.bfloat16)

    @pl.when(group == 0)
    def _():
        kv_out[BLK:span, :] = jnp.zeros((span - BLK, 2 * HD), jnp.bfloat16)

    for copy in grads:
        copy.wait_recv()
    for needed, copy in halo:
        pl.when(needed & has_before)(copy.wait_recv)
        pl.when(needed & has_after)(copy.wait_send)
    for copy in sent:
        copy.wait_send()
    for copy in local:
        copy.wait()


def front(tokens, grad_out, w_in, w_out):
    rows = tokens.shape[0]
    span = rows * HEADS
    dma = pltpu.SemaphoreType.DMA
    vmem, hbm = pl.BlockSpec(memory_space=pltpu.VMEM), pl.BlockSpec(memory_space=pltpu.HBM)

    def shape(*dims):
        return jax.ShapeDtypeStruct(dims, jnp.bfloat16)

    def scratch(*dims):
        return pltpu.VMEM(dims, jnp.bfloat16)

    return pl.pallas_call(
        front_kernel,
        out_shape=[shape(HEADS, rows, D), shape(span, HD), shape(span, HD), shape(2 * span, 2 * HD),
                   shape(span, HD), shape(span, 4 * HD)],
        in_specs=[hbm] * 4,
        out_specs=[hbm] + [vmem] * 4 + [hbm],
        scratch_shapes=[
            scratch(rows, D), scratch(rows, D), scratch(HEADS, rows, D), scratch(D, 4 * HD), scratch(D, D),
            scratch(rows, D), scratch(span, 4 * HD), dma((7,)), dma((HEADS,)), dma((HEADS, 2)), dma((3, 2)), dma((3, 2)), dma((4, 2)), dma((4, 2)),
            dma((7,)), dma((7,)), dma((HEADS, 2)), dma((HEADS, 2)),
        ],
        compiler_params=pltpu.CompilerParams(collective_id=1, has_side_effects=True, vmem_limit_bytes=48 * 2**20),
        name="front",
    )(tokens, grad_out, w_in, w_out)


def stats_kernel(s_ref, out_ref, held, send_sem, recv_sem):
    me, pos, _ = place()
    peers = group_peers(me, pos)
    pl.semaphore_wait(greet(peers), len(peers))
    copies = []
    for i, peer in enumerate(peers):
        copy = remote(s_ref, held.at[i], send_sem.at[i], recv_sem.at[i], peer)
        copy.start()
        copies.append(copy)
    total = s_ref[...]
    for i, copy in enumerate(copies):
        copy.wait_recv()
        total = total + held[i]
    out_ref[...] = total
    for copy in copies:
        copy.wait_send()


def sum_stats(stats):
    dma = pltpu.SemaphoreType.DMA
    return pl.pallas_call(
        stats_kernel,
        out_shape=jax.ShapeDtypeStruct(stats.shape, jnp.float32),
        in_specs=[pl.BlockSpec(memory_space=pltpu.VMEM)],
        out_specs=pl.BlockSpec(memory_space=pltpu.VMEM),
        scratch_shapes=[pltpu.VMEM((7,) + stats.shape, jnp.float32), dma((7,)), dma((7,))],
        compiler_params=pltpu.CompilerParams(collective_id=2, has_side_effects=True, vmem_limit_bytes=2 * 2**20),
        name="stats",
    )(stats)


def back_kernel(tok_ref, go_ref, gated_ref, du_ref, dq_ref, own_ref, far_ref, slope_ref, x_ref, win_ref,
                wout_ref, out_ref, gt_ref, gw_ref, xs, wi, wo, near, d_full, g_full, d_kv, grads, parts, held, total, landed,
                load_sem, move_s, move_r, halo_s, halo_r, late_s, late_r, w_s, w_r, last_s, last_r):
    me, pos, group = place()
    n = lax.axis_size("seq")
    groups, piece = held.shape[1] + 1, held.shape[2]
    rows = tok_ref.shape[0]
    peers = group_peers(me, pos)
    steps = sorted(((dz, dx) for dz in range(4) for dx in range(4) if dz or dx), key=lambda s: -min(s[0], 4 - s[0]) - min(s[1], 4 - s[1]))
    plane_groups = [lax.rem(group // 4 + dz, 4) * 4 + lax.rem(lax.rem(group, 4) + dx, 4) for dz, dx in steps]
    plane = [to * HEADS + pos for to in plane_groups]
    after, before = lax.rem(me + HEADS, n), lax.rem(me + n - HEADS, n)
    has_before, has_after = group > 0, group < groups - 1
    dests = [(2 * (group // 8) + r) * 32 + pos * 4 + lax.rem(group, 8) // 2 for r in range(2)]
    sources = [((me // 64) * 8 + 2 * lax.rem(me, 4) + i) * HEADS + lax.rem(me, 32) // 4 for i in range(2)]
    barrier = greet(peers + plane)
    for source in sources:
        @pl.when(source != me)
        def _():
            pl.semaphore_signal(barrier, inc=1, device_id=(source,), device_id_type=MESH)

    loads = [
        pltpu.make_async_copy(x_ref, xs, load_sem.at[0]),
        pltpu.make_async_copy(wout_ref, wo, load_sem.at[1]),
        pltpu.make_async_copy(win_ref, wi, load_sem.at[2]),
    ]
    loads[0].start()
    loads[1].start()

    def block(p):
        return pl.ds(pl.multiple_of(p * rows, rows), rows)

    def columns(b):
        return pl.ds(pl.multiple_of(b * D + pos * HD, HD), HD)

    def send(src, dst, s, r, device):
        copy = remote(src, dst, s, r, device)
        copy.start()
        return copy

    pl.semaphore_wait(barrier, len(peers) + len(plane) + sum(jnp.where(dest != me, 1, 0) for dest in dests))
    turn = [lax.rem(pos + i + 1, HEADS) for i in range(HEADS)]
    halo = []
    for i, to in enumerate(turn):
        for h in (0, 1):
            part = pl.ds(pl.multiple_of(to * rows + h * BLK, BLK), BLK)
            copy = remote(far_ref.at[part], near.at[part], halo_s.at[i, h], halo_r.at[i, h], before)
            needed = to + h > 0
            pl.when(needed & has_before)(copy.start)
            halo.append((needed, copy))
    near[:BLK, :] = jnp.zeros((BLK, 2 * HD), jnp.bfloat16)

    @pl.when(jnp.logical_not(has_after))
    def _():
        near[BLK:, :] = jnp.zeros((near.shape[0] - BLK, 2 * HD), jnp.bfloat16)

    mine = pl.ds(pl.multiple_of(pos * HD, HD), HD)
    moved = []
    for i, peer in enumerate(peers):
        moved.append([
            send(gated_ref.at[block(turn[i])], g_full.at[:, mine], move_s.at[0, i], move_r.at[0, i], peer),
            send(du_ref.at[block(turn[i])], d_full.at[:, columns(0)], move_s.at[1, i], move_r.at[1, i], peer),
            send(dq_ref.at[block(turn[i])], d_full.at[:, columns(2)], move_s.at[2, i], move_r.at[2, i], peer),
        ])
    g_full[:, mine] = gated_ref[block(pos), :]
    d_full[:, columns(0)] = du_ref[block(pos), :]
    d_full[:, columns(2)] = dq_ref[block(pos), :]

    scattered = []

    def fill(r, pair):
        for j, grad in enumerate(pair):
            parts[r, j * HD : (j + 1) * HD, :] = grad.astype(jnp.bfloat16)

    def share(index, size):
        return pl.ds(pl.multiple_of(index * size, piece), size)

    def scatter(r):
        for i, peer in enumerate(plane):
            scattered.append(send(parts.at[r, share(plane_groups[i], piece)], held.at[r, i], w_s.at[r, i], w_r.at[r, i], peer))

    def collect(r):
        acc = parts[r, share(group, piece), :].astype(jnp.float32)
        for i in range(groups - 1):
            scattered[r * (groups - 1) + i].wait_recv()
            acc = acc + held[r, i].astype(jnp.float32)
        return acc

    half = share(lax.rem(group, 2), piece)

    def pass_on(r, acc):
        total[r] = acc.astype(jnp.bfloat16)
        copy = remote(total.at[r], landed.at[half], last_s.at[r], last_r.at[lax.rem(group, 2)], dests[r])
        pl.when(dests[r] != me)(copy.start)

        @pl.when(dests[r] == me)
        def _():
            landed[half, :] = total[r]

        return copy

    loads[0].wait()
    loads[2].start()
    grad = dot(jnp.concatenate([du_ref[...], dq_ref[...]], axis=1), xs[...], TN)
    fill(0, [grad[:HD], grad[HD:]])
    late = []
    for i, to in enumerate(turn):
        for needed, copy in halo[2 * i : 2 * i + 2]:
            pl.when(needed & has_after)(copy.wait_recv)
        here = block(to)
        for j, b in ((0, 3), (1, 1)):
            cols = slice(j * HD, (j + 1) * HD)
            slope = slope_ref[here, b * HD : (b + 1) * HD].astype(jnp.float32)
            val = ((own_ref[here, cols] + near[here, cols].astype(jnp.float32)) * slope).astype(jnp.bfloat16)
            d_kv[here, cols] = val
            if i < HEADS - 1:
                dst = d_full.at[:, columns(b)]
                late.append(send(d_kv.at[here, cols], dst, late_s.at[j, i], late_r.at[j, i], peers[i]))
            else:
                d_full[:, columns(b)] = val
        if i == 5:
            scatter(0)
        grad = dot(d_kv[here, :], xs[here, :], TN)
        if i < HEADS - 1:
            grads[...] = grad if i == 0 else grads[...] + grad
    grad = grads[...] + grad
    fill(1, [grad[HD:], grad[:HD]])
    scatter(1)
    loads[1].wait()
    for trio in moved:
        trio[0].wait_recv()
    out_ref[...] = (tok_ref[...].astype(jnp.float32) + dot(g_full[...], wo[...], NN)).astype(jnp.bfloat16)
    loads[2].wait()

    def back_dot(b):
        return dot(d_full[:, b * D : (b + 1) * D], wi[:, b * D : (b + 1) * D], NT)

    for trio in moved:
        trio[1].wait_recv()
        trio[2].wait_recv()
    d_normed = back_dot(0) + back_dot(2)
    last = [pass_on(0, collect(0)), pass_on(1, collect(1))]
    for copy in late:
        copy.wait_recv()
    d_normed = d_normed + back_dot(3) + back_dot(1)
    xf = tok_ref[...].astype(jnp.float32)
    inv = lax.rsqrt(jnp.mean(xf * xf, axis=-1, keepdims=True) + eps)
    mean = jnp.mean(d_normed * xf, axis=-1, keepdims=True)
    gt_ref[...] = (go_ref[...].astype(jnp.float32) + inv * (d_normed - xf * (inv * inv * mean))).astype(jnp.bfloat16)
    for i, source in enumerate(sources):
        rows_i = landed.at[pl.ds(i * piece, piece)]
        copy = remote(total.at[0], rows_i, last_s.at[0], last_r.at[i], after)
        pl.when(source != me)(copy.wait_recv)
    gw_ref[...] = landed[...].astype(jnp.float32)
    for dest, copy in zip(dests, last):
        pl.when(dest != me)(copy.wait_send)
    for needed, copy in halo:
        pl.when(needed & has_before)(copy.wait_send)
    for copy in [copy for trio in moved for copy in trio] + late + scattered:
        copy.wait_send()


def back(tokens, grad_out, gated, d_u, d_q, own, far, slope, all_normed, w_in, w_out, groups):
    rows = tokens.shape[0]
    span = rows * HEADS
    dma = pltpu.SemaphoreType.DMA
    piece = 2 * HD // groups
    bf, f32 = jnp.bfloat16, jnp.float32
    vmem, anywhere = pl.BlockSpec(memory_space=pltpu.VMEM), pl.BlockSpec(memory_space=pl.ANY)
    shape = jax.ShapeDtypeStruct
    return pl.pallas_call(
        back_kernel,
        out_shape=[shape((rows, D), bf), shape((rows, D), bf), shape((2 * piece, D), f32)],
        in_specs=[vmem] * 8 + [anywhere] * 3,
        out_specs=[vmem] * 3,
        scratch_shapes=[
            pltpu.VMEM((span, D), bf), pltpu.VMEM((D, 4 * D), bf), pltpu.VMEM((D, D), bf),
            pltpu.VMEM((span, 2 * HD), bf), pltpu.VMEM((rows, 4 * D), bf), pltpu.VMEM((rows, D), bf),
            pltpu.VMEM((span, 2 * HD), bf), pltpu.VMEM((2 * HD, D), f32), pltpu.VMEM((2, 2 * HD, D), bf),
            pltpu.VMEM((2, groups - 1, piece, D), bf), pltpu.VMEM((2, piece, D), bf), pltpu.VMEM((2 * piece, D), bf),
            dma((3,)), dma((3, 7)), dma((3, 7)), dma((HEADS, 2)), dma((HEADS, 2)), dma((2, 7)), dma((2, 7)),
            dma((2, groups - 1)), dma((2, groups - 1)), dma((2,)), dma((2,)),
        ],
        compiler_params=pltpu.CompilerParams(collective_id=3, has_side_effects=True, vmem_limit_bytes=46 * 2**20),
        name="back",
    )(tokens, grad_out, gated, d_u, d_q, own, far, slope, all_normed, w_in, w_out)


def store_kernel(*refs):
    count = len(refs) // 2
    sems = refs[-1]
    copies = [pltpu.make_async_copy(refs[i], refs[count + i], sems.at[i]) for i in range(count)]
    for copy in copies:
        copy.start()
    for copy in copies:
        copy.wait()


def store(*arrays):
    return pl.pallas_call(
        store_kernel,
        out_shape=[jax.ShapeDtypeStruct(a.shape, a.dtype) for a in arrays],
        in_specs=[pl.BlockSpec(memory_space=pltpu.VMEM)] * len(arrays),
        out_specs=[pl.BlockSpec(memory_space=pltpu.HBM)] * len(arrays),
        scratch_shapes=[pltpu.SemaphoreType.DMA((len(arrays),))],
        compiler_params=pltpu.CompilerParams(vmem_limit_bytes=2 * 2**20),
        name="store",
    )(*arrays)


def attention_call(kernel, name, tables, arrays, outs, flops, scratch=()):
    vmem = pl.BlockSpec(memory_space=pltpu.VMEM)
    return pl.pallas_call(
        kernel,
        grid_spec=pltpu.PrefetchScalarGridSpec(
            num_scalar_prefetch=2, grid=(1,), in_specs=[vmem] * len(arrays), out_specs=[vmem] * len(outs),
            scratch_shapes=scratch),
        out_shape=outs,
        compiler_params=pltpu.CompilerParams(vmem_limit_bytes=40 * 2**20),
        cost_estimate=pl.CostEstimate(flops=flops, bytes_accessed=4 * 2**20, transcendentals=2**21),
        name=name,
    )(*tables, *arrays)


def per_device(n, tokens, w_in, w_out, counts, tails, grad_out):
    rows = tokens.shape[0]
    span = rows * HEADS
    shape = jax.ShapeDtypeStruct
    bf, f32 = jnp.bfloat16, jnp.float32
    all_normed, q, u, kv, dg, slope = front(*(pltpu.with_memory_space_constraint(a, pltpu.HBM) for a in (tokens, grad_out, w_in, w_out)))
    all_normed = all_normed.reshape(span, D)
    users = (counts, tails)
    attn, stats = attention_call(
        fwd_kernel, "attn_fwd", users, (q, kv, u, dg),
        [shape((span, HD), f32), shape((2, span // BLK, HD), f32)], 10**9)
    stats = sum_stats(stats)
    small, pair = shape((span, HD), bf), (span, 2 * HD)
    both = pltpu.VMEM((2 * span, HD), f32)
    gradients = attention_call(
        bwd_kernel, "attn_bwd", users, (q, kv, u, dg, attn, stats, slope),
        [small, small, small, shape(pair, f32), shape(pair, bf)], 2 * 10**9,
        [both, both, pltpu.VMEM((span, HD), bf), pltpu.VMEM((span, HD), f32)])
    return store(*back(tokens, grad_out, *gradients, slope, all_normed, w_in, w_out, n // HEADS))


def solution(mesh):
    in_specs = (P("seq", None), P(), P(), P(), P(), P("seq", None))
    out_specs = (P("seq", None), P("seq", None), P("seq", None))
    return jax.shard_map(
        functools.partial(per_device, mesh.shape["seq"]),
        mesh=mesh, in_specs=in_specs, out_specs=out_specs, check_vma=False,
    )
```

```python
import functools

import jax
import jax.numpy as jnp
from jax import lax
from jax.experimental import pallas as pl
from jax.experimental.pallas import tpu as pltpu
from jax.sharding import PartitionSpec as P

MESH = pl.DeviceIdType.MESH
HEADS = 8
HD = 128
BLK = 128
D = 1024
eps = 1e-05
HALF = 0.5 * HD ** (-0.5)
NT = (((1,), (1,)), ((), ()))
NN = (((1,), (0,)), ((), ()))
TN = (((0,), (0,)), ((), ()))
WIDE = 512
STEP = 256


def dot(a, b, dims):
    return lax.dot_general(a, b, dims, preferred_element_type=jnp.float32)


def group_index():
    return lax.axis_index("seq") // HEADS


def rows_at(start, size):
    return pl.ds(pl.multiple_of(start, BLK), size)


def for_query_tiles(counts_ref, tails_ref, span, visit):
    blocks = span // BLK
    first = group_index() * blocks
    shift = span - first * BLK

    def user(n, begin):
        end = begin + counts_ref[n]
        low, high = jnp.maximum(begin, first), jnp.minimum(end, first + blocks)

        @pl.when(high > low)
        def _():
            top = jnp.minimum((end - 1) * BLK + tails_ref[n], high * BLK) + shift

            @pl.loop((low - begin) // 4, (high - begin + 3) // 4)
            def _(tile):
                near = jnp.maximum(begin + 4 * tile, low)
                past = jnp.minimum(begin + 4 * tile + 4, high)
                row, stop = near * BLK + shift, jnp.minimum(top, past * BLK + shift)
                pl.when(past - near > 2)(lambda: visit(WIDE, row, begin * BLK + shift, stop))
                pl.when(past - near <= 2)(lambda: visit(WIDE // 2, row, begin * BLK + shift, stop))

        return end

    lax.fori_loop(0, counts_ref.shape[0], user, 0)


def valid_rows(size, start, row, stop):
    r = lax.broadcasted_iota(jnp.int32, (size, HD), 0) + start
    return (r >= row) & (r < stop)


def for_key_tiles(size, start, key, body, diagonal, carry, k_dim):
    back = jnp.maximum(start - key, 0)
    full = back // WIDE

    def index(shape, dim):
        return lax.broadcasted_iota(jnp.int32, shape, dim)

    def plain(j, carry):
        return carry + body(rows_at(start - (j + 1) * WIDE, WIDE), slice(0, size), None)

    def part(_, carry):
        end = start - full * WIDE
        base = jnp.maximum(end - WIDE, 0)
        col = index((size, WIDE) if k_dim else (WIDE, size), k_dim) + base
        return carry + body(rows_at(base, WIDE), slice(0, size), (col >= key) & (col < end))

    def piece(q_low, q_high, k_low, k_high):
        dims = (q_high - q_low, k_high - k_low)
        dims = dims if k_dim else dims[::-1]
        r, c = index(dims, 1 - k_dim) + q_low, index(dims, k_dim) + k_low
        keep = (c <= r) & (c >= key - start)
        return body(rows_at(start + k_low, k_high - k_low), slice(q_low, q_high), keep)

    pairs = full // 2 if k_dim == 0 else 0

    def pair(j, carry):
        return carry + body(rows_at(start - (j + 1) * 2 * WIDE, 2 * WIDE), slice(0, size), None)

    carry = lax.fori_loop(0, pairs, pair, carry)
    carry = lax.fori_loop(2 * pairs, full, plain, carry)
    carry = lax.fori_loop(0, jnp.where(back > full * WIDE, 1, 0), part, carry)
    return carry + diagonal(piece, size)


def fwd_kernel(counts_ref, tails_ref, q_ref, kv_ref, u_ref, dg_ref, attn_ref, stat_ref):
    span = q_ref.shape[0]
    attn_ref[...] = jnp.zeros_like(attn_ref)

    def visit(size, row, key, stop):
        start = jnp.minimum(row, 2 * span - size)
        at = rows_at(start - span, size)
        q = jnp.where(valid_rows(size, start, row, stop), q_ref[at, :], jnp.zeros((), jnp.bfloat16))

        def body(cols, picked, keep):
            x = dot(q[picked, :], kv_ref[cols, :HD], NT)
            if keep is not None:
                x = jnp.where(keep, x, 0.0)
            w = (x + x * jnp.tanh(x)).astype(jnp.bfloat16)
            return dot(w, kv_ref[cols, HD:], NN)

        def diagonal(piece, size):
            return piece(0, size, 0, size)

        acc = for_key_tiles(size, start, key, body, diagonal, jnp.zeros((size, HD), jnp.float32), 1)
        attn_ref[at, :] += acc * (1.0 / 2048)

    for_query_tiles(counts_ref, tails_ref, span, visit)
    ones = jnp.ones((8, HD), jnp.float32)
    for t in range(span // STEP):
        at = pl.ds(t * STEP, STEP)
        acc = attn_ref[at, :]
        da = dg_ref[at, :].astype(jnp.float32) * u_ref[at, :].astype(jnp.float32)
        for s, val in enumerate((acc * acc, da * acc)):
            sums = dot(ones, val, NT)
            for i in range(STEP // BLK):
                stat_ref[s, pl.ds(t * (STEP // BLK) + i, 1), :] = sums[0:1, i * BLK : (i + 1) * BLK]


def bwd_kernel(counts_ref, tails_ref, q_ref, kv_ref, u_ref, dg_ref, attn_ref, stat_ref, slope_ref,
               gated_ref, du_ref, dq_ref, own_ref, far_ref, dk_ref, dv_ref, do_ref, dq_sum):
    span = q_ref.shape[0]
    for ref in (dk_ref, dv_ref, dq_sum):
        ref[...] = jnp.zeros_like(ref)
    r_all = lax.rsqrt(stat_ref[0] * (1.0 / D) + eps)
    c_all = r_all * r_all * r_all * stat_ref[1] * (1.0 / D)
    r_all, c_all = r_all.T, c_all.T
    for t in range(span // BLK):
        at = pl.ds(t * BLK, BLK)
        r, c = (jnp.broadcast_to(val[:, t : t + 1], (BLK, HD)) for val in (r_all, c_all))
        attn = attn_ref[at, :]
        u = u_ref[at, :].astype(jnp.float32)
        dg = dg_ref[at, :].astype(jnp.float32)
        na = attn * r
        gated_ref[at, :] = (na * u).astype(gated_ref.dtype)
        du_ref[at, :] = (na * dg * slope_ref[at, :HD].astype(jnp.float32)).astype(du_ref.dtype)
        do_ref[at, :] = (r * (dg * u) - attn * c).astype(do_ref.dtype)

    def visit(size, row, key, stop):
        start = jnp.minimum(row, 2 * span - size)
        at = rows_at(start - span, size)
        valid = valid_rows(size, start, row, stop)
        q = jnp.where(valid, q_ref[at, :], jnp.zeros((), jnp.bfloat16))
        do = jnp.where(valid, do_ref[at, :], jnp.zeros((), jnp.bfloat16))

        def body(cols, picked, keep):
            k, here, d_here = kv_ref[cols, :HD], q[picked, :], do[picked, :]
            x = dot(k, here, NT)
            dw = dot(kv_ref[cols, HD:], d_here, NT)
            a = 1.0 + jnp.tanh(x)
            w = x * a
            ds = dw * (a + w * (2.0 - a))
            if keep is not None:
                w = jnp.where(keep, w, 0.0)
                ds = jnp.where(keep, ds, 0.0)
            w = w.astype(jnp.bfloat16)
            ds = ds.astype(jnp.bfloat16)
            dv_ref[cols, :] += dot(w, d_here, NN)
            dk_ref[cols, :] += dot(ds, here, NN)
            return dot(k, ds, TN)

        def diagonal(piece, size):
            if size < WIDE:
                return piece(0, size, 0, size)
            mid = size // 2
            early, late = piece(0, size, 0, mid), piece(mid, size, mid, size)
            return jnp.concatenate([early[:, :mid], early[:, mid:] + late], axis=1)

        dq = for_key_tiles(size, start, key, body, diagonal, jnp.zeros((HD, size), jnp.float32), 0)
        dq_sum[at, :] += dq.T

    for_query_tiles(counts_ref, tails_ref, span, visit)
    dq = dq_sum[...] * (HALF / 2048) * slope_ref[:, 2 * HD : 3 * HD].astype(jnp.float32)
    dq_ref[...] = dq.astype(dq_ref.dtype)
    for total, cols in ((dk_ref, slice(0, HD)), (dv_ref, slice(HD, 2 * HD))):
        far_ref[:, cols] = (total[:span, :] * (1.0 / 2048)).astype(far_ref.dtype)
        own_ref[:, cols] = total[span:, :] * (1.0 / 2048)


def remote(src, dst, send, recv, device):
    return pltpu.make_async_remote_copy(
        src_ref=src, dst_ref=dst, send_sem=send, recv_sem=recv, device_id=(device,), device_id_type=MESH
    )


def greet(devices):
    barrier = pltpu.get_barrier_semaphore()
    for device in devices:
        pl.semaphore_signal(barrier, inc=1, device_id=(device,), device_id_type=MESH)
    return barrier


def place():
    me = lax.axis_index("seq")
    return me, lax.rem(me, HEADS), me // HEADS


def group_peers(me, pos):
    return [me - pos + lax.rem(pos + step, HEADS) for step in range(1, HEADS)]


def front_kernel(tok_ref, go_ref, win_ref, wout_ref, x_out, q_out, u_out, kv_out, dg_out, slope_out,
                 tok, go, xs, wh, wo, dgs, slope, load_sem, out_sem, slope_sem, link_s, link_r, core_s, core_r, dg_s, dg_r, kv_s, kv_r):
    me, pos, group = place()
    n = lax.axis_size("seq")
    base, core, y = me - pos, lax.rem(pos, 2), pos // 2
    rows = tok.shape[0]
    span = rows * HEADS
    half = rows // 2
    peers = group_peers(me, pos)
    after, before = lax.rem(me + HEADS, n), lax.rem(me + n - HEADS, n)
    loads = [pltpu.make_async_copy(tok_ref, tok, load_sem.at[0])]
    loads += [
        pltpu.make_async_copy(
            win_ref.at[:, pl.ds(pl.multiple_of(b * D + pos * HD, HD), HD)], wh.at[:, pl.ds(b * HD, HD)],
            load_sem.at[1 + b])
        for b in range(4)
    ]
    loads += [pltpu.make_async_copy(go_ref, go, load_sem.at[5]), pltpu.make_async_copy(wout_ref, wo, load_sem.at[6])]
    for copy in loads:
        copy.start()
    barrier = greet(peers)
    has_before, has_after = group > 0, group < n // HEADS - 1
    for has, device in ((has_before, before), (has_after, after)):
        @pl.when(has)
        def _():
            pl.semaphore_signal(barrier, inc=1, device_id=(device,), device_id_type=MESH)

    loads[0].wait()
    xf = tok[...].astype(jnp.float32)
    inv = lax.rsqrt(jnp.mean(xf * xf, axis=-1, keepdims=True) + eps)
    xs[pos] = (xf * inv).astype(jnp.bfloat16)

    def at(step):
        return lax.rem(y + step + 4, 4) * 2 + core

    flip = 1 - 2 * core
    ahead, behind, other = base + at(1), base + at(-1), base + pos + flip
    low, high, far = at(-1), at(1), at(2)
    sent, local, halo = [], [], []

    def send(src, dst, s, r, device):
        copy = remote(src, dst, s, r, device)
        copy.start()
        sent.append(copy)
        return copy

    def part(slot, h):
        return xs.at[slot, pl.ds(h * half, half)]

    def link(slot, i, h, device):
        return send(part(slot, h), part(slot, h), link_s.at[i, h], link_r.at[i, h], device)

    def across(slot, i, h):
        return send(part(slot, h), part(slot, h), core_s.at[i, h], core_r.at[i, h], other)

    pl.semaphore_wait(barrier, len(peers) + jnp.where(has_before, 1, 0) + jnp.where(has_after, 1, 0))
    up = {0: link(pos, 0, 0, ahead)}
    down = {1: link(pos, 1, 1, behind)}
    cores = {}
    for h in (0, 1):
        cores[0, h] = across(pos, 0, h)
    up[1] = link(pos, 0, 1, ahead)
    down[0] = link(pos, 1, 0, behind)
    for copy in loads[1:5]:
        copy.wait()

    def process(slot, h, i):
        pre = dot(xs[slot, h * half : (h + 1) * half, :], wh[...], NN)
        sig = 0.5 + 0.5 * jnp.tanh(0.5 * pre)
        hidden = pre * sig
        at_row = pl.multiple_of(slot * rows + h * half, half)
        where, own = pl.ds(at_row, half), pl.ds(pl.multiple_of(span + at_row, half), half)
        kv_out[own, :HD] = hidden[:, 3 * HD :].astype(jnp.bfloat16)
        kv_out[own, HD:] = hidden[:, HD : 2 * HD].astype(jnp.bfloat16)
        copy = remote(kv_out.at[own], kv_out.at[where], kv_s.at[i, h], kv_r.at[i, h], after)
        needed = slot + h > 0
        pl.when(needed & has_after)(copy.start)
        halo.append((needed, copy))
        slope[where, :] = (sig * (1.0 + pre - hidden)).astype(jnp.bfloat16)
        local.append(pltpu.make_async_copy(slope.at[where], slope_out.at[where], slope_sem.at[i, h]))
        local[-1].start()
        u_out[where, :] = hidden[:, :HD].astype(jnp.bfloat16)
        q_out[where, :] = (hidden[:, 2 * HD : 3 * HD] * HALF).astype(jnp.bfloat16)

    def keep(slot):
        local.append(pltpu.make_async_copy(xs.at[slot], x_out.at[slot], out_sem.at[slot]))
        local[-1].start()

    for h in (0, 1):
        process(pos, h, 0)
    for h in (0, 1):
        cores[0, h].wait_recv()
        process(pos + flip, h, 1)
    up[0].wait_recv()
    second_up = link(low, 2, 0, ahead)
    cores[1, 0] = across(low, 1, 0)
    down[1].wait_recv()
    second_down = link(high, 2, 1, behind)
    cores[2, 1] = across(high, 2, 1)
    process(low, 0, 2)
    process(high, 1, 3)
    loads[5].wait()
    loads[6].wait()
    dgs[...] = dot(go[...], wo[...], NT).astype(jnp.bfloat16)
    mine = pl.ds(pl.multiple_of(pos * rows, rows), rows)
    grads = []
    for i, peer in enumerate(peers):
        to = lax.rem(pos + i + 1, HEADS)
        cols = pl.ds(pl.multiple_of(to * HD, HD), HD)
        grads.append(send(dgs.at[:, cols], dg_out.at[mine], dg_s.at[i], dg_r.at[i], peer))
    dg_out[mine, :] = dgs[:, pl.ds(pl.multiple_of(pos * HD, HD), HD)]
    cores[1, 0].wait_recv()
    process(low + flip, 0, 4)
    cores[2, 1].wait_recv()
    process(high + flip, 1, 5)
    up[1].wait_recv()
    cores[1, 1] = across(low, 1, 1)
    down[0].wait_recv()
    cores[2, 0] = across(high, 2, 0)
    process(low, 1, 2)
    process(high, 0, 3)
    cores[1, 1].wait_recv()
    process(low + flip, 1, 4)
    cores[2, 0].wait_recv()
    process(high + flip, 0, 5)
    keep(pos)
    keep(pos + flip)
    keep(low)
    keep(high)
    keep(low + flip)
    keep(high + flip)
    second_up.wait_recv()
    cores[3, 0] = across(far, 3, 0)
    second_down.wait_recv()
    cores[3, 1] = across(far, 3, 1)
    for h in (0, 1):
        process(far, h, 6)
    for h in (0, 1):
        cores[3, h].wait_recv()
        process(far + flip, h, 7)
    keep(far)
    keep(far + flip)
    kv_out[:BLK, :] = jnp.zeros((BLK, 2 * HD), jnp.bfloat16)

    @pl.when(group == 0)
    def _():
        kv_out[BLK:span, :] = jnp.zeros((span - BLK, 2 * HD), jnp.bfloat16)

    for copy in grads:
        copy.wait_recv()
    for needed, copy in halo:
        pl.when(needed & has_before)(copy.wait_recv)
        pl.when(needed & has_after)(copy.wait_send)
    for copy in sent:
        copy.wait_send()
    for copy in local:
        copy.wait()


def front(tokens, grad_out, w_in, w_out):
    rows = tokens.shape[0]
    span = rows * HEADS
    dma = pltpu.SemaphoreType.DMA
    vmem, hbm = pl.BlockSpec(memory_space=pltpu.VMEM), pl.BlockSpec(memory_space=pltpu.HBM)

    def shape(*dims):
        return jax.ShapeDtypeStruct(dims, jnp.bfloat16)

    def scratch(*dims):
        return pltpu.VMEM(dims, jnp.bfloat16)

    return pl.pallas_call(
        front_kernel,
        out_shape=[shape(HEADS, rows, D), shape(span, HD), shape(span, HD), shape(2 * span, 2 * HD),
                   shape(span, HD), shape(span, 4 * HD)],
        in_specs=[hbm] * 4,
        out_specs=[hbm] + [vmem] * 4 + [hbm],
        scratch_shapes=[
            scratch(rows, D), scratch(rows, D), scratch(HEADS, rows, D), scratch(D, 4 * HD), scratch(D, D),
            scratch(rows, D), scratch(span, 4 * HD), dma((7,)), dma((HEADS,)), dma((HEADS, 2)), dma((3, 2)), dma((3, 2)), dma((4, 2)), dma((4, 2)),
            dma((7,)), dma((7,)), dma((HEADS, 2)), dma((HEADS, 2)),
        ],
        compiler_params=pltpu.CompilerParams(collective_id=1, has_side_effects=True, vmem_limit_bytes=48 * 2**20),
        name="front",
    )(tokens, grad_out, w_in, w_out)


def stats_kernel(s_ref, out_ref, held, send_sem, recv_sem):
    me, pos, _ = place()
    peers = group_peers(me, pos)
    pl.semaphore_wait(greet(peers), len(peers))
    copies = []
    for i, peer in enumerate(peers):
        copy = remote(s_ref, held.at[i], send_sem.at[i], recv_sem.at[i], peer)
        copy.start()
        copies.append(copy)
    total = s_ref[...]
    for i, copy in enumerate(copies):
        copy.wait_recv()
        total = total + held[i]
    out_ref[...] = total
    for copy in copies:
        copy.wait_send()


def sum_stats(stats):
    dma = pltpu.SemaphoreType.DMA
    return pl.pallas_call(
        stats_kernel,
        out_shape=jax.ShapeDtypeStruct(stats.shape, jnp.float32),
        in_specs=[pl.BlockSpec(memory_space=pltpu.VMEM)],
        out_specs=pl.BlockSpec(memory_space=pltpu.VMEM),
        scratch_shapes=[pltpu.VMEM((7,) + stats.shape, jnp.float32), dma((7,)), dma((7,))],
        compiler_params=pltpu.CompilerParams(collective_id=2, has_side_effects=True, vmem_limit_bytes=2 * 2**20),
        name="stats",
    )(stats)


def back_kernel(tok_ref, go_ref, gated_ref, du_ref, dq_ref, own_ref, far_ref, slope_ref, x_ref, win_ref,
                wout_ref, out_ref, gt_ref, gw_ref, xs, wi, wo, near, d_full, g_full, d_kv, grads, parts, held, total, landed,
                load_sem, move_s, move_r, halo_s, halo_r, late_s, late_r, w_s, w_r, last_s, last_r):
    me, pos, group = place()
    n = lax.axis_size("seq")
    groups, piece = held.shape[1] + 1, held.shape[2]
    rows = tok_ref.shape[0]
    peers = group_peers(me, pos)
    steps = sorted(((dz, dx) for dz in range(4) for dx in range(4) if dz or dx), key=lambda s: -min(s[0], 4 - s[0]) - min(s[1], 4 - s[1]))
    plane_groups = [lax.rem(group // 4 + dz, 4) * 4 + lax.rem(lax.rem(group, 4) + dx, 4) for dz, dx in steps]
    plane = [to * HEADS + pos for to in plane_groups]
    after, before = lax.rem(me + HEADS, n), lax.rem(me + n - HEADS, n)
    has_before, has_after = group > 0, group < groups - 1
    dests = [(2 * (group // 8) + r) * 32 + pos * 4 + lax.rem(group, 8) // 2 for r in range(2)]
    sources = [((me // 64) * 8 + 2 * lax.rem(me, 4) + i) * HEADS + lax.rem(me, 32) // 4 for i in range(2)]
    barrier = greet(peers + plane)
    for source in sources:
        @pl.when(source != me)
        def _():
            pl.semaphore_signal(barrier, inc=1, device_id=(source,), device_id_type=MESH)

    loads = [
        pltpu.make_async_copy(x_ref, xs, load_sem.at[0]),
        pltpu.make_async_copy(wout_ref, wo, load_sem.at[1]),
        pltpu.make_async_copy(win_ref, wi, load_sem.at[2]),
    ]
    loads[0].start()
    loads[1].start()

    def block(p):
        return pl.ds(pl.multiple_of(p * rows, rows), rows)

    def columns(b):
        return pl.ds(pl.multiple_of(b * D + pos * HD, HD), HD)

    def send(src, dst, s, r, device):
        copy = remote(src, dst, s, r, device)
        copy.start()
        return copy

    pl.semaphore_wait(barrier, len(peers) + len(plane) + sum(jnp.where(dest != me, 1, 0) for dest in dests))
    turn = [lax.rem(pos + i + 1, HEADS) for i in range(HEADS)]
    halo = []
    for i, to in enumerate(turn):
        half = pl.ds(pl.multiple_of(to * rows + BLK, BLK), rows - BLK)
        for h, (part, needed) in enumerate(((block(to), to > 0), (half, to == 0))):
            copy = remote(far_ref.at[part], near.at[part], halo_s.at[i, h], halo_r.at[i, h], before)
            pl.when(needed & has_before)(copy.start)
            halo.append((needed, copy))
    near[:BLK, :] = jnp.zeros((BLK, 2 * HD), jnp.bfloat16)

    @pl.when(jnp.logical_not(has_after))
    def _():
        near[BLK:, :] = jnp.zeros((near.shape[0] - BLK, 2 * HD), jnp.bfloat16)

    mine = pl.ds(pl.multiple_of(pos * HD, HD), HD)
    moved = []
    for i, peer in enumerate(peers):
        moved.append([
            send(gated_ref.at[block(turn[i])], g_full.at[:, mine], move_s.at[0, i], move_r.at[0, i], peer),
            send(du_ref.at[block(turn[i])], d_full.at[:, columns(0)], move_s.at[1, i], move_r.at[1, i], peer),
            send(dq_ref.at[block(turn[i])], d_full.at[:, columns(2)], move_s.at[2, i], move_r.at[2, i], peer),
        ])
    g_full[:, mine] = gated_ref[block(pos), :]
    d_full[:, columns(0)] = du_ref[block(pos), :]
    d_full[:, columns(2)] = dq_ref[block(pos), :]

    scattered = []

    def fill(r, pair):
        for j, grad in enumerate(pair):
            parts[r, j * HD : (j + 1) * HD, :] = grad.astype(jnp.bfloat16)

    def share(index, size):
        return pl.ds(pl.multiple_of(index * size, piece), size)

    def scatter(r):
        for i, peer in enumerate(plane):
            scattered.append(send(parts.at[r, share(plane_groups[i], piece)], held.at[r, i], w_s.at[r, i], w_r.at[r, i], peer))

    def collect(r):
        acc = parts[r, share(group, piece), :].astype(jnp.float32)
        for i in range(groups - 1):
            scattered[r * (groups - 1) + i].wait_recv()
            acc = acc + held[r, i].astype(jnp.float32)
        return acc

    half = share(lax.rem(group, 2), piece)

    def pass_on(r, acc):
        total[r] = acc.astype(jnp.bfloat16)
        copy = remote(total.at[r], landed.at[half], last_s.at[r], last_r.at[lax.rem(group, 2)], dests[r])
        pl.when(dests[r] != me)(copy.start)

        @pl.when(dests[r] == me)
        def _():
            landed[half, :] = total[r]

        return copy

    loads[0].wait()
    loads[2].start()
    grad = dot(jnp.concatenate([du_ref[...], dq_ref[...]], axis=1), xs[...], TN)
    fill(0, [grad[:HD], grad[HD:]])
    late = []
    for i, to in enumerate(turn):
        for needed, copy in halo[2 * i : 2 * i + 2]:
            pl.when(needed & has_after)(copy.wait_recv)
        here = block(to)
        for j, b in ((0, 3), (1, 1)):
            cols = slice(j * HD, (j + 1) * HD)
            slope = slope_ref[here, b * HD : (b + 1) * HD].astype(jnp.float32)
            val = ((own_ref[here, cols] + near[here, cols].astype(jnp.float32)) * slope).astype(jnp.bfloat16)
            d_kv[here, cols] = val
            if i < HEADS - 1:
                dst = d_full.at[:, columns(b)]
                late.append(send(d_kv.at[here, cols], dst, late_s.at[j, i], late_r.at[j, i], peers[i]))
            else:
                d_full[:, columns(b)] = val
        if i == 5:
            scatter(0)
        grad = dot(d_kv[here, :], xs[here, :], TN)
        if i < HEADS - 1:
            grads[...] = grad if i == 0 else grads[...] + grad
    grad = grads[...] + grad
    fill(1, [grad[HD:], grad[:HD]])
    scatter(1)
    loads[1].wait()
    for trio in moved:
        trio[0].wait_recv()
    out_ref[...] = (tok_ref[...].astype(jnp.float32) + dot(g_full[...], wo[...], NN)).astype(jnp.bfloat16)
    loads[2].wait()

    def back_dot(b):
        return dot(d_full[:, b * D : (b + 1) * D], wi[:, b * D : (b + 1) * D], NT)

    for trio in moved:
        trio[1].wait_recv()
        trio[2].wait_recv()
    d_normed = back_dot(0) + back_dot(2)
    last = [pass_on(0, collect(0)), pass_on(1, collect(1))]
    for copy in late:
        copy.wait_recv()
    d_normed = d_normed + back_dot(3) + back_dot(1)
    xf = tok_ref[...].astype(jnp.float32)
    inv = lax.rsqrt(jnp.mean(xf * xf, axis=-1, keepdims=True) + eps)
    mean = jnp.mean(d_normed * xf, axis=-1, keepdims=True)
    gt_ref[...] = (go_ref[...].astype(jnp.float32) + inv * (d_normed - xf * (inv * inv * mean))).astype(jnp.bfloat16)
    for i, source in enumerate(sources):
        rows_i = landed.at[pl.ds(i * piece, piece)]
        copy = remote(total.at[0], rows_i, last_s.at[0], last_r.at[i], after)
        pl.when(source != me)(copy.wait_recv)
    gw_ref[...] = landed[...].astype(jnp.float32)
    for dest, copy in zip(dests, last):
        pl.when(dest != me)(copy.wait_send)
    for needed, copy in halo:
        pl.when(needed & has_before)(copy.wait_send)
    for copy in [copy for trio in moved for copy in trio] + late + scattered:
        copy.wait_send()


def back(tokens, grad_out, gated, d_u, d_q, own, far, slope, all_normed, w_in, w_out, groups):
    rows = tokens.shape[0]
    span = rows * HEADS
    dma = pltpu.SemaphoreType.DMA
    piece = 2 * HD // groups
    bf, f32 = jnp.bfloat16, jnp.float32
    vmem, anywhere = pl.BlockSpec(memory_space=pltpu.VMEM), pl.BlockSpec(memory_space=pl.ANY)
    shape = jax.ShapeDtypeStruct
    return pl.pallas_call(
        back_kernel,
        out_shape=[shape((rows, D), bf), shape((rows, D), bf), shape((2 * piece, D), f32)],
        in_specs=[vmem] * 8 + [anywhere] * 3,
        out_specs=[vmem] * 3,
        scratch_shapes=[
            pltpu.VMEM((span, D), bf), pltpu.VMEM((D, 4 * D), bf), pltpu.VMEM((D, D), bf),
            pltpu.VMEM((span, 2 * HD), bf), pltpu.VMEM((rows, 4 * D), bf), pltpu.VMEM((rows, D), bf),
            pltpu.VMEM((span, 2 * HD), bf), pltpu.VMEM((2 * HD, D), f32), pltpu.VMEM((2, 2 * HD, D), bf),
            pltpu.VMEM((2, groups - 1, piece, D), bf), pltpu.VMEM((2, piece, D), bf), pltpu.VMEM((2 * piece, D), bf),
            dma((3,)), dma((3, 7)), dma((3, 7)), dma((HEADS, 2)), dma((HEADS, 2)), dma((2, 7)), dma((2, 7)),
            dma((2, groups - 1)), dma((2, groups - 1)), dma((2,)), dma((2,)),
        ],
        compiler_params=pltpu.CompilerParams(collective_id=3, has_side_effects=True, vmem_limit_bytes=46 * 2**20),
        name="back",
    )(tokens, grad_out, gated, d_u, d_q, own, far, slope, all_normed, w_in, w_out)


def store_kernel(*refs):
    count = len(refs) // 2
    sems = refs[-1]
    copies = [pltpu.make_async_copy(refs[i], refs[count + i], sems.at[i]) for i in range(count)]
    for copy in copies:
        copy.start()
    for copy in copies:
        copy.wait()


def store(*arrays):
    return pl.pallas_call(
        store_kernel,
        out_shape=[jax.ShapeDtypeStruct(a.shape, a.dtype) for a in arrays],
        in_specs=[pl.BlockSpec(memory_space=pltpu.VMEM)] * len(arrays),
        out_specs=[pl.BlockSpec(memory_space=pltpu.HBM)] * len(arrays),
        scratch_shapes=[pltpu.SemaphoreType.DMA((len(arrays),))],
        compiler_params=pltpu.CompilerParams(vmem_limit_bytes=2 * 2**20),
        name="store",
    )(*arrays)


def attention_call(kernel, name, tables, arrays, outs, flops, scratch=()):
    vmem = pl.BlockSpec(memory_space=pltpu.VMEM)
    return pl.pallas_call(
        kernel,
        grid_spec=pltpu.PrefetchScalarGridSpec(
            num_scalar_prefetch=2, grid=(1,), in_specs=[vmem] * len(arrays), out_specs=[vmem] * len(outs),
            scratch_shapes=scratch),
        out_shape=outs,
        compiler_params=pltpu.CompilerParams(vmem_limit_bytes=40 * 2**20),
        cost_estimate=pl.CostEstimate(flops=flops, bytes_accessed=4 * 2**20, transcendentals=2**21),
        name=name,
    )(*tables, *arrays)


def per_device(n, tokens, w_in, w_out, counts, tails, grad_out):
    rows = tokens.shape[0]
    span = rows * HEADS
    shape = jax.ShapeDtypeStruct
    bf, f32 = jnp.bfloat16, jnp.float32
    all_normed, q, u, kv, dg, slope = front(*(pltpu.with_memory_space_constraint(a, pltpu.HBM) for a in (tokens, grad_out, w_in, w_out)))
    all_normed = all_normed.reshape(span, D)
    users = (counts, tails)
    attn, stats = attention_call(
        fwd_kernel, "attn_fwd", users, (q, kv, u, dg),
        [shape((span, HD), f32), shape((2, span // BLK, HD), f32)], 10**9)
    stats = sum_stats(stats)
    small, pair = shape((span, HD), bf), (span, 2 * HD)
    both = pltpu.VMEM((2 * span, HD), f32)
    gradients = attention_call(
        bwd_kernel, "attn_bwd", users, (q, kv, u, dg, attn, stats, slope),
        [small, small, small, shape(pair, f32), shape(pair, bf)], 2 * 10**9,
        [both, both, pltpu.VMEM((span, HD), bf), pltpu.VMEM((span, HD), f32)])
    return store(*back(tokens, grad_out, *gradients, slope, all_normed, w_in, w_out, n // HEADS))


def solution(mesh):
    in_specs = (P("seq", None), P(), P(), P(), P(), P("seq", None))
    out_specs = (P("seq", None), P("seq", None), P("seq", None))
    return jax.shard_map(
        functools.partial(per_device, mesh.shape["seq"]),
        mesh=mesh, in_specs=in_specs, out_specs=out_specs, check_vma=False,
    )
```

```python
import functools

import jax
import jax.numpy as jnp
from jax import lax
from jax.experimental import pallas as pl
from jax.experimental.pallas import tpu as pltpu
from jax.sharding import PartitionSpec as P

MESH = pl.DeviceIdType.MESH
HEADS = 8
HD = 128
BLK = 128
D = 1024
eps = 1e-05
HALF = 0.5 * HD ** (-0.5)
NT = (((1,), (1,)), ((), ()))
NN = (((1,), (0,)), ((), ()))
TN = (((0,), (0,)), ((), ()))
WIDE = 512
STEP = 256


def dot(a, b, dims):
    return lax.dot_general(a, b, dims, preferred_element_type=jnp.float32)


def group_index():
    return lax.axis_index("seq") // HEADS


def rows_at(start, size):
    return pl.ds(pl.multiple_of(start, BLK), size)


def for_query_tiles(counts_ref, tails_ref, span, visit):
    blocks = span // BLK
    first = group_index() * blocks
    shift = span - first * BLK

    def user(n, begin):
        end = begin + counts_ref[n]
        low, high = jnp.maximum(begin, first), jnp.minimum(end, first + blocks)

        @pl.when(high > low)
        def _():
            top = jnp.minimum((end - 1) * BLK + tails_ref[n], high * BLK) + shift

            @pl.loop((low - begin) // 4, (high - begin + 3) // 4)
            def _(tile):
                near = jnp.maximum(begin + 4 * tile, low)
                past = jnp.minimum(begin + 4 * tile + 4, high)
                row, stop = near * BLK + shift, jnp.minimum(top, past * BLK + shift)
                pl.when(past - near > 2)(lambda: visit(WIDE, row, begin * BLK + shift, stop))
                pl.when(past - near <= 2)(lambda: visit(WIDE // 2, row, begin * BLK + shift, stop))

        return end

    lax.fori_loop(0, counts_ref.shape[0], user, 0)


def valid_rows(size, start, row, stop):
    r = lax.broadcasted_iota(jnp.int32, (size, HD), 0) + start
    return (r >= row) & (r < stop)


def for_key_tiles(size, start, key, body, diagonal, carry, k_dim):
    back = jnp.maximum(start - key, 0)
    full = back // WIDE

    def index(shape, dim):
        return lax.broadcasted_iota(jnp.int32, shape, dim)

    def plain(j, carry):
        return carry + body(rows_at(start - (j + 1) * WIDE, WIDE), slice(0, size), None)

    def part(_, carry):
        end = start - full * WIDE
        base = jnp.maximum(end - WIDE, 0)
        col = index((size, WIDE) if k_dim else (WIDE, size), k_dim) + base
        return carry + body(rows_at(base, WIDE), slice(0, size), (col >= key) & (col < end))

    def piece(q_low, q_high, k_low, k_high):
        dims = (q_high - q_low, k_high - k_low)
        dims = dims if k_dim else dims[::-1]
        r, c = index(dims, 1 - k_dim) + q_low, index(dims, k_dim) + k_low
        keep = (c <= r) & (c >= key - start)
        return body(rows_at(start + k_low, k_high - k_low), slice(q_low, q_high), keep)

    pairs = full // 2

    def pair(j, carry):
        return carry + body(rows_at(start - (j + 1) * 2 * WIDE, 2 * WIDE), slice(0, size), None)

    carry = lax.fori_loop(0, pairs, pair, carry)
    carry = lax.fori_loop(2 * pairs, full, plain, carry)
    carry = lax.fori_loop(0, jnp.where(back > full * WIDE, 1, 0), part, carry)
    return carry + diagonal(piece, size)


def fwd_kernel(counts_ref, tails_ref, q_ref, kv_ref, u_ref, dg_ref, attn_ref, stat_ref):
    span = q_ref.shape[0]
    attn_ref[...] = jnp.zeros_like(attn_ref)

    def visit(size, row, key, stop):
        start = jnp.minimum(row, 2 * span - size)
        at = rows_at(start - span, size)
        q = jnp.where(valid_rows(size, start, row, stop), q_ref[at, :], jnp.zeros((), jnp.bfloat16))

        def body(cols, picked, keep):
            x = dot(q[picked, :], kv_ref[cols, :HD], NT)
            if keep is not None:
                x = jnp.where(keep, x, 0.0)
            w = (x + x * jnp.tanh(x)).astype(jnp.bfloat16)
            return dot(w, kv_ref[cols, HD:], NN)

        def diagonal(piece, size):
            return piece(0, size, 0, size)

        acc = for_key_tiles(size, start, key, body, diagonal, jnp.zeros((size, HD), jnp.float32), 1)
        attn_ref[at, :] += acc * (1.0 / 2048)

    for_query_tiles(counts_ref, tails_ref, span, visit)
    ones = jnp.ones((8, HD), jnp.float32)
    for t in range(span // STEP):
        at = pl.ds(t * STEP, STEP)
        acc = attn_ref[at, :]
        da = dg_ref[at, :].astype(jnp.float32) * u_ref[at, :].astype(jnp.float32)
        for s, val in enumerate((acc * acc, da * acc)):
            sums = dot(ones, val, NT)
            for i in range(STEP // BLK):
                stat_ref[s, pl.ds(t * (STEP // BLK) + i, 1), :] = sums[0:1, i * BLK : (i + 1) * BLK]


def bwd_kernel(counts_ref, tails_ref, q_ref, kv_ref, u_ref, dg_ref, attn_ref, stat_ref, slope_ref,
               gated_ref, du_ref, dq_ref, own_ref, far_ref, dk_ref, dv_ref, do_ref, dq_sum):
    span = q_ref.shape[0]
    for ref in (dk_ref, dv_ref, dq_sum):
        ref[...] = jnp.zeros_like(ref)
    r_all = lax.rsqrt(stat_ref[0] * (1.0 / D) + eps)
    c_all = r_all * r_all * r_all * stat_ref[1] * (1.0 / D)
    r_all, c_all = r_all.T, c_all.T
    for t in range(span // BLK):
        at = pl.ds(t * BLK, BLK)
        r, c = (jnp.broadcast_to(val[:, t : t + 1], (BLK, HD)) for val in (r_all, c_all))
        attn = attn_ref[at, :]
        u = u_ref[at, :].astype(jnp.float32)
        dg = dg_ref[at, :].astype(jnp.float32)
        na = attn * r
        gated_ref[at, :] = (na * u).astype(gated_ref.dtype)
        du_ref[at, :] = (na * dg * slope_ref[at, :HD].astype(jnp.float32)).astype(du_ref.dtype)
        do_ref[at, :] = (r * (dg * u) - attn * c).astype(do_ref.dtype)

    def visit(size, row, key, stop):
        start = jnp.minimum(row, 2 * span - size)
        at = rows_at(start - span, size)
        valid = valid_rows(size, start, row, stop)
        q = jnp.where(valid, q_ref[at, :], jnp.zeros((), jnp.bfloat16))
        do = jnp.where(valid, do_ref[at, :], jnp.zeros((), jnp.bfloat16))

        def body(cols, picked, keep):
            k, here, d_here = kv_ref[cols, :HD], q[picked, :], do[picked, :]
            x = dot(k, here, NT)
            dw = dot(kv_ref[cols, HD:], d_here, NT)
            a = 1.0 + jnp.tanh(x)
            w = x * a
            ds = dw * (a + w * (2.0 - a))
            if keep is not None:
                w = jnp.where(keep, w, 0.0)
                ds = jnp.where(keep, ds, 0.0)
            w = w.astype(jnp.bfloat16)
            ds = ds.astype(jnp.bfloat16)
            dv_ref[cols, :] += dot(w, d_here, NN)
            dk_ref[cols, :] += dot(ds, here, NN)
            return dot(k, ds, TN)

        def diagonal(piece, size):
            if size < WIDE:
                return piece(0, size, 0, size)
            mid = size // 2
            early, late = piece(0, size, 0, mid), piece(mid, size, mid, size)
            return jnp.concatenate([early[:, :mid], early[:, mid:] + late], axis=1)

        dq = for_key_tiles(size, start, key, body, diagonal, jnp.zeros((HD, size), jnp.float32), 0)
        dq_sum[at, :] += dq.T

    for_query_tiles(counts_ref, tails_ref, span, visit)
    dq = dq_sum[...] * (HALF / 2048) * slope_ref[:, 2 * HD : 3 * HD].astype(jnp.float32)
    dq_ref[...] = dq.astype(dq_ref.dtype)
    for total, cols in ((dk_ref, slice(0, HD)), (dv_ref, slice(HD, 2 * HD))):
        far_ref[:, cols] = (total[:span, :] * (1.0 / 2048)).astype(far_ref.dtype)
        own_ref[:, cols] = total[span:, :] * (1.0 / 2048)


def remote(src, dst, send, recv, device):
    return pltpu.make_async_remote_copy(
        src_ref=src, dst_ref=dst, send_sem=send, recv_sem=recv, device_id=(device,), device_id_type=MESH
    )


def greet(devices):
    barrier = pltpu.get_barrier_semaphore()
    for device in devices:
        pl.semaphore_signal(barrier, inc=1, device_id=(device,), device_id_type=MESH)
    return barrier


def place():
    me = lax.axis_index("seq")
    return me, lax.rem(me, HEADS), me // HEADS


def group_peers(me, pos):
    return [me - pos + lax.rem(pos + step, HEADS) for step in range(1, HEADS)]


def front_kernel(tok_ref, go_ref, win_ref, wout_ref, x_out, q_out, u_out, kv_out, dg_out, slope_out,
                 tok, go, xs, wh, wo, dgs, slope, load_sem, out_sem, slope_sem, link_s, link_r, core_s, core_r, dg_s, dg_r, kv_s, kv_r):
    me, pos, group = place()
    n = lax.axis_size("seq")
    base, core, y = me - pos, lax.rem(pos, 2), pos // 2
    rows = tok.shape[0]
    span = rows * HEADS
    half = rows // 2
    peers = group_peers(me, pos)
    after, before = lax.rem(me + HEADS, n), lax.rem(me + n - HEADS, n)
    loads = [pltpu.make_async_copy(tok_ref, tok, load_sem.at[0])]
    loads += [
        pltpu.make_async_copy(
            win_ref.at[:, pl.ds(pl.multiple_of(b * D + pos * HD, HD), HD)], wh.at[:, pl.ds(b * HD, HD)],
            load_sem.at[1 + b])
        for b in range(4)
    ]
    loads += [pltpu.make_async_copy(go_ref, go, load_sem.at[5]), pltpu.make_async_copy(wout_ref, wo, load_sem.at[6])]
    for copy in loads:
        copy.start()
    barrier = greet(peers)
    has_before, has_after = group > 0, group < n // HEADS - 1
    for has, device in ((has_before, before), (has_after, after)):
        @pl.when(has)
        def _():
            pl.semaphore_signal(barrier, inc=1, device_id=(device,), device_id_type=MESH)

    loads[0].wait()
    xf = tok[...].astype(jnp.float32)
    inv = lax.rsqrt(jnp.mean(xf * xf, axis=-1, keepdims=True) + eps)
    xs[pos] = (xf * inv).astype(jnp.bfloat16)

    def at(step):
        return lax.rem(y + step + 4, 4) * 2 + core

    flip = 1 - 2 * core
    ahead, behind, other = base + at(1), base + at(-1), base + pos + flip
    low, high, far = at(-1), at(1), at(2)
    sent, local, halo = [], [], []

    def send(src, dst, s, r, device):
        copy = remote(src, dst, s, r, device)
        copy.start()
        sent.append(copy)
        return copy

    def part(slot, h):
        return xs.at[slot, pl.ds(h * half, half)]

    def link(slot, i, h, device):
        return send(part(slot, h), part(slot, h), link_s.at[i, h], link_r.at[i, h], device)

    def across(slot, i, h):
        return send(part(slot, h), part(slot, h), core_s.at[i, h], core_r.at[i, h], other)

    pl.semaphore_wait(barrier, len(peers) + jnp.where(has_before, 1, 0) + jnp.where(has_after, 1, 0))
    up = {0: link(pos, 0, 0, ahead)}
    down = {1: link(pos, 1, 1, behind)}
    cores = {}
    for h in (0, 1):
        cores[0, h] = across(pos, 0, h)
    up[1] = link(pos, 0, 1, ahead)
    down[0] = link(pos, 1, 0, behind)
    for copy in loads[1:5]:
        copy.wait()

    def process(slot, h, i):
        pre = dot(xs[slot, h * half : (h + 1) * half, :], wh[...], NN)
        sig = 0.5 + 0.5 * jnp.tanh(0.5 * pre)
        hidden = pre * sig
        at_row = pl.multiple_of(slot * rows + h * half, half)
        where, own = pl.ds(at_row, half), pl.ds(pl.multiple_of(span + at_row, half), half)
        kv_out[own, :HD] = hidden[:, 3 * HD :].astype(jnp.bfloat16)
        kv_out[own, HD:] = hidden[:, HD : 2 * HD].astype(jnp.bfloat16)
        copy = remote(kv_out.at[own], kv_out.at[where], kv_s.at[i, h], kv_r.at[i, h], after)
        needed = slot + h > 0
        pl.when(needed & has_after)(copy.start)
        halo.append((needed, copy))
        slope[where, :] = (sig * (1.0 + pre - hidden)).astype(jnp.bfloat16)
        local.append(pltpu.make_async_copy(slope.at[where], slope_out.at[where], slope_sem.at[i, h]))
        local[-1].start()
        u_out[where, :] = hidden[:, :HD].astype(jnp.bfloat16)
        q_out[where, :] = (hidden[:, 2 * HD : 3 * HD] * HALF).astype(jnp.bfloat16)

    def keep(slot):
        local.append(pltpu.make_async_copy(xs.at[slot], x_out.at[slot], out_sem.at[slot]))
        local[-1].start()

    for h in (0, 1):
        process(pos, h, 0)
    for h in (0, 1):
        cores[0, h].wait_recv()
        process(pos + flip, h, 1)
    up[0].wait_recv()
    second_up = link(low, 2, 0, ahead)
    cores[1, 0] = across(low, 1, 0)
    down[1].wait_recv()
    second_down = link(high, 2, 1, behind)
    cores[2, 1] = across(high, 2, 1)
    process(low, 0, 2)
    process(high, 1, 3)
    loads[5].wait()
    loads[6].wait()
    dgs[...] = dot(go[...], wo[...], NT).astype(jnp.bfloat16)
    mine = pl.ds(pl.multiple_of(pos * rows, rows), rows)
    grads = []
    for i, peer in enumerate(peers):
        to = lax.rem(pos + i + 1, HEADS)
        cols = pl.ds(pl.multiple_of(to * HD, HD), HD)
        grads.append(send(dgs.at[:, cols], dg_out.at[mine], dg_s.at[i], dg_r.at[i], peer))
    dg_out[mine, :] = dgs[:, pl.ds(pl.multiple_of(pos * HD, HD), HD)]
    cores[1, 0].wait_recv()
    process(low + flip, 0, 4)
    cores[2, 1].wait_recv()
    process(high + flip, 1, 5)
    up[1].wait_recv()
    cores[1, 1] = across(low, 1, 1)
    down[0].wait_recv()
    cores[2, 0] = across(high, 2, 0)
    process(low, 1, 2)
    process(high, 0, 3)
    cores[1, 1].wait_recv()
    process(low + flip, 1, 4)
    cores[2, 0].wait_recv()
    process(high + flip, 0, 5)
    keep(pos)
    keep(pos + flip)
    keep(low)
    keep(high)
    keep(low + flip)
    keep(high + flip)
    second_up.wait_recv()
    cores[3, 0] = across(far, 3, 0)
    second_down.wait_recv()
    cores[3, 1] = across(far, 3, 1)
    for h in (0, 1):
        process(far, h, 6)
    for h in (0, 1):
        cores[3, h].wait_recv()
        process(far + flip, h, 7)
    keep(far)
    keep(far + flip)
    kv_out[:BLK, :] = jnp.zeros((BLK, 2 * HD), jnp.bfloat16)

    @pl.when(group == 0)
    def _():
        kv_out[BLK:span, :] = jnp.zeros((span - BLK, 2 * HD), jnp.bfloat16)

    for copy in grads:
        copy.wait_recv()
    for needed, copy in halo:
        pl.when(needed & has_before)(copy.wait_recv)
        pl.when(needed & has_after)(copy.wait_send)
    for copy in sent:
        copy.wait_send()
    for copy in local:
        copy.wait()


def front(tokens, grad_out, w_in, w_out):
    rows = tokens.shape[0]
    span = rows * HEADS
    dma = pltpu.SemaphoreType.DMA
    vmem, hbm = pl.BlockSpec(memory_space=pltpu.VMEM), pl.BlockSpec(memory_space=pltpu.HBM)

    def shape(*dims):
        return jax.ShapeDtypeStruct(dims, jnp.bfloat16)

    def scratch(*dims):
        return pltpu.VMEM(dims, jnp.bfloat16)

    return pl.pallas_call(
        front_kernel,
        out_shape=[shape(HEADS, rows, D), shape(span, HD), shape(span, HD), shape(2 * span, 2 * HD),
                   shape(span, HD), shape(span, 4 * HD)],
        in_specs=[hbm] * 4,
        out_specs=[hbm] + [vmem] * 4 + [hbm],
        scratch_shapes=[
            scratch(rows, D), scratch(rows, D), scratch(HEADS, rows, D), scratch(D, 4 * HD), scratch(D, D),
            scratch(rows, D), scratch(span, 4 * HD), dma((7,)), dma((HEADS,)), dma((HEADS, 2)), dma((3, 2)), dma((3, 2)), dma((4, 2)), dma((4, 2)),
            dma((7,)), dma((7,)), dma((HEADS, 2)), dma((HEADS, 2)),
        ],
        compiler_params=pltpu.CompilerParams(collective_id=1, has_side_effects=True, vmem_limit_bytes=48 * 2**20),
        name="front",
    )(tokens, grad_out, w_in, w_out)


def stats_kernel(s_ref, out_ref, held, send_sem, recv_sem):
    me, pos, _ = place()
    peers = group_peers(me, pos)
    pl.semaphore_wait(greet(peers), len(peers))
    copies = []
    for i, peer in enumerate(peers):
        copy = remote(s_ref, held.at[i], send_sem.at[i], recv_sem.at[i], peer)
        copy.start()
        copies.append(copy)
    total = s_ref[...]
    for i, copy in enumerate(copies):
        copy.wait_recv()
        total = total + held[i]
    out_ref[...] = total
    for copy in copies:
        copy.wait_send()


def sum_stats(stats):
    dma = pltpu.SemaphoreType.DMA
    return pl.pallas_call(
        stats_kernel,
        out_shape=jax.ShapeDtypeStruct(stats.shape, jnp.float32),
        in_specs=[pl.BlockSpec(memory_space=pltpu.VMEM)],
        out_specs=pl.BlockSpec(memory_space=pltpu.VMEM),
        scratch_shapes=[pltpu.VMEM((7,) + stats.shape, jnp.float32), dma((7,)), dma((7,))],
        compiler_params=pltpu.CompilerParams(collective_id=2, has_side_effects=True, vmem_limit_bytes=2 * 2**20),
        name="stats",
    )(stats)


def back_kernel(tok_ref, go_ref, gated_ref, du_ref, dq_ref, own_ref, far_ref, slope_ref, x_ref, win_ref,
                wout_ref, out_ref, gt_ref, gw_ref, xs, wi, wo, near, d_full, g_full, d_kv, grads, parts, held, total, landed,
                load_sem, move_s, move_r, halo_s, halo_r, late_s, late_r, w_s, w_r, last_s, last_r):
    me, pos, group = place()
    n = lax.axis_size("seq")
    groups, piece = held.shape[1] + 1, held.shape[2]
    rows = tok_ref.shape[0]
    peers = group_peers(me, pos)
    steps = sorted(((dz, dx) for dz in range(4) for dx in range(4) if dz or dx), key=lambda s: -min(s[0], 4 - s[0]) - min(s[1], 4 - s[1]))
    plane_groups = [lax.rem(group // 4 + dz, 4) * 4 + lax.rem(lax.rem(group, 4) + dx, 4) for dz, dx in steps]
    plane = [to * HEADS + pos for to in plane_groups]
    after, before = lax.rem(me + HEADS, n), lax.rem(me + n - HEADS, n)
    has_before, has_after = group > 0, group < groups - 1
    dests = [(2 * (group // 8) + r) * 32 + pos * 4 + lax.rem(group, 8) // 2 for r in range(2)]
    sources = [((me // 64) * 8 + 2 * lax.rem(me, 4) + i) * HEADS + lax.rem(me, 32) // 4 for i in range(2)]
    barrier = greet(peers + plane)
    for source in sources:
        @pl.when(source != me)
        def _():
            pl.semaphore_signal(barrier, inc=1, device_id=(source,), device_id_type=MESH)

    loads = [
        pltpu.make_async_copy(x_ref, xs, load_sem.at[0]),
        pltpu.make_async_copy(wout_ref, wo, load_sem.at[1]),
        pltpu.make_async_copy(win_ref, wi, load_sem.at[2]),
    ]
    loads[0].start()
    loads[1].start()

    def block(p):
        return pl.ds(pl.multiple_of(p * rows, rows), rows)

    def columns(b):
        return pl.ds(pl.multiple_of(b * D + pos * HD, HD), HD)

    def send(src, dst, s, r, device):
        copy = remote(src, dst, s, r, device)
        copy.start()
        return copy

    pl.semaphore_wait(barrier, len(peers) + len(plane) + sum(jnp.where(dest != me, 1, 0) for dest in dests))
    turn = [lax.rem(pos + i + 1, HEADS) for i in range(HEADS)]
    halo = []
    for i, to in enumerate(turn):
        for h in (0, 1):
            part = pl.ds(pl.multiple_of(to * rows + h * BLK, BLK), BLK)
            copy = remote(far_ref.at[part], near.at[part], halo_s.at[i, h], halo_r.at[i, h], before)
            needed = to + h > 0
            pl.when(needed & has_before)(copy.start)
            halo.append((needed, copy))
    near[:BLK, :] = jnp.zeros((BLK, 2 * HD), jnp.bfloat16)

    @pl.when(jnp.logical_not(has_after))
    def _():
        near[BLK:, :] = jnp.zeros((near.shape[0] - BLK, 2 * HD), jnp.bfloat16)

    mine = pl.ds(pl.multiple_of(pos * HD, HD), HD)
    moved = []
    for i, peer in enumerate(peers):
        moved.append([
            send(gated_ref.at[block(turn[i])], g_full.at[:, mine], move_s.at[0, i], move_r.at[0, i], peer),
            send(du_ref.at[block(turn[i])], d_full.at[:, columns(0)], move_s.at[1, i], move_r.at[1, i], peer),
            send(dq_ref.at[block(turn[i])], d_full.at[:, columns(2)], move_s.at[2, i], move_r.at[2, i], peer),
        ])
    g_full[:, mine] = gated_ref[block(pos), :]
    d_full[:, columns(0)] = du_ref[block(pos), :]
    d_full[:, columns(2)] = dq_ref[block(pos), :]

    scattered = []

    def fill(r, pair):
        for j, grad in enumerate(pair):
            parts[r, j * HD : (j + 1) * HD, :] = grad.astype(jnp.bfloat16)

    def share(index, size):
        return pl.ds(pl.multiple_of(index * size, piece), size)

    def scatter(r):
        for i, peer in enumerate(plane):
            scattered.append(send(parts.at[r, share(plane_groups[i], piece)], held.at[r, i], w_s.at[r, i], w_r.at[r, i], peer))

    def collect(r):
        acc = parts[r, share(group, piece), :].astype(jnp.float32)
        for i in range(groups - 1):
            scattered[r * (groups - 1) + i].wait_recv()
            acc = acc + held[r, i].astype(jnp.float32)
        return acc

    half = share(lax.rem(group, 2), piece)

    def pass_on(r, acc):
        total[r] = acc.astype(jnp.bfloat16)
        copy = remote(total.at[r], landed.at[half], last_s.at[r], last_r.at[lax.rem(group, 2)], dests[r])
        pl.when(dests[r] != me)(copy.start)

        @pl.when(dests[r] == me)
        def _():
            landed[half, :] = total[r]

        return copy

    loads[0].wait()
    loads[2].start()
    grad = dot(jnp.concatenate([du_ref[...], dq_ref[...]], axis=1), xs[...], TN)
    fill(0, [grad[:HD], grad[HD:]])
    late = []
    for i, to in enumerate(turn):
        for needed, copy in halo[2 * i : 2 * i + 2]:
            pl.when(needed & has_after)(copy.wait_recv)
        here = block(to)
        for j, b in ((0, 3), (1, 1)):
            cols = slice(j * HD, (j + 1) * HD)
            slope = slope_ref[here, b * HD : (b + 1) * HD].astype(jnp.float32)
            val = ((own_ref[here, cols] + near[here, cols].astype(jnp.float32)) * slope).astype(jnp.bfloat16)
            d_kv[here, cols] = val
            if i < HEADS - 1:
                dst = d_full.at[:, columns(b)]
                late.append(send(d_kv.at[here, cols], dst, late_s.at[j, i], late_r.at[j, i], peers[i]))
            else:
                d_full[:, columns(b)] = val
        if i == 5:
            scatter(0)
        grad = dot(d_kv[here, :], xs[here, :], TN)
        if i < HEADS - 1:
            grads[...] = grad if i == 0 else grads[...] + grad
    grad = grads[...] + grad
    fill(1, [grad[HD:], grad[:HD]])
    scatter(1)
    loads[1].wait()
    for trio in moved:
        trio[0].wait_recv()
    out_ref[...] = (tok_ref[...].astype(jnp.float32) + dot(g_full[...], wo[...], NN)).astype(jnp.bfloat16)
    loads[2].wait()

    def back_dot(b):
        return dot(d_full[:, b * D : (b + 1) * D], wi[:, b * D : (b + 1) * D], NT)

    for trio in moved:
        trio[1].wait_recv()
        trio[2].wait_recv()
    d_normed = back_dot(0) + back_dot(2)
    last = [pass_on(0, collect(0)), pass_on(1, collect(1))]
    for copy in late:
        copy.wait_recv()
    d_normed = d_normed + back_dot(3) + back_dot(1)
    xf = tok_ref[...].astype(jnp.float32)
    inv = lax.rsqrt(jnp.mean(xf * xf, axis=-1, keepdims=True) + eps)
    mean = jnp.mean(d_normed * xf, axis=-1, keepdims=True)
    gt_ref[...] = (go_ref[...].astype(jnp.float32) + inv * (d_normed - xf * (inv * inv * mean))).astype(jnp.bfloat16)
    for i, source in enumerate(sources):
        rows_i = landed.at[pl.ds(i * piece, piece)]
        copy = remote(total.at[0], rows_i, last_s.at[0], last_r.at[i], after)
        pl.when(source != me)(copy.wait_recv)
    gw_ref[...] = landed[...].astype(jnp.float32)
    for dest, copy in zip(dests, last):
        pl.when(dest != me)(copy.wait_send)
    for needed, copy in halo:
        pl.when(needed & has_before)(copy.wait_send)
    for copy in [copy for trio in moved for copy in trio] + late + scattered:
        copy.wait_send()


def back(tokens, grad_out, gated, d_u, d_q, own, far, slope, all_normed, w_in, w_out, groups):
    rows = tokens.shape[0]
    span = rows * HEADS
    dma = pltpu.SemaphoreType.DMA
    piece = 2 * HD // groups
    bf, f32 = jnp.bfloat16, jnp.float32
    vmem, anywhere = pl.BlockSpec(memory_space=pltpu.VMEM), pl.BlockSpec(memory_space=pl.ANY)
    shape = jax.ShapeDtypeStruct
    return pl.pallas_call(
        back_kernel,
        out_shape=[shape((rows, D), bf), shape((rows, D), bf), shape((2 * piece, D), f32)],
        in_specs=[vmem] * 8 + [anywhere] * 3,
        out_specs=[vmem] * 3,
        scratch_shapes=[
            pltpu.VMEM((span, D), bf), pltpu.VMEM((D, 4 * D), bf), pltpu.VMEM((D, D), bf),
            pltpu.VMEM((span, 2 * HD), bf), pltpu.VMEM((rows, 4 * D), bf), pltpu.VMEM((rows, D), bf),
            pltpu.VMEM((span, 2 * HD), bf), pltpu.VMEM((2 * HD, D), f32), pltpu.VMEM((2, 2 * HD, D), bf),
            pltpu.VMEM((2, groups - 1, piece, D), bf), pltpu.VMEM((2, piece, D), bf), pltpu.VMEM((2 * piece, D), bf),
            dma((3,)), dma((3, 7)), dma((3, 7)), dma((HEADS, 2)), dma((HEADS, 2)), dma((2, 7)), dma((2, 7)),
            dma((2, groups - 1)), dma((2, groups - 1)), dma((2,)), dma((2,)),
        ],
        compiler_params=pltpu.CompilerParams(collective_id=3, has_side_effects=True, vmem_limit_bytes=46 * 2**20),
        name="back",
    )(tokens, grad_out, gated, d_u, d_q, own, far, slope, all_normed, w_in, w_out)


def store_kernel(*refs):
    count = len(refs) // 2
    sems = refs[-1]
    copies = [pltpu.make_async_copy(refs[i], refs[count + i], sems.at[i]) for i in range(count)]
    for copy in copies:
        copy.start()
    for copy in copies:
        copy.wait()


def store(*arrays):
    return pl.pallas_call(
        store_kernel,
        out_shape=[jax.ShapeDtypeStruct(a.shape, a.dtype) for a in arrays],
        in_specs=[pl.BlockSpec(memory_space=pltpu.VMEM)] * len(arrays),
        out_specs=[pl.BlockSpec(memory_space=pltpu.HBM)] * len(arrays),
        scratch_shapes=[pltpu.SemaphoreType.DMA((len(arrays),))],
        compiler_params=pltpu.CompilerParams(vmem_limit_bytes=2 * 2**20),
        name="store",
    )(*arrays)


def attention_call(kernel, name, tables, arrays, outs, flops, scratch=()):
    vmem = pl.BlockSpec(memory_space=pltpu.VMEM)
    return pl.pallas_call(
        kernel,
        grid_spec=pltpu.PrefetchScalarGridSpec(
            num_scalar_prefetch=2, grid=(1,), in_specs=[vmem] * len(arrays), out_specs=[vmem] * len(outs),
            scratch_shapes=scratch),
        out_shape=outs,
        compiler_params=pltpu.CompilerParams(vmem_limit_bytes=40 * 2**20),
        cost_estimate=pl.CostEstimate(flops=flops, bytes_accessed=4 * 2**20, transcendentals=2**21),
        name=name,
    )(*tables, *arrays)


def per_device(n, tokens, w_in, w_out, counts, tails, grad_out):
    rows = tokens.shape[0]
    span = rows * HEADS
    shape = jax.ShapeDtypeStruct
    bf, f32 = jnp.bfloat16, jnp.float32
    all_normed, q, u, kv, dg, slope = front(*(pltpu.with_memory_space_constraint(a, pltpu.HBM) for a in (tokens, grad_out, w_in, w_out)))
    all_normed = all_normed.reshape(span, D)
    users = (counts, tails)
    attn, stats = attention_call(
        fwd_kernel, "attn_fwd", users, (q, kv, u, dg),
        [shape((span, HD), f32), shape((2, span // BLK, HD), f32)], 10**9)
    stats = sum_stats(stats)
    small, pair = shape((span, HD), bf), (span, 2 * HD)
    both = pltpu.VMEM((2 * span, HD), f32)
    gradients = attention_call(
        bwd_kernel, "attn_bwd", users, (q, kv, u, dg, attn, stats, slope),
        [small, small, small, shape(pair, f32), shape(pair, bf)], 2 * 10**9,
        [both, both, pltpu.VMEM((span, HD), bf), pltpu.VMEM((span, HD), f32)])
    return store(*back(tokens, grad_out, *gradients, slope, all_normed, w_in, w_out, n // HEADS))


def solution(mesh):
    in_specs = (P("seq", None), P(), P(), P(), P(), P("seq", None))
    out_specs = (P("seq", None), P("seq", None), P("seq", None))
    return jax.shard_map(
        functools.partial(per_device, mesh.shape["seq"]),
        mesh=mesh, in_specs=in_specs, out_specs=out_specs, check_vma=False,
    )
```
